32 devices in a mesh: gx: 8 (over z, core), gy: 4 (over y, x).
Axes of the slice: x: 2, y: 2, z: 4, core: 2. Of those that a mesh axis runs over, the one named last changes fastest.
Arguments:
- density: bfloat16 [32, 16, 1024], P('gx', 'gy'), may hold values from -6 to 6
- p2m_operator: bfloat16 [64, 56], replicated, may hold values from -0.75 to 0.75
- m2l_table: bfloat16 [7, 7, 7, 56, 56], replicated, may hold values from -0.0625 to 0.0625
- near_table: bfloat16 [3, 3, 3, 64, 64], replicated, may hold values from -0.15625 to 0.15625
- l2p_operator: bfloat16 [56, 64], replicated, may hold values from -0.75 to 0.75
Outputs:
- potential: float32 [32, 16, 1024], P('gx', 'gy')
The draws below stay inside these ranges and needn't reach their ends.
All inputs are finite; a program needn't handle non-finite values.
Results may differ from the reference program's by a relative error of at most 0.003.
Values may be sent and summed in bfloat16 or wider, within the bound.
No kernel may reach another device: no remote copies, remote signals or barrier semaphores. Data moves between devices by JAX's collectives and lax.ppermute only.
A program may use at most 128 MiB of HBM per device.

```python
import jax
import jax.numpy as jnp
from jax import lax

Q = 64
NE = 56
LZ = 16
LX = 32
LY = 16


def shard_levels(own_key, shape, split, least, top_value):
    loudness, own = 1.0, jax.random.fold_in(own_key, 6)
    for dim, parts in split:
        steps = jnp.exp(jax.random.uniform(jax.random.fold_in(own, dim), (parts,), jnp.float32, least / len(split), top_value / len(split)))
        loudness = loudness * jnp.repeat(steps, shape[dim] // parts).reshape([-1 if axis == dim else 1 for axis in range(len(shape))])
    return loudness


def gaussian(rng, extent, spread, reach, cuts=(), held_as=jnp.bfloat16):
    array = spread * jax.random.normal(rng, extent, jnp.float32)
    if cuts:
        array = array * shard_levels(rng, extent, cuts, -0.22, 0.18)
    return jnp.clip(array, -reach, reach).astype(held_as)


def setup_inputs(seed: int = 0) -> dict:
    streams_of = jax.random.split(jax.random.key(seed), 6)
    return {
        "density": gaussian(streams_of[0], (LX, LY, LZ * Q), 1.0, 6.0, ((0, 8), (1, 4))),
        "p2m_operator": gaussian(streams_of[1], (Q, NE), Q ** -0.5, 0.75),
        "m2l_table": gaussian(streams_of[2], (7, 7, 7, NE, NE), (189 * NE) ** -0.5, 0.0625),
        "near_table": gaussian(streams_of[3], (3, 3, 3, Q, Q), (27 * Q) ** -0.5, 0.15625),
        "l2p_operator": gaussian(streams_of[4], (NE, Q), NE ** -0.5, 0.75),
    }


def masked_table(kernel_table):
    offsets = jnp.abs(jnp.arange(7) - 3)
    largest = jnp.maximum(jnp.maximum(offsets[:, None, None], offsets[None, :, None]), offsets[None, None, :])
    distant = (largest >= 2).astype(kernel_table.dtype)
    return kernel_table * distant[:, :, :, None, None]


def class_matrix(kernel_table):
    surface = kernel_table.shape[-1]
    blocks = []
    for parity_x in range(2):
        for parity_y in range(2):
            for parity_z in range(2):
                window = kernel_table[1 - parity_x:7 - parity_x, 1 - parity_y:7 - parity_y, 1 - parity_z:7 - parity_z]
                blocks.append(window.reshape(216 * surface, surface))
    return jnp.concatenate(blocks, axis=1)


def far_local(blocked, weights):
    across = blocked.shape[0] - 2
    sideways = blocked.shape[2] - 2
    height = blocked.shape[4] - 2
    surface = blocked.shape[-1]
    pieces = []
    for offset_x in range(3):
        for offset_y in range(3):
            for offset_z in range(3):
                pieces.append(blocked[offset_x:offset_x + across, :, offset_y:offset_y + sideways, :, offset_z:offset_z + height, :, :])
    stacked = jnp.stack(pieces, 0).reshape((3, 3, 3, across, 2, sideways, 2, height, 2, surface))
    stacked = stacked.transpose(3, 5, 7, 0, 4, 1, 6, 2, 8, 9).reshape(across * sideways * height, 216 * surface)
    expansion = jnp.dot(stacked, weights, preferred_element_type=jnp.float32)
    expansion = expansion.reshape(across, sideways, height, 2, 2, 2, surface).transpose(0, 3, 1, 4, 2, 5, 6)
    return expansion.reshape(2 * across, 2 * sideways, 2 * height, surface)


def near_field(padded, near_matrix):
    across = padded.shape[0] - 2
    sideways = padded.shape[1] - 2
    height = padded.shape[2] - 2
    node_count = padded.shape[-1]
    pieces = []
    for offset_x in range(3):
        for offset_y in range(3):
            for offset_z in range(3):
                pieces.append(padded[offset_x:offset_x + across, offset_y:offset_y + sideways, offset_z:offset_z + height, :])
    stacked = jnp.concatenate(pieces, axis=-1).reshape(across * sideways * height, 27 * node_count)
    result = jnp.dot(stacked, near_matrix, preferred_element_type=jnp.float32)
    return result.reshape(across, sideways, height, node_count)


def reference(density, p2m_operator, m2l_table, near_table, l2p_operator):
    leaf_cells = density.reshape(LX, LY, LZ, Q)
    multipole = jnp.dot(leaf_cells.reshape(LX * LY * LZ, Q), p2m_operator, preferred_element_type=jnp.float32).astype(jnp.bfloat16)
    multipole = multipole.reshape(LX, LY, LZ, NE)
    weights = class_matrix(masked_table(m2l_table))
    blocked = jnp.pad(multipole, ((2, 2), (2, 2), (2, 2), (0, 0))).reshape(LX // 2 + 2, 2, LY // 2 + 2, 2, LZ // 2 + 2, 2, NE)

    def far_slab(position):
        slab_rows = lax.dynamic_slice_in_dim(blocked, position, 3, 0)
        return far_local(slab_rows, weights)

    expansion = lax.map(far_slab, jnp.arange(LX // 2, dtype=jnp.int32)).reshape(LX, LY, LZ, NE)
    rounded = expansion.astype(jnp.bfloat16)
    padded = jnp.pad(leaf_cells, ((1, 1), (1, 1), (1, 1), (0, 0)))
    near_matrix = near_table.reshape(27 * Q, Q)

    def near_slab(position):
        slab_rows = lax.dynamic_slice_in_dim(padded, position, 3, 0)
        return near_field(slab_rows, near_matrix)

    close_part = lax.map(near_slab, jnp.arange(LX, dtype=jnp.int32)).reshape(LX, LY, LZ, Q)
    distant_part = jnp.dot(rounded.reshape(LX * LY * LZ, NE), l2p_operator, preferred_element_type=jnp.float32)
    potential = close_part + distant_part.reshape(LX, LY, LZ, Q)
    return potential.reshape(LX, LY, LZ * Q)
```

```python
import jax
import jax.numpy as jnp
from jax import lax
from jax.experimental import pallas as pl
from jax.experimental.pallas import tpu as pltpu
from jax.sharding import PartitionSpec as P

BF16 = jnp.bfloat16
F32 = jnp.float32
WIDTH = 64
PAIR = 2 * WIDTH
VMEM_LIMIT = 40 * 1024 * 1024


def swapped(cells, axis, odd):
    count = lax.axis_size(axis)
    pairs = []
    for i in range(odd, count - 1, 2):
        pairs += [(i, i + 1), (i + 1, i)]
    return lax.ppermute(cells, axis, pairs)


def exchanged(cells, axis, dim):
    parity = lax.axis_index(axis) % 2
    size = cells.shape[dim]
    odd = swapped(cells, axis, 1)
    even = swapped(cells, axis, 0)

    def head(part):
        return lax.slice_in_dim(part, 0, 2, axis=dim)

    def tail(part):
        return lax.slice_in_dim(part, size - 2, size, axis=dim)

    low = jnp.where(parity == 0, tail(odd), tail(even))
    high = jnp.where(parity == 0, head(even), head(odd))
    return low, high


def sent(cells, axis, dim):
    parity = lax.axis_index(axis) % 2
    size = cells.shape[dim]
    head = lax.slice_in_dim(cells, 0, 2, axis=dim)
    tail = lax.slice_in_dim(cells, size - 2, size, axis=dim)
    even = swapped(jnp.where(parity == 0, tail, head), axis, 0)
    odd = swapped(jnp.where(parity == 0, head, tail), axis, 1)
    low = jnp.where(parity == 0, odd, even)
    high = jnp.where(parity == 0, even, odd)
    return low, high


def widened(density):
    low, high = exchanged(density, "gy", 1)
    wide = jnp.concatenate([low, density, high], axis=1)
    low, high = sent(wide, "gx", 0)
    return jnp.concatenate([low, wide, high], axis=0)


def square(block):
    rows, columns = block.shape
    if columns < WIDTH:
        block = jnp.concatenate([block, jnp.zeros((rows, WIDTH - columns), BF16)], axis=1)
    if rows < WIDTH:
        block = jnp.concatenate([block, jnp.zeros((WIDTH - rows, WIDTH), BF16)], axis=0)
    return block


def pack_kernel(p2m_ref, m2l_ref, near_ref, l2p_ref, far_out, near_out, p2m_out, l2p_out):
    blank = jnp.zeros((WIDTH, WIDTH), BF16)

    def far_blocks(offset_x, offset_y):
        inner = 2 <= offset_x <= 4 and 2 <= offset_y <= 4
        entries = []
        for offset_z in range(7):
            if inner and 2 <= offset_z <= 4:
                entries.append(blank)
            else:
                entries.append(square(m2l_ref[offset_x, offset_y, offset_z]))
        for s in range(6):
            far_out[offset_x, offset_y, s] = jnp.concatenate([entries[s + 1], entries[s]], axis=1)

    for offset_x in range(7):
        for offset_y in range(7):
            far_blocks(offset_x, offset_y)
    for offset_x in range(3):
        near_out[offset_x, 0] = jnp.zeros((2, PAIR, PAIR), BF16)
        near_out[offset_x, 4] = jnp.zeros((2, PAIR, PAIR), BF16)
        for offset_y in range(3):
            before, same, after = [near_ref[offset_x, offset_y, z] for z in range(3)]
            upper = jnp.concatenate([same, before], axis=1)
            lower = jnp.concatenate([after, same], axis=1)
            near_out[offset_x, offset_y + 1, 0] = jnp.concatenate([upper, lower], axis=0)
            upper = jnp.concatenate([blank, after], axis=1)
            lower = jnp.concatenate([before, blank], axis=1)
            near_out[offset_x, offset_y + 1, 1] = jnp.concatenate([upper, lower], axis=0)
    p2m = square(p2m_ref[...])
    p2m_out[...] = jnp.concatenate(
        [jnp.concatenate([p2m, blank], axis=1), jnp.concatenate([blank, p2m], axis=1)], axis=0
    )
    l2p = square(l2p_ref[...])
    double = jnp.concatenate(
        [jnp.concatenate([l2p, blank], axis=1), jnp.concatenate([blank, l2p], axis=1)], axis=0
    )
    empty = jnp.zeros((PAIR, PAIR), BF16)
    l2p_out[...] = jnp.concatenate(
        [jnp.concatenate([double, empty], axis=1), jnp.concatenate([empty, double], axis=1)], axis=0
    )


def packed(p2m_operator, m2l_table, near_table, l2p_operator):
    shapes = [(7, 7, 6, WIDTH, PAIR), (3, 5, 2, PAIR, PAIR), (PAIR, PAIR), (2 * PAIR, 2 * PAIR)]
    return pl.pallas_call(
        pack_kernel,
        out_shape=[pltpu.VMEM(shape, BF16) for shape in shapes],
        in_specs=[pl.BlockSpec(memory_space=pltpu.VMEM)] * 4,
        out_specs=[pl.BlockSpec(memory_space=pltpu.VMEM)] * 4,
        compiler_params=pltpu.CompilerParams(vmem_limit_bytes=VMEM_LIMIT),
        cost_estimate=pl.CostEstimate(flops=4000000, bytes_accessed=10000000, transcendentals=0),
        name="pack",
    )(p2m_operator, m2l_table, near_table, l2p_operator)


def shifted(rows):
    place = lax.broadcasted_iota(jnp.int32, rows.shape, 0) % 8
    before = jnp.where(place == 0, 0.0, jnp.roll(rows, 1, axis=0))
    after = jnp.where(place == 7, 0.0, jnp.roll(rows, -1, axis=0))
    return before, rows, after


def window_rows(slab, first):
    if first == -1:
        blank = jnp.zeros_like(slab[:8])
        parts = [blank, slab[0:8], blank, slab[16:24]]
        return jnp.concatenate(parts, axis=0)
    if first == 5:
        blank = jnp.zeros_like(slab[:8])
        parts = [slab[40:48], blank, slab[56:64], blank]
        return jnp.concatenate(parts, axis=0)
    return slab[8 * first : 8 * first + 32]


def main_kernel(cells_ref, far_ref, near_ref, p2m_ref, l2p_ref, out_ref, rows_ref, out_rows):
    pairs = cells_ref.shape[2] // PAIR
    for x in range(8):
        for pair in range(pairs):
            rows_ref[pl.ds(x * pairs + pair, 8, stride=8 * pairs), :] = cells_ref[
                x, :, pair * PAIR : (pair + 1) * PAIR
            ].astype(F32)
    cells = rows_ref[...]
    multipole = jnp.dot(cells.astype(BF16), p2m_ref[...], preferred_element_type=F32)
    multipole = multipole.astype(BF16).astype(F32)
    sources = shifted(multipole)
    far = jnp.zeros((64, 2 * PAIR), F32)
    for offset_x in range(7):
        chunks = []
        for j in range(6):
            for b in range(3):
                upper = window_rows(sources[b][64 * j : 64 * j + 64], offset_x - 1)
                lower = window_rows(sources[b][64 * j + 128 : 64 * j + 192], offset_x - 1)
                chunks.append(jnp.concatenate([upper, lower], axis=0).astype(BF16))
        weights = jnp.concatenate(
            [
                far_ref[offset_x, 1:7].reshape(36 * WIDTH, PAIR),
                far_ref[offset_x, 0:6].reshape(36 * WIDTH, PAIR),
            ],
            axis=1,
        )
        far += jnp.dot(jnp.concatenate(chunks, axis=1), weights, preferred_element_type=F32)
    before, same, after = shifted(cells)
    lane = lax.broadcasted_iota(jnp.int32, cells.shape, 1)
    beside = jnp.where(lane < WIDTH, after, before)
    total = jnp.dot(far.astype(BF16), l2p_ref[...], preferred_element_type=F32)
    for offset_x in range(3):
        chunks = []
        for j in range(1, 5):
            for kind in (same, beside):
                upper = window_rows(kind[64 * j : 64 * j + 64], offset_x + 1)
                lower = window_rows(kind[64 * j + 128 : 64 * j + 192], offset_x + 1)
                chunks.append(jnp.concatenate([upper, lower], axis=0).astype(BF16))
        weights = jnp.concatenate(
            [
                near_ref[offset_x, 1:5].reshape(8 * PAIR, PAIR),
                near_ref[offset_x, 0:4].reshape(8 * PAIR, PAIR),
            ],
            axis=1,
        )
        total += jnp.dot(jnp.concatenate(chunks, axis=1), weights, preferred_element_type=F32)
    for y in range(4):
        out_rows[32 * y : 32 * y + 32, :] = total[
            32 * (y // 2) : 32 * (y // 2) + 32, PAIR * (y % 2) : PAIR * (y % 2) + PAIR
        ]
    for x in range(4):
        for pair in range(pairs):
            out_ref[x, :, pair * PAIR : (pair + 1) * PAIR] = out_rows[
                pl.ds(x * pairs + pair, 4, stride=4 * pairs), :
            ]


def local(density, p2m_operator, m2l_table, near_table, l2p_operator):
    tables = packed(p2m_operator, m2l_table, near_table, l2p_operator)
    cells = widened(density)
    return pl.pallas_call(
        main_kernel,
        out_shape=jax.ShapeDtypeStruct(density.shape, F32),
        in_specs=[pl.BlockSpec(memory_space=pltpu.VMEM)] * 5,
        out_specs=pl.BlockSpec(memory_space=pltpu.VMEM),
        scratch_shapes=[pltpu.VMEM((512, PAIR), F32), pltpu.VMEM((128, PAIR), F32)],
        compiler_params=pltpu.CompilerParams(vmem_limit_bytes=VMEM_LIMIT),
        cost_estimate=pl.CostEstimate(flops=600000000, bytes_accessed=10000000, transcendentals=0),
        name="main",
    )(cells, *tables)


def solution(mesh):
    placed = (P("gx", "gy", None), P(), P(), P(), P())
    return jax.shard_map(
        local, mesh=mesh, in_specs=placed, out_specs=P("gx", "gy", None), check_vma=False
    )
```

```python
import jax
import jax.numpy as jnp
from jax import lax
from jax.experimental import pallas as pl
from jax.experimental.pallas import tpu as pltpu
from jax.sharding import PartitionSpec as P

BF16 = jnp.bfloat16
F32 = jnp.float32
WIDTH = 64
PAIR = 2 * WIDTH
VMEM_LIMIT = 40 * 1024 * 1024


def swapped(cells, axis, odd):
    count = lax.axis_size(axis)
    pairs = []
    for i in range(odd, count - 1, 2):
        pairs += [(i, i + 1), (i + 1, i)]
    return lax.ppermute(cells, axis, pairs)


def exchanged(cells, axis, dim):
    parity = lax.axis_index(axis) % 2
    size = cells.shape[dim]
    odd = swapped(cells, axis, 1)
    even = swapped(cells, axis, 0)

    def head(part):
        return lax.slice_in_dim(part, 0, 2, axis=dim)

    def tail(part):
        return lax.slice_in_dim(part, size - 2, size, axis=dim)

    low = jnp.where(parity == 0, tail(odd), tail(even))
    high = jnp.where(parity == 0, head(even), head(odd))
    return low, high


def sent(cells, axis, dim):
    parity = lax.axis_index(axis) % 2
    size = cells.shape[dim]
    head = lax.slice_in_dim(cells, 0, 2, axis=dim)
    tail = lax.slice_in_dim(cells, size - 2, size, axis=dim)
    even = swapped(jnp.where(parity == 0, tail, head), axis, 0)
    odd = swapped(jnp.where(parity == 0, head, tail), axis, 1)
    low = jnp.where(parity == 0, odd, even)
    high = jnp.where(parity == 0, even, odd)
    return low, high


def widened(low, own, high):
    wide = jnp.concatenate([low, own, high], axis=1)
    low, high = sent(wide, "gx", 0)
    return jnp.concatenate([low, wide, high], axis=0)


def square(block):
    rows, columns = block.shape
    if columns < WIDTH:
        block = jnp.concatenate([block, jnp.zeros((rows, WIDTH - columns), BF16)], axis=1)
    if rows < WIDTH:
        block = jnp.concatenate([block, jnp.zeros((WIDTH - rows, WIDTH), BF16)], axis=0)
    return block


def pack_kernel(
    own_hbm, p2m_hbm, m2l_hbm, near_hbm, l2p_hbm,
    own_out, far_out, near_out, p2m_out, l2p_out,
    p2m_ref, m2l_ref, near_ref, l2p_ref, sems,
):
    copies = [
        pltpu.make_async_copy(m2l_hbm.at[offset_x], m2l_ref.at[offset_x], sems.at[offset_x])
        for offset_x in range(7)
    ]
    pieces = ((near_hbm, near_ref), (p2m_hbm, p2m_ref), (l2p_hbm, l2p_ref), (own_hbm, own_out))
    for index, (source, target) in enumerate(pieces):
        copies.append(pltpu.make_async_copy(source, target, sems.at[7 + index]))
    for copy in copies:
        copy.start()
    blank = jnp.zeros((WIDTH, WIDTH), BF16)

    def far_blocks(offset_x, offset_y):
        inner = 2 <= offset_x <= 4 and 2 <= offset_y <= 4
        entries = []
        for offset_z in range(7):
            if inner and 2 <= offset_z <= 4:
                entries.append(blank)
            else:
                entries.append(square(m2l_ref[offset_x, offset_y, offset_z]))
        for s in range(6):
            far_out[offset_x, offset_y, s] = jnp.concatenate([entries[s + 1], entries[s]], axis=1)

    for offset_x in range(7):
        copies[offset_x].wait()
        for offset_y in range(7):
            far_blocks(offset_x, offset_y)
    for copy in copies[7:]:
        copy.wait()
    for offset_x in range(3):
        for offset_y in range(3):
            before, same, after = [near_ref[offset_x, offset_y, z] for z in range(3)]
            upper = jnp.concatenate([same, before], axis=1)
            lower = jnp.concatenate([after, same], axis=1)
            near_out[offset_x, offset_y, 0] = jnp.concatenate([upper, lower], axis=0)
            upper = jnp.concatenate([blank, after], axis=1)
            lower = jnp.concatenate([before, blank], axis=1)
            near_out[offset_x, offset_y, 1] = jnp.concatenate([upper, lower], axis=0)
    p2m = square(p2m_ref[...])
    p2m_out[...] = jnp.concatenate(
        [jnp.concatenate([p2m, blank], axis=1), jnp.concatenate([blank, p2m], axis=1)], axis=0
    )
    l2p = square(l2p_ref[...])
    l2p_out[...] = jnp.concatenate(
        [jnp.concatenate([l2p, blank], axis=1), jnp.concatenate([blank, l2p], axis=1)], axis=0
    )


def packed(density, p2m_operator, m2l_table, near_table, l2p_operator):
    shapes = [density.shape, (7, 7, 6, WIDTH, PAIR), (3, 3, 2, PAIR, PAIR), (PAIR, PAIR), (PAIR, PAIR)]
    return pl.pallas_call(
        pack_kernel,
        out_shape=[pltpu.VMEM(shape, BF16) for shape in shapes],
        in_specs=[pl.BlockSpec(memory_space=pltpu.HBM)] * 5,
        out_specs=[pl.BlockSpec(memory_space=pltpu.VMEM)] * 5,
        scratch_shapes=[
            pltpu.VMEM(p2m_operator.shape[::-1], BF16),
            pltpu.VMEM(m2l_table.shape, BF16),
            pltpu.VMEM(near_table.shape, BF16),
            pltpu.VMEM(l2p_operator.shape, BF16),
            pltpu.SemaphoreType.DMA((11,)),
        ],
        compiler_params=pltpu.CompilerParams(vmem_limit_bytes=VMEM_LIMIT),
        cost_estimate=pl.CostEstimate(flops=4000000, bytes_accessed=10000000, transcendentals=0),
        name="pack",
    )(
        *(
            pltpu.with_memory_space_constraint(array, pltpu.HBM)
            for array in (density, p2m_operator.T, m2l_table, near_table, l2p_operator)
        )
    )


def shifted(rows):
    place = lax.broadcasted_iota(jnp.int32, rows.shape, 0) % 8
    before = jnp.where(place == 0, 0.0, jnp.roll(rows, 1, axis=0))
    after = jnp.where(place == 7, 0.0, jnp.roll(rows, -1, axis=0))
    return before, rows, after


def parity_window(slabs, offset, size):
    first = offset - 1
    if 0 <= first <= 4:
        return slabs[size * first : size * first + 4 * size]
    blank = jnp.zeros((size, slabs.shape[1]), slabs.dtype)
    if first < 0:
        parts = [blank, slabs[0:size], blank, slabs[2 * size : 3 * size]]
    else:
        parts = [slabs[5 * size : 6 * size], blank, slabs[7 * size : 8 * size], blank]
    return jnp.concatenate(parts, axis=0)


def main_kernel(cells_ref, far_ref, near_ref, p2m_ref, l2p_ref, out_ref, rows_ref, out_rows, far_rows, near_rows):
    pairs = cells_ref.shape[2] // PAIR
    for x in range(8):
        for pair in range(pairs):
            rows_ref[pl.ds(x * pairs + pair, 8, stride=8 * pairs), :] = cells_ref[
                x, :, pair * PAIR : (pair + 1) * PAIR
            ].astype(F32)
    cells = rows_ref[...]
    multipole = lax.dot_general(
        cells.astype(BF16), p2m_ref[...], (((1,), (1,)), ((), ())), preferred_element_type=F32
    )
    multipole = multipole.astype(BF16).astype(F32)
    sources = shifted(multipole)
    for offset_x in range(7):
        for b in range(3):
            for y in range(8):
                far_rows[offset_x, b, 32 * y : 32 * y + 32] = parity_window(
                    sources[b][64 * y : 64 * y + 64], offset_x, 8
                ).astype(BF16)
    before, same, after = shifted(cells)
    lane = lax.broadcasted_iota(jnp.int32, cells.shape, 1)
    beside = jnp.where(lane < WIDTH, after, before)
    for offset_x in range(3):
        for k, kind in enumerate((same, beside)):
            for y in range(1, 7):
                near_rows[offset_x, k, 32 * (y - 1) : 32 * y] = kind[
                    64 * y + 8 * (offset_x + 1) : 64 * y + 8 * (offset_x + 5)
                ].astype(BF16)
    far = jnp.zeros((128, PAIR), F32)
    for offset_x in range(7):
        chunks, weights = [], []
        for offset_y in range(7):
            inner = 2 <= offset_x <= 4 and 2 <= offset_y <= 4
            for b in range(3):
                if inner and b == 1:
                    continue
                chunks.append(parity_window(far_rows[offset_x, b], offset_y, 32))
                weights.append(far_ref[offset_x, offset_y, 2 * b : 2 * b + 2].reshape(PAIR, PAIR))
        far += jnp.dot(
            jnp.concatenate(chunks, axis=1), jnp.concatenate(weights, axis=0), preferred_element_type=F32
        )
    total = jnp.dot(far.astype(BF16), l2p_ref[...], preferred_element_type=F32)
    for offset_x in range(3):
        chunks = []
        for offset_y in range(3):
            for k in range(2):
                chunks.append(near_rows[offset_x, k, 32 * offset_y : 32 * offset_y + 128])
        total += jnp.dot(
            jnp.concatenate(chunks, axis=1),
            near_ref[offset_x].reshape(6 * PAIR, PAIR),
            preferred_element_type=F32,
        )
    out_rows[...] = total
    for x in range(4):
        for pair in range(pairs):
            out_ref[x, :, pair * PAIR : (pair + 1) * PAIR] = out_rows[
                pl.ds(x * pairs + pair, 4, stride=4 * pairs), :
            ]


def local(density, p2m_operator, m2l_table, near_table, l2p_operator):
    low, high = exchanged(density, "gy", 1)
    own, *tables = packed(density, p2m_operator, m2l_table, near_table, l2p_operator)
    cells = widened(low, own, high)
    return pl.pallas_call(
        main_kernel,
        out_shape=jax.ShapeDtypeStruct(density.shape, F32),
        in_specs=[pl.BlockSpec(memory_space=pltpu.VMEM)] * 5,
        out_specs=pl.BlockSpec(memory_space=pltpu.VMEM),
        scratch_shapes=[
            pltpu.VMEM((512, PAIR), F32),
            pltpu.VMEM((128, PAIR), F32),
            pltpu.VMEM((7, 3, 256, PAIR), BF16),
            pltpu.VMEM((3, 2, 192, PAIR), BF16),
        ],
        compiler_params=pltpu.CompilerParams(vmem_limit_bytes=VMEM_LIMIT),
        cost_estimate=pl.CostEstimate(flops=600000000, bytes_accessed=10000000, transcendentals=0),
        name="main",
    )(cells, *tables)


def solution(mesh):
    placed = (P("gx", "gy", None), P(), P(), P(), P())
    return jax.shard_map(
        local, mesh=mesh, in_specs=placed, out_specs=P("gx", "gy", None), check_vma=False
    )
```

```python
import jax
import jax.numpy as jnp
from jax import lax
from jax.experimental import pallas as pl
from jax.experimental.pallas import tpu as pltpu
from jax.sharding import PartitionSpec as P

BF16 = jnp.bfloat16
F32 = jnp.float32
WIDTH = 64
PAIR = 2 * WIDTH
VMEM_LIMIT = 40 * 1024 * 1024


AXES = ("gx", "gy")


def swapped(cells, axis, odd):
    sizes = [lax.axis_size(name) for name in AXES]
    dim = AXES.index(axis)
    pairs = []
    for place in range(sizes[0] * sizes[1]):
        at = list(divmod(place, sizes[1]))
        partner = (at[dim] - odd) ^ 1
        if at[dim] >= odd and partner + odd < sizes[dim]:
            at[dim] = partner + odd
        elif (at[1 - dim] ^ 1) < sizes[1 - dim]:
            at[1 - dim] ^= 1
        else:
            continue
        pairs.append((place, at[0] * sizes[1] + at[1]))
    return lax.ppermute(cells, AXES, pairs)


def chosen(axis, even_low, odd_low, even_high, odd_high):
    place = lax.axis_index(axis)
    lower = place % 2 == 0
    low = jnp.where(place == 0, 0, jnp.where(lower, odd_low, even_low))
    high = jnp.where(place == lax.axis_size(axis) - 1, 0, jnp.where(lower, even_high, odd_high))
    return low.astype(BF16), high.astype(BF16)


def exchanged(cells, axis, dim):
    size = cells.shape[dim]
    odd = swapped(cells, axis, 1)
    even = swapped(cells, axis, 0)

    def head(part):
        return lax.slice_in_dim(part, 0, 2, axis=dim)

    def tail(part):
        return lax.slice_in_dim(part, size - 2, size, axis=dim)

    return chosen(axis, tail(even), tail(odd), head(even), head(odd))


def traded(cells, axis, dim):
    lower = lax.axis_index(axis) % 2 == 0
    size = cells.shape[dim]
    head = lax.slice_in_dim(cells, 0, 2, axis=dim)
    tail = lax.slice_in_dim(cells, size - 2, size, axis=dim)
    even = swapped(jnp.where(lower, tail, head), axis, 0)
    odd = swapped(jnp.where(lower, head, tail), axis, 1)
    return even, odd


def square(block):
    rows, columns = block.shape
    if columns < WIDTH:
        block = jnp.concatenate([block, jnp.zeros((rows, WIDTH - columns), BF16)], axis=1)
    if rows < WIDTH:
        block = jnp.concatenate([block, jnp.zeros((WIDTH - rows, WIDTH), BF16)], axis=0)
    return block


def pack_kernel(
    own_hbm, p2m_hbm, m2l_hbm, near_hbm, l2p_hbm,
    own_out, far_out, near_out, p2m_out, l2p_out,
    p2m_ref, m2l_ref, near_ref, l2p_ref, sems,
):
    copies = [
        pltpu.make_async_copy(m2l_hbm.at[offset_x], m2l_ref.at[offset_x], sems.at[offset_x])
        for offset_x in range(7)
    ]
    pieces = ((near_hbm, near_ref), (p2m_hbm, p2m_ref), (l2p_hbm, l2p_ref), (own_hbm, own_out))
    for index, (source, target) in enumerate(pieces):
        copies.append(pltpu.make_async_copy(source, target, sems.at[7 + index]))
    for copy in copies:
        copy.start()
    blank = jnp.zeros((WIDTH, WIDTH), BF16)

    def far_blocks(offset_x, offset_y):
        inner = 2 <= offset_x <= 4 and 2 <= offset_y <= 4
        entries = []
        for offset_z in range(7):
            if inner and 2 <= offset_z <= 4:
                entries.append(blank)
            else:
                entries.append(square(m2l_ref[offset_x, offset_y, offset_z]))
        for s in range(6):
            far_out[offset_x, offset_y, s] = jnp.concatenate([entries[s + 1], entries[s]], axis=1)

    for offset_x in range(7):
        copies[offset_x].wait()
        for offset_y in range(7):
            far_blocks(offset_x, offset_y)
    for copy in copies[7:]:
        copy.wait()
    for offset_x in range(3):
        for offset_y in range(3):
            before, same, after = [near_ref[offset_x, offset_y, z] for z in range(3)]
            upper = jnp.concatenate([same, before], axis=1)
            lower = jnp.concatenate([after, same], axis=1)
            near_out[offset_x, offset_y, 0] = jnp.concatenate([upper, lower], axis=0)
            upper = jnp.concatenate([blank, after], axis=1)
            lower = jnp.concatenate([before, blank], axis=1)
            near_out[offset_x, offset_y, 1] = jnp.concatenate([upper, lower], axis=0)
    p2m = square(p2m_ref[...])
    p2m_out[...] = jnp.concatenate(
        [jnp.concatenate([p2m, blank], axis=1), jnp.concatenate([blank, p2m], axis=1)], axis=0
    )
    l2p = square(l2p_ref[...])
    l2p_out[...] = jnp.concatenate(
        [jnp.concatenate([l2p, blank], axis=1), jnp.concatenate([blank, l2p], axis=1)], axis=0
    )


def packed(density, p2m_operator, m2l_table, near_table, l2p_operator):
    shapes = [density.shape, (7, 7, 6, WIDTH, PAIR), (3, 3, 2, PAIR, PAIR), (PAIR, PAIR), (PAIR, PAIR)]
    return pl.pallas_call(
        pack_kernel,
        out_shape=[pltpu.VMEM(shape, BF16) for shape in shapes],
        in_specs=[pl.BlockSpec(memory_space=pltpu.HBM)] * 5,
        out_specs=[pl.BlockSpec(memory_space=pltpu.VMEM)] * 5,
        scratch_shapes=[
            pltpu.VMEM(p2m_operator.shape[::-1], BF16),
            pltpu.VMEM(m2l_table.shape, BF16),
            pltpu.VMEM(near_table.shape, BF16),
            pltpu.VMEM(l2p_operator.shape, BF16),
            pltpu.SemaphoreType.DMA((11,)),
        ],
        compiler_params=pltpu.CompilerParams(vmem_limit_bytes=VMEM_LIMIT),
        cost_estimate=pl.CostEstimate(flops=4000000, bytes_accessed=10000000, transcendentals=0),
        name="pack",
    )(
        *(
            pltpu.with_memory_space_constraint(array, pltpu.HBM)
            for array in (density, p2m_operator.T, m2l_table, near_table, l2p_operator)
        )
    )


def shifted(rows):
    place = lax.broadcasted_iota(jnp.int32, rows.shape, 0) % 8
    before = jnp.where(place == 0, 0.0, jnp.roll(rows, 1, axis=0))
    after = jnp.where(place == 7, 0.0, jnp.roll(rows, -1, axis=0))
    return before, rows, after


def parity_window(slabs, offset, size):
    first = offset - 1
    if 0 <= first <= 4:
        return slabs[size * first : size * first + 4 * size]
    blank = jnp.zeros((size, slabs.shape[1]), slabs.dtype)
    if first < 0:
        parts = [blank, slabs[0:size], blank, slabs[2 * size : 3 * size]]
    else:
        parts = [slabs[5 * size : 6 * size], blank, slabs[7 * size : 8 * size], blank]
    return jnp.concatenate(parts, axis=0)


def main_kernel(
    own_ref, even_ref, odd_ref, far_ref, near_ref, p2m_ref, l2p_ref,
    out_ref, rows_ref, out_rows, far_rows, near_rows,
):
    pairs = own_ref.shape[2] // PAIR
    place = lax.axis_index("gx")
    lower = lax.rem(place, 2) == 0
    for x in range(8):
        for pair in range(pairs):
            lanes = slice(pair * PAIR, (pair + 1) * PAIR)
            if 2 <= x < 6:
                cells = own_ref[x - 2, :, lanes].astype(F32)
            else:
                even = even_ref[x % 2, :, lanes].astype(F32)
                odd = odd_ref[x % 2, :, lanes].astype(F32)
                if x < 2:
                    cells = jnp.where(place == 0, 0.0, jnp.where(lower, odd, even))
                else:
                    last = place == lax.axis_size("gx") - 1
                    cells = jnp.where(last, 0.0, jnp.where(lower, even, odd))
            rows_ref[pl.ds(x * pairs + pair, 8, stride=8 * pairs), :] = cells
    cells = rows_ref[...]
    multipole = lax.dot_general(
        cells.astype(BF16), p2m_ref[...], (((1,), (1,)), ((), ())), preferred_element_type=F32
    )
    multipole = multipole.astype(BF16).astype(F32)
    sources = shifted(multipole)
    for offset_x in range(7):
        for b in range(3):
            for y in range(8):
                far_rows[offset_x, b, 32 * y : 32 * y + 32] = parity_window(
                    sources[b][64 * y : 64 * y + 64], offset_x, 8
                ).astype(BF16)
    before, same, after = shifted(cells)
    lane = lax.broadcasted_iota(jnp.int32, cells.shape, 1)
    beside = jnp.where(lane < WIDTH, after, before)
    for offset_x in range(3):
        for k, kind in enumerate((same, beside)):
            for y in range(1, 7):
                near_rows[offset_x, k, 32 * (y - 1) : 32 * y] = kind[
                    64 * y + 8 * (offset_x + 1) : 64 * y + 8 * (offset_x + 5)
                ].astype(BF16)
    far = jnp.zeros((128, PAIR), F32)
    for offset_x in range(7):
        chunks, weights = [], []
        for offset_y in range(7):
            inner = 2 <= offset_x <= 4 and 2 <= offset_y <= 4
            for b in range(3):
                if inner and b == 1:
                    continue
                chunks.append(parity_window(far_rows[offset_x, b], offset_y, 32))
                weights.append(far_ref[offset_x, offset_y, 2 * b : 2 * b + 2].reshape(PAIR, PAIR))
        far += jnp.dot(
            jnp.concatenate(chunks, axis=1), jnp.concatenate(weights, axis=0), preferred_element_type=F32
        )
    total = jnp.dot(far.astype(BF16), l2p_ref[...], preferred_element_type=F32)
    for offset_x in range(3):
        chunks = []
        for offset_y in range(3):
            for k in range(2):
                chunks.append(near_rows[offset_x, k, 32 * offset_y : 32 * offset_y + 128])
        total += jnp.dot(
            jnp.concatenate(chunks, axis=1),
            near_ref[offset_x].reshape(6 * PAIR, PAIR),
            preferred_element_type=F32,
        )
    out_rows[...] = total
    for x in range(4):
        for pair in range(pairs):
            out_ref[x, :, pair * PAIR : (pair + 1) * PAIR] = out_rows[
                pl.ds(x * pairs + pair, 4, stride=4 * pairs), :
            ]


def local(density, p2m_operator, m2l_table, near_table, l2p_operator):
    low, high = exchanged(density, "gy", 1)
    own, *tables = packed(density, p2m_operator, m2l_table, near_table, l2p_operator)
    wide = jnp.concatenate([low, own, high], axis=1)
    even, odd = traded(wide, "gx", 0)
    return pl.pallas_call(
        main_kernel,
        out_shape=jax.ShapeDtypeStruct(density.shape, F32),
        in_specs=[pl.BlockSpec(memory_space=pltpu.VMEM)] * 7,
        out_specs=pl.BlockSpec(memory_space=pltpu.VMEM),
        scratch_shapes=[
            pltpu.VMEM((512, PAIR), F32),
            pltpu.VMEM((128, PAIR), F32),
            pltpu.VMEM((7, 3, 256, PAIR), BF16),
            pltpu.VMEM((3, 2, 192, PAIR), BF16),
        ],
        compiler_params=pltpu.CompilerParams(vmem_limit_bytes=VMEM_LIMIT),
        cost_estimate=pl.CostEstimate(flops=600000000, bytes_accessed=10000000, transcendentals=0),
        name="main",
    )(wide, even, odd, *tables)


def solution(mesh):
    placed = (P("gx", "gy", None), P(), P(), P(), P())
    return jax.shard_map(
        local, mesh=mesh, in_specs=placed, out_specs=P("gx", "gy", None), check_vma=False
    )
```

```python
import jax
import jax.numpy as jnp
from jax import lax
from jax.experimental import pallas as pl
from jax.experimental.pallas import tpu as pltpu
from jax.sharding import PartitionSpec as P

BF16 = jnp.bfloat16
F32 = jnp.float32
WIDTH = 64
PAIR = 2 * WIDTH
VMEM_LIMIT = 40 * 1024 * 1024
SMALL_LIMIT = 8 * 1024 * 1024


AXES = ("gx", "gy")


def swapped(cells, axis, odd):
    sizes = [lax.axis_size(name) for name in AXES]
    dim = AXES.index(axis)
    pairs = []
    for place in range(sizes[0] * sizes[1]):
        at = list(divmod(place, sizes[1]))
        partner = (at[dim] - odd) ^ 1
        if at[dim] >= odd and partner + odd < sizes[dim]:
            at[dim] = partner + odd
        elif (at[1 - dim] ^ 1) < sizes[1 - dim]:
            at[1 - dim] ^= 1
        else:
            continue
        pairs.append((place, at[0] * sizes[1] + at[1]))
    return lax.ppermute(cells, AXES, pairs)


def square(block):
    rows, columns = block.shape
    if columns < WIDTH:
        block = jnp.concatenate([block, jnp.zeros((rows, WIDTH - columns), BF16)], axis=1)
    if rows < WIDTH:
        block = jnp.concatenate([block, jnp.zeros((WIDTH - rows, WIDTH), BF16)], axis=0)
    return block


def first_kernel(out_ref):
    out_ref[...] = jnp.zeros_like(out_ref)


def first():
    return pl.pallas_call(
        first_kernel,
        out_shape=pltpu.VMEM((8, PAIR), F32),
        out_specs=pl.BlockSpec(memory_space=pltpu.VMEM),
        compiler_params=pltpu.CompilerParams(vmem_limit_bytes=1024 * 1024),
        cost_estimate=pl.CostEstimate(flops=10000000000, bytes_accessed=1000, transcendentals=0),
        name="first",
    )()


def pack_kernel(first_ref, p2m_ref, m2l_ref, near_ref, l2p_ref, far_out, near_out, p2m_out, l2p_out):
    blank = jnp.zeros((WIDTH, WIDTH), BF16)

    def far_blocks(offset_x, offset_y):
        inner = 2 <= offset_x <= 4 and 2 <= offset_y <= 4
        entries = []
        for offset_z in range(7):
            if inner and 2 <= offset_z <= 4:
                entries.append(blank)
            else:
                entries.append(square(m2l_ref[offset_x, offset_y, offset_z]))
        for s in range(6):
            far_out[offset_x, offset_y, s] = jnp.concatenate([entries[s + 1], entries[s]], axis=1)

    for offset_x in range(7):
        for offset_y in range(7):
            far_blocks(offset_x, offset_y)
    for offset_x in range(3):
        for offset_y in range(3):
            before, same, after = [near_ref[offset_x, offset_y, z] for z in range(3)]
            upper = jnp.concatenate([same, before], axis=1)
            lower = jnp.concatenate([after, same], axis=1)
            near_out[offset_x, offset_y, 0] = jnp.concatenate([upper, lower], axis=0)
            upper = jnp.concatenate([blank, after], axis=1)
            lower = jnp.concatenate([before, blank], axis=1)
            near_out[offset_x, offset_y, 1] = jnp.concatenate([upper, lower], axis=0)
    p2m = square(p2m_ref[...])
    p2m_out[...] = jnp.concatenate(
        [jnp.concatenate([p2m, blank], axis=1), jnp.concatenate([blank, p2m], axis=1)], axis=0
    )
    l2p = square(l2p_ref[...])
    l2p_out[...] = jnp.concatenate(
        [jnp.concatenate([l2p, blank], axis=1), jnp.concatenate([blank, l2p], axis=1)], axis=0
    )


def packed(start, p2m_operator, m2l_table, near_table, l2p_operator):
    shapes = [(7, 7, 6, WIDTH, PAIR), (3, 3, 2, PAIR, PAIR), (PAIR, PAIR), (PAIR, PAIR)]
    return pl.pallas_call(
        pack_kernel,
        out_shape=[pltpu.VMEM(shape, BF16) for shape in shapes],
        in_specs=[pl.BlockSpec(memory_space=pltpu.VMEM)] * 5,
        out_specs=[pl.BlockSpec(memory_space=pltpu.VMEM)] * 4,
        compiler_params=pltpu.CompilerParams(vmem_limit_bytes=VMEM_LIMIT),
        cost_estimate=pl.CostEstimate(flops=4000000, bytes_accessed=10000000, transcendentals=0),
        name="pack",
    )(start, p2m_operator.T, m2l_table, near_table, l2p_operator)


def from_neighbours(axis, even_low, odd_low, even_high, odd_high):
    place = lax.axis_index(axis)
    lower = lax.rem(place, 2) == 0
    low = jnp.where(place == 0, 0.0, jnp.where(lower, odd_low, even_low))
    last = place == lax.axis_size(axis) - 1
    high = jnp.where(last, 0.0, jnp.where(lower, even_high, odd_high))
    return low, high


def join_kernel(after_ref, own_ref, odd_ref, even_ref, own_out, odd_out, even_out, rows_ref):
    pairs = own_ref.shape[2] // PAIR
    for pair in range(pairs):
        lanes = slice(pair * PAIR, (pair + 1) * PAIR)

        def part(ref, x):
            return ref[x, :, lanes].astype(F32)

        for x in range(8):
            if 2 <= x < 6:
                cells = part(own_ref, x - 2)
            else:
                low, high = from_neighbours(
                    "gx",
                    *((part(even_ref, 2 + x), part(odd_ref, 2 + x)) if x < 2 else (0.0, 0.0)),
                    *((part(even_ref, x - 6), part(odd_ref, x - 6)) if x > 5 else (0.0, 0.0)),
                )
                cells = low if x < 2 else high
            rows_ref[pl.ds(x * pairs + pair, 4, stride=8 * pairs), :] = cells
    rows = rows_ref[...]
    own_out[...] = rows.astype(BF16)
    lower = lax.rem(lax.axis_index("gy"), 2) == 0
    head, tail = rows[:128], rows[128:]
    even_out[...] = jnp.where(lower, tail, head).astype(BF16)
    odd_out[...] = jnp.where(lower, head, tail).astype(BF16)


def joined(after, own, odd, even):
    return pl.pallas_call(
        join_kernel,
        out_shape=[pltpu.VMEM((rows, PAIR), BF16) for rows in (256, 128, 128)],
        in_specs=[pl.BlockSpec(memory_space=pltpu.VMEM)] * 4,
        out_specs=[pl.BlockSpec(memory_space=pltpu.VMEM)] * 3,
        scratch_shapes=[pltpu.VMEM((256, PAIR), F32)],
        compiler_params=pltpu.CompilerParams(vmem_limit_bytes=SMALL_LIMIT),
        cost_estimate=pl.CostEstimate(flops=1000000, bytes_accessed=100000, transcendentals=0),
        name="join",
    )(after, own, odd, even)


def shifted(rows):
    place = lax.broadcasted_iota(jnp.int32, rows.shape, 0) % 8
    before = jnp.where(place == 0, 0.0, jnp.roll(rows, 1, axis=0))
    after = jnp.where(place == 7, 0.0, jnp.roll(rows, -1, axis=0))
    return before, rows, after


def column_windows(cells, p2m_ref, far_rows, near_rows):
    multipole = lax.dot_general(
        cells.astype(BF16), p2m_ref[...], (((1,), (1,)), ((), ())), preferred_element_type=F32
    )
    sources = shifted(multipole.astype(BF16).astype(F32))
    blank = jnp.zeros((8, PAIR), F32)
    for b in range(3):
        for y in range(4):
            slab = sources[b][64 * y : 64 * y + 64]
            for offset_x in range(7):
                if offset_x == 0:
                    window = jnp.concatenate([blank, slab[0:8], blank, slab[16:24]], axis=0)
                elif offset_x == 6:
                    window = jnp.concatenate([slab[40:48], blank, slab[56:64], blank], axis=0)
                else:
                    window = slab[8 * (offset_x - 1) : 8 * (offset_x + 3)]
                far_rows[offset_x, b, 32 * y : 32 * y + 32] = window.astype(BF16)
    before, same, after = shifted(cells)
    lane = lax.broadcasted_iota(jnp.int32, cells.shape, 1)
    beside = jnp.where(lane < WIDTH, after, before)
    for k, kind in enumerate((same, beside)):
        for y in range(4):
            for offset_x in range(3):
                near_rows[offset_x, k, 32 * y : 32 * y + 32] = kind[
                    64 * y + 8 * (offset_x + 1) : 64 * y + 8 * (offset_x + 5)
                ].astype(BF16)


def spans(places, first, offset, parity):
    found = [
        (target, places.index(target + offset + first))
        for target in range(4)
        if target + offset + first in places
        and not (parity and ((offset == 0 and target % 2 == 0) or (offset == 6 and target % 2 == 1)))
    ]
    return found


def add_products(far, near, places, far_rows, near_rows, far_ref, near_ref):
    for offset_y in range(7):
        found = spans(places, -1, offset_y, True)
        if not found:
            continue
        rows = slice(32 * found[0][1], 32 * found[-1][1] + 32)
        chunks, weights = [], []
        for offset_x in range(7):
            inner = 2 <= offset_x <= 4 and 2 <= offset_y <= 4
            for b in range(3):
                if inner and b == 1:
                    continue
                chunks.append(far_rows[offset_x, b, rows])
                weights.append(far_ref[offset_x, offset_y, 2 * b : 2 * b + 2].reshape(PAIR, PAIR))
        product = jnp.dot(
            jnp.concatenate(chunks, axis=1), jnp.concatenate(weights, axis=0), preferred_element_type=F32
        )
        for index, (target, _) in enumerate(found):
            far[target] += product[32 * index : 32 * index + 32]
    for offset_y in range(3):
        found = spans(places, 1, offset_y, False)
        if not found:
            continue
        rows = slice(32 * found[0][1], 32 * found[-1][1] + 32)
        chunks = [near_rows[offset_x, k, rows] for offset_x in range(3) for k in range(2)]
        weights = [near_ref[offset_x, offset_y].reshape(2 * PAIR, PAIR) for offset_x in range(3)]
        product = jnp.dot(
            jnp.concatenate(chunks, axis=1), jnp.concatenate(weights, axis=0), preferred_element_type=F32
        )
        for index, (target, _) in enumerate(found):
            near[target] += product[32 * index : 32 * index + 32]


def inner_kernel(own_ref, far_ref, near_ref, p2m_ref, far_out, near_out, far_rows, near_rows):
    column_windows(own_ref[...].astype(F32), p2m_ref, far_rows, near_rows)
    far = [jnp.zeros((32, PAIR), F32) for _ in range(4)]
    near = [jnp.zeros((32, PAIR), F32) for _ in range(4)]
    add_products(far, near, [2, 3, 4, 5], far_rows, near_rows, far_ref, near_ref)
    for y in range(4):
        far_out[32 * y : 32 * y + 32] = far[y]
        near_out[32 * y : 32 * y + 32] = near[y]


def outer_kernel(
    odd_ref, even_ref, far_part, near_part, far_ref, near_ref, p2m_ref, l2p_ref,
    out_ref, out_rows, far_rows, near_rows,
):
    pairs = out_ref.shape[2] // PAIR
    even, odd = even_ref[...].astype(F32), odd_ref[...].astype(F32)
    low, high = from_neighbours("gy", even, odd, even, odd)
    column_windows(jnp.concatenate([low, high], axis=0), p2m_ref, far_rows, near_rows)
    far = [far_part[32 * y : 32 * y + 32] for y in range(4)]
    near = [near_part[32 * y : 32 * y + 32] for y in range(4)]
    add_products(far, near, [0, 1, 6, 7], far_rows, near_rows, far_ref, near_ref)
    rounded = jnp.concatenate(far, axis=0).astype(BF16)
    total = jnp.concatenate(near, axis=0)
    out_rows[...] = total + jnp.dot(rounded, l2p_ref[...], preferred_element_type=F32)
    for x in range(4):
        for pair in range(pairs):
            out_ref[x, :, pair * PAIR : (pair + 1) * PAIR] = out_rows[
                pl.ds(x * pairs + pair, 4, stride=4 * pairs), :
            ]


def inner(own, far, near, p2m):
    return pl.pallas_call(
        inner_kernel,
        out_shape=[pltpu.VMEM((128, PAIR), F32)] * 2,
        in_specs=[pl.BlockSpec(memory_space=pltpu.VMEM)] * 4,
        out_specs=[pl.BlockSpec(memory_space=pltpu.VMEM)] * 2,
        scratch_shapes=[pltpu.VMEM((7, 3, 128, PAIR), BF16), pltpu.VMEM((3, 2, 128, PAIR), BF16)],
        compiler_params=pltpu.CompilerParams(vmem_limit_bytes=VMEM_LIMIT),
        cost_estimate=pl.CostEstimate(flops=400000000, bytes_accessed=6000000, transcendentals=0),
        name="inner",
    )(own, far, near, p2m)


def outer(shape, odd, even, far_part, near_part, far, near, p2m, l2p):
    return pl.pallas_call(
        outer_kernel,
        out_shape=jax.ShapeDtypeStruct(shape, F32),
        in_specs=[pl.BlockSpec(memory_space=pltpu.VMEM)] * 8,
        out_specs=pl.BlockSpec(memory_space=pltpu.VMEM),
        scratch_shapes=[
            pltpu.VMEM((128, PAIR), F32),
            pltpu.VMEM((7, 3, 128, PAIR), BF16),
            pltpu.VMEM((3, 2, 128, PAIR), BF16),
        ],
        compiler_params=pltpu.CompilerParams(vmem_limit_bytes=VMEM_LIMIT),
        cost_estimate=pl.CostEstimate(flops=400000000, bytes_accessed=6000000, transcendentals=0),
        name="outer",
    )(odd, even, far_part, near_part, far, near, p2m, l2p)


def local(density, p2m_operator, m2l_table, near_table, l2p_operator):
    odd, even = swapped(density, "gx", 1), swapped(density, "gx", 0)
    far, near, p2m, l2p = packed(first(), p2m_operator, m2l_table, near_table, l2p_operator)
    own, to_odd, to_even = joined(p2m, density, odd, even)
    odd, even = swapped(to_odd, "gy", 1), swapped(to_even, "gy", 0)
    parts = inner(own, far, near, p2m)
    return outer(density.shape, odd, even, *parts, far, near, p2m, l2p)


def solution(mesh):
    placed = (P("gx", "gy", None), P(), P(), P(), P())
    return jax.shard_map(
        local, mesh=mesh, in_specs=placed, out_specs=P("gx", "gy", None), check_vma=False
    )
```

```python
import jax
import jax.numpy as jnp
from jax import lax
from jax.experimental import pallas as pl
from jax.experimental.pallas import tpu as pltpu
from jax.sharding import PartitionSpec as P

BF16 = jnp.bfloat16
F32 = jnp.float32
WIDTH = 64
PAIR = 2 * WIDTH
VMEM_LIMIT = 40 * 1024 * 1024
SMALL_LIMIT = 8 * 1024 * 1024


AXES = ("gx", "gy")


def swapped(cells, axis, odd):
    sizes = [lax.axis_size(name) for name in AXES]
    dim = AXES.index(axis)
    pairs = []
    for place in range(sizes[0] * sizes[1]):
        at = list(divmod(place, sizes[1]))
        partner = (at[dim] - odd) ^ 1
        if at[dim] >= odd and partner + odd < sizes[dim]:
            at[dim] = partner + odd
        elif (at[1 - dim] ^ 1) < sizes[1 - dim]:
            at[1 - dim] ^= 1
        else:
            continue
        pairs.append((place, at[0] * sizes[1] + at[1]))
    return lax.ppermute(cells, AXES, pairs)


def square(block):
    rows, columns = block.shape
    if columns < WIDTH:
        block = jnp.concatenate([block, jnp.zeros((rows, WIDTH - columns), BF16)], axis=1)
    if rows < WIDTH:
        block = jnp.concatenate([block, jnp.zeros((WIDTH - rows, WIDTH), BF16)], axis=0)
    return block


def first_kernel(out_ref):
    out_ref[...] = jnp.zeros_like(out_ref)


def first():
    return pl.pallas_call(
        first_kernel,
        out_shape=pltpu.VMEM((8, PAIR), F32),
        out_specs=pl.BlockSpec(memory_space=pltpu.VMEM),
        compiler_params=pltpu.CompilerParams(vmem_limit_bytes=1024 * 1024),
        cost_estimate=pl.CostEstimate(flops=10000000000, bytes_accessed=1000, transcendentals=0),
        name="first",
    )()


def pack_kernel(first_ref, p2m_ref, m2l_ref, near_ref, l2p_ref, far_out, near_out, p2m_out, l2p_out):
    blank = jnp.zeros((WIDTH, WIDTH), BF16)

    def far_blocks(offset_x, offset_y):
        inner = 2 <= offset_x <= 4 and 2 <= offset_y <= 4
        entries = []
        for offset_z in range(7):
            if inner and 2 <= offset_z <= 4:
                entries.append(blank)
            else:
                entries.append(square(m2l_ref[offset_x, offset_y, offset_z]))
        for s in range(6):
            far_out[offset_x, offset_y, s] = jnp.concatenate([entries[s + 1], entries[s]], axis=1)

    for offset_x in range(7):
        for offset_y in range(7):
            far_blocks(offset_x, offset_y)
    for offset_x in range(3):
        for offset_y in range(3):
            before, same, after = [near_ref[offset_x, offset_y, z] for z in range(3)]
            upper = jnp.concatenate([same, before], axis=1)
            lower = jnp.concatenate([after, same], axis=1)
            near_out[offset_x, offset_y, 0] = jnp.concatenate([upper, lower], axis=0)
            upper = jnp.concatenate([blank, after], axis=1)
            lower = jnp.concatenate([before, blank], axis=1)
            near_out[offset_x, offset_y, 1] = jnp.concatenate([upper, lower], axis=0)
    p2m = square(p2m_ref[...])
    p2m_out[...] = jnp.concatenate(
        [jnp.concatenate([p2m, blank], axis=1), jnp.concatenate([blank, p2m], axis=1)], axis=0
    )
    l2p = square(l2p_ref[...])
    l2p_out[...] = jnp.concatenate(
        [jnp.concatenate([l2p, blank], axis=1), jnp.concatenate([blank, l2p], axis=1)], axis=0
    )


def packed(start, p2m_operator, m2l_table, near_table, l2p_operator):
    shapes = [(7, 7, 6, WIDTH, PAIR), (3, 3, 2, PAIR, PAIR), (PAIR, PAIR), (PAIR, PAIR)]
    return pl.pallas_call(
        pack_kernel,
        out_shape=[pltpu.VMEM(shape, BF16) for shape in shapes],
        in_specs=[pl.BlockSpec(memory_space=pltpu.VMEM)] * 5,
        out_specs=[pl.BlockSpec(memory_space=pltpu.VMEM)] * 4,
        compiler_params=pltpu.CompilerParams(vmem_limit_bytes=VMEM_LIMIT),
        cost_estimate=pl.CostEstimate(flops=4000000, bytes_accessed=10000000, transcendentals=0),
        name="pack",
    )(start, p2m_operator.T, m2l_table, near_table, l2p_operator)


def from_neighbours(axis, even_low, odd_low, even_high, odd_high):
    place = lax.axis_index(axis)
    lower = lax.rem(place, 2) == 0
    low = jnp.where(place == 0, 0.0, jnp.where(lower, odd_low, even_low))
    last = place == lax.axis_size(axis) - 1
    high = jnp.where(last, 0.0, jnp.where(lower, even_high, odd_high))
    return low, high


def join_kernel(after_ref, own_ref, odd_ref, even_ref, own_out, odd_out, even_out, rows_ref):
    pairs = own_ref.shape[2] // PAIR
    for pair in range(pairs):
        lanes = slice(pair * PAIR, (pair + 1) * PAIR)

        def part(ref, x):
            return ref[x, :, lanes].astype(F32)

        for x in range(8):
            if 2 <= x < 6:
                cells = part(own_ref, x - 2)
            else:
                low, high = from_neighbours(
                    "gx",
                    *((part(even_ref, 2 + x), part(odd_ref, 2 + x)) if x < 2 else (0.0, 0.0)),
                    *((part(even_ref, x - 6), part(odd_ref, x - 6)) if x > 5 else (0.0, 0.0)),
                )
                cells = low if x < 2 else high
            rows_ref[pl.ds(x * pairs + pair, 4, stride=8 * pairs), :] = cells
    rows = rows_ref[...]
    own_out[...] = rows.astype(BF16)
    lower = lax.rem(lax.axis_index("gy"), 2) == 0
    head, tail = rows[:128], rows[128:]
    even_out[...] = jnp.where(lower, tail, head).astype(BF16)
    odd_out[...] = jnp.where(lower, head, tail).astype(BF16)


def joined(after, own, odd, even):
    return pl.pallas_call(
        join_kernel,
        out_shape=[pltpu.VMEM((rows, PAIR), BF16) for rows in (256, 128, 128)],
        in_specs=[pl.BlockSpec(memory_space=pltpu.VMEM)] * 4,
        out_specs=[pl.BlockSpec(memory_space=pltpu.VMEM)] * 3,
        scratch_shapes=[pltpu.VMEM((256, PAIR), F32)],
        compiler_params=pltpu.CompilerParams(vmem_limit_bytes=SMALL_LIMIT),
        cost_estimate=pl.CostEstimate(flops=1000000, bytes_accessed=100000, transcendentals=0),
        name="join",
    )(after, own, odd, even)


def shifted(rows):
    place = lax.broadcasted_iota(jnp.int32, rows.shape, 0) % 8
    before = jnp.where(place == 0, 0.0, jnp.roll(rows, 1, axis=0))
    after = jnp.where(place == 7, 0.0, jnp.roll(rows, -1, axis=0))
    return before, rows, after


def column_windows(cells, p2m_ref, far_rows, near_rows):
    multipole = lax.dot_general(
        cells.astype(BF16), p2m_ref[...], (((1,), (1,)), ((), ())), preferred_element_type=F32
    )
    sources = shifted(multipole.astype(BF16).astype(F32))
    blank = jnp.zeros((8, PAIR), F32)
    count = cells.shape[0] // 64
    for b in range(3):
        for y in range(count):
            slab = sources[b][64 * y : 64 * y + 64]
            for offset_x in range(7):
                if offset_x == 0:
                    window = jnp.concatenate([blank, slab[0:8], blank, slab[16:24]], axis=0)
                elif offset_x == 6:
                    window = jnp.concatenate([slab[40:48], blank, slab[56:64], blank], axis=0)
                else:
                    window = slab[8 * (offset_x - 1) : 8 * (offset_x + 3)]
                far_rows[offset_x, b, 32 * y : 32 * y + 32] = window.astype(BF16)
    before, same, after = shifted(cells)
    lane = lax.broadcasted_iota(jnp.int32, cells.shape, 1)
    beside = jnp.where(lane < WIDTH, after, before)
    for k, kind in enumerate((same, beside)):
        for y in range(count):
            for offset_x in range(3):
                near_rows[offset_x, k, 32 * y : 32 * y + 32] = kind[
                    64 * y + 8 * (offset_x + 1) : 64 * y + 8 * (offset_x + 5)
                ].astype(BF16)


def spans(places, first, offset, parity):
    found = [
        (target, places.index(target + offset + first))
        for target in range(4)
        if target + offset + first in places
        and not (parity and ((offset == 0 and target % 2 == 0) or (offset == 6 and target % 2 == 1)))
    ]
    return found


def add_products(far, near, places, far_rows, near_rows, far_ref, near_ref):
    for offset_y in range(7):
        found = spans(places, -1, offset_y, True)
        if not found:
            continue
        rows = slice(32 * found[0][1], 32 * found[-1][1] + 32)
        chunks, weights = [], []
        for offset_x in range(7):
            inner = 2 <= offset_x <= 4 and 2 <= offset_y <= 4
            for b in range(3):
                if inner and b == 1:
                    continue
                chunks.append(far_rows[offset_x, b, rows])
                weights.append(far_ref[offset_x, offset_y, 2 * b : 2 * b + 2].reshape(PAIR, PAIR))
        product = jnp.dot(
            jnp.concatenate(chunks, axis=1), jnp.concatenate(weights, axis=0), preferred_element_type=F32
        )
        for index, (target, _) in enumerate(found):
            far[32 * target : 32 * target + 32] += product[32 * index : 32 * index + 32]
    for offset_y in range(3):
        found = spans(places, 1, offset_y, False)
        if not found:
            continue
        rows = slice(32 * found[0][1], 32 * found[-1][1] + 32)
        chunks = [near_rows[offset_x, k, rows] for offset_x in range(3) for k in range(2)]
        weights = [near_ref[offset_x, offset_y].reshape(2 * PAIR, PAIR) for offset_x in range(3)]
        product = jnp.dot(
            jnp.concatenate(chunks, axis=1), jnp.concatenate(weights, axis=0), preferred_element_type=F32
        )
        for index, (target, _) in enumerate(found):
            near[32 * target : 32 * target + 32] += product[32 * index : 32 * index + 32]


def inner_kernel(own_ref, far_ref, near_ref, p2m_ref, far_out, near_out, far_rows, near_rows):
    column_windows(own_ref[...].astype(F32), p2m_ref, far_rows, near_rows)
    far_out[...] = jnp.zeros_like(far_out)
    near_out[...] = jnp.zeros_like(near_out)
    add_products(far_out, near_out, [2, 3, 4, 5], far_rows, near_rows, far_ref, near_ref)


def add_halo(cells_ref, odd, far, near, far_ref, near_ref, p2m_ref, far_rows, near_rows):
    place = lax.axis_index("gy")
    before = lax.rem(place, 2) == (0 if odd else 1)
    outside = place == jnp.where(before, 0, lax.axis_size("gy") - 1)
    cells = jnp.where(outside, 0.0, cells_ref[...].astype(F32))
    column_windows(cells, p2m_ref, far_rows, near_rows)

    @pl.when(before)
    def _():
        add_products(far, near, [0, 1], far_rows, near_rows, far_ref, near_ref)

    @pl.when(jnp.logical_not(before))
    def _():
        add_products(far, near, [6, 7], far_rows, near_rows, far_ref, near_ref)


def outer_kernel(
    cells_ref, far_part, near_part, far_ref, near_ref, p2m_ref, far_out, near_out, far_rows, near_rows
):
    far_out[...] = far_part[...]
    near_out[...] = near_part[...]
    add_halo(cells_ref, False, far_out, near_out, far_ref, near_ref, p2m_ref, far_rows, near_rows)


def last_kernel(
    far_part, near_part, cells_ref, far_ref, near_ref, p2m_ref, l2p_ref,
    out_ref, far, near, far_rows, near_rows,
):
    pairs = out_ref.shape[2] // PAIR
    far[...] = far_part[...]
    near[...] = near_part[...]
    add_halo(cells_ref, True, far, near, far_ref, near_ref, p2m_ref, far_rows, near_rows)
    near[...] += jnp.dot(far[...].astype(BF16), l2p_ref[...], preferred_element_type=F32)
    for x in range(4):
        for pair in range(pairs):
            out_ref[x, :, pair * PAIR : (pair + 1) * PAIR] = near[
                pl.ds(x * pairs + pair, 4, stride=4 * pairs), :
            ]


def inner(own, far, near, p2m):
    return pl.pallas_call(
        inner_kernel,
        out_shape=[pltpu.VMEM((128, PAIR), F32)] * 2,
        in_specs=[pl.BlockSpec(memory_space=pltpu.VMEM)] * 4,
        out_specs=[pl.BlockSpec(memory_space=pltpu.VMEM)] * 2,
        scratch_shapes=[pltpu.VMEM((7, 3, 128, PAIR), BF16), pltpu.VMEM((3, 2, 128, PAIR), BF16)],
        compiler_params=pltpu.CompilerParams(vmem_limit_bytes=VMEM_LIMIT),
        cost_estimate=pl.CostEstimate(flops=400000000, bytes_accessed=6000000, transcendentals=0),
        name="inner",
    )(own, far, near, p2m)


def outer(cells, far_part, near_part, far, near, p2m):
    return pl.pallas_call(
        outer_kernel,
        out_shape=[pltpu.VMEM((128, PAIR), F32)] * 2,
        in_specs=[pl.BlockSpec(memory_space=pltpu.VMEM)] * 6,
        out_specs=[pl.BlockSpec(memory_space=pltpu.VMEM)] * 2,
        scratch_shapes=[pltpu.VMEM((7, 3, 64, PAIR), BF16), pltpu.VMEM((3, 2, 64, PAIR), BF16)],
        compiler_params=pltpu.CompilerParams(vmem_limit_bytes=VMEM_LIMIT),
        cost_estimate=pl.CostEstimate(flops=200000000, bytes_accessed=3000000, transcendentals=0),
        name="outer",
    )(cells, far_part, near_part, far, near, p2m)


def last(shape, cells, far_part, near_part, far, near, p2m, l2p):
    return pl.pallas_call(
        last_kernel,
        out_shape=jax.ShapeDtypeStruct(shape, F32),
        in_specs=[pl.BlockSpec(memory_space=pltpu.VMEM)] * 7,
        out_specs=pl.BlockSpec(memory_space=pltpu.VMEM),
        scratch_shapes=[
            pltpu.VMEM((128, PAIR), F32),
            pltpu.VMEM((128, PAIR), F32),
            pltpu.VMEM((7, 3, 64, PAIR), BF16),
            pltpu.VMEM((3, 2, 64, PAIR), BF16),
        ],
        compiler_params=pltpu.CompilerParams(vmem_limit_bytes=VMEM_LIMIT),
        cost_estimate=pl.CostEstimate(flops=200000000, bytes_accessed=3000000, transcendentals=0),
        name="last",
    )(far_part, near_part, cells, far, near, p2m, l2p)


def local(density, p2m_operator, m2l_table, near_table, l2p_operator):
    odd, even = swapped(density, "gx", 1), swapped(density, "gx", 0)
    far, near, p2m, l2p = packed(first(), p2m_operator, m2l_table, near_table, l2p_operator)
    own, to_odd, to_even = joined(p2m, density, odd, even)
    odd, even = swapped(to_odd, "gy", 1), swapped(to_even, "gy", 0)
    parts = inner(own, far, near, p2m)
    parts = outer(even, *parts, far, near, p2m)
    return last(density.shape, odd, *parts, far, near, p2m, l2p)


def solution(mesh):
    placed = (P("gx", "gy", None), P(), P(), P(), P())
    return jax.shard_map(
        local, mesh=mesh, in_specs=placed, out_specs=P("gx", "gy", None), check_vma=False
    )
```

```python
import functools

import jax
import jax.numpy as jnp
from jax import lax
from jax.experimental import pallas as pl
from jax.experimental.pallas import tpu as pltpu
from jax.sharding import PartitionSpec as P

BF16 = jnp.bfloat16
F32 = jnp.float32
WIDTH = 64
PAIR = 2 * WIDTH
VMEM_LIMIT = 40 * 1024 * 1024
SMALL_LIMIT = 8 * 1024 * 1024


AXES = ("gx", "gy")


def swapped(cells, axis, first, step):
    sizes = [lax.axis_size(name) for name in AXES]
    dim = AXES.index(axis)
    pairs = []
    for place in range(sizes[0] * sizes[1]):
        at = list(divmod(place, sizes[1]))
        if at[dim] % step == first and at[dim] + 1 < sizes[dim]:
            at[dim] += 1
        elif at[dim] > 0 and (at[dim] - 1) % step == first:
            at[dim] -= 1
        elif (at[1 - dim] ^ 1) < sizes[1 - dim]:
            at[1 - dim] ^= 1
        else:
            continue
        pairs.append((place, at[0] * sizes[1] + at[1]))
    return lax.ppermute(cells, AXES, pairs)


def square(block):
    rows, columns = block.shape
    if columns < WIDTH:
        block = jnp.concatenate([block, jnp.zeros((rows, WIDTH - columns), BF16)], axis=1)
    if rows < WIDTH:
        block = jnp.concatenate([block, jnp.zeros((WIDTH - rows, WIDTH), BF16)], axis=0)
    return block


def first_kernel(out_ref):
    out_ref[...] = jnp.zeros_like(out_ref)


def first():
    return pl.pallas_call(
        first_kernel,
        out_shape=pltpu.VMEM((8, PAIR), F32),
        out_specs=pl.BlockSpec(memory_space=pltpu.VMEM),
        compiler_params=pltpu.CompilerParams(vmem_limit_bytes=1024 * 1024),
        cost_estimate=pl.CostEstimate(flops=10000000000, bytes_accessed=1000, transcendentals=0),
        name="first",
    )()


def pack_kernel(first_ref, p2m_ref, m2l_ref, near_ref, l2p_ref, far_out, near_out, p2m_out, l2p_out):
    blank = jnp.zeros((WIDTH, WIDTH), BF16)

    def far_blocks(offset_x, offset_y):
        inner = 2 <= offset_x <= 4 and 2 <= offset_y <= 4
        entries = []
        for offset_z in range(7):
            if inner and 2 <= offset_z <= 4:
                entries.append(blank)
            else:
                entries.append(square(m2l_ref[offset_x, offset_y, offset_z]))
        for s in range(6):
            far_out[offset_x, offset_y, s] = jnp.concatenate([entries[s + 1], entries[s]], axis=1)

    for offset_x in range(7):
        for offset_y in range(7):
            far_blocks(offset_x, offset_y)
    for offset_x in range(3):
        for offset_y in range(3):
            before, same, after = [near_ref[offset_x, offset_y, z] for z in range(3)]
            upper = jnp.concatenate([same, before], axis=1)
            lower = jnp.concatenate([after, same], axis=1)
            near_out[offset_x, offset_y, 0] = jnp.concatenate([upper, lower], axis=0)
            upper = jnp.concatenate([blank, after], axis=1)
            lower = jnp.concatenate([before, blank], axis=1)
            near_out[offset_x, offset_y, 1] = jnp.concatenate([upper, lower], axis=0)
    p2m = square(p2m_ref[...])
    p2m_out[...] = jnp.concatenate(
        [jnp.concatenate([p2m, blank], axis=1), jnp.concatenate([blank, p2m], axis=1)], axis=0
    )
    l2p = square(l2p_ref[...])
    l2p_out[...] = jnp.concatenate(
        [jnp.concatenate([l2p, blank], axis=1), jnp.concatenate([blank, l2p], axis=1)], axis=0
    )


def packed(start, p2m_operator, m2l_table, near_table, l2p_operator):
    shapes = [(7, 7, 6, WIDTH, PAIR), (3, 3, 2, PAIR, PAIR), (PAIR, PAIR), (PAIR, PAIR)]
    return pl.pallas_call(
        pack_kernel,
        out_shape=[pltpu.VMEM(shape, BF16) for shape in shapes],
        in_specs=[pl.BlockSpec(memory_space=pltpu.VMEM)] * 5,
        out_specs=[pl.BlockSpec(memory_space=pltpu.VMEM)] * 4,
        compiler_params=pltpu.CompilerParams(vmem_limit_bytes=VMEM_LIMIT),
        cost_estimate=pl.CostEstimate(flops=4000000, bytes_accessed=10000000, transcendentals=0),
        name="pack",
    )(start, p2m_operator.T, m2l_table, near_table, l2p_operator)


def from_neighbours(axis, even_low, odd_low, even_high, odd_high):
    place = lax.axis_index(axis)
    lower = lax.rem(place, 2) == 0
    low = jnp.where(place == 0, 0.0, jnp.where(lower, odd_low, even_low))
    last = place == lax.axis_size(axis) - 1
    high = jnp.where(last, 0.0, jnp.where(lower, even_high, odd_high))
    return low, high


def join_kernel(after_ref, own_ref, odd_ref, even_ref, own_out, odd_out, even_out, again_out, rows_ref):
    pairs = own_ref.shape[2] // PAIR
    for pair in range(pairs):
        lanes = slice(pair * PAIR, (pair + 1) * PAIR)

        def part(ref, x):
            return ref[x, :, lanes].astype(F32)

        for x in range(8):
            if 2 <= x < 6:
                cells = part(own_ref, x - 2)
            else:
                low, high = from_neighbours(
                    "gx",
                    *((part(even_ref, 2 + x), part(odd_ref, 2 + x)) if x < 2 else (0.0, 0.0)),
                    *((part(even_ref, x - 6), part(odd_ref, x - 6)) if x > 5 else (0.0, 0.0)),
                )
                cells = low if x < 2 else high
            rows_ref[pl.ds(x * pairs + pair, 4, stride=8 * pairs), :] = cells
    rows = rows_ref[...]
    own_out[...] = rows.astype(BF16)
    lower = lax.rem(lax.axis_index("gy"), 2) == 0
    head, tail = rows[:128], rows[128:]
    even_out[...] = jnp.where(lower, tail, head).astype(BF16)
    odd_out[...] = jnp.where(lower, head, tail).astype(BF16)
    again_out[...] = jnp.where(lower, tail, head).astype(BF16)


def joined(after, own, odd, even):
    return pl.pallas_call(
        join_kernel,
        out_shape=[pltpu.VMEM((rows, PAIR), BF16) for rows in (256, 128, 128, 128)],
        in_specs=[pl.BlockSpec(memory_space=pltpu.VMEM)] * 4,
        out_specs=[pl.BlockSpec(memory_space=pltpu.VMEM)] * 4,
        scratch_shapes=[pltpu.VMEM((256, PAIR), F32)],
        compiler_params=pltpu.CompilerParams(vmem_limit_bytes=SMALL_LIMIT),
        cost_estimate=pl.CostEstimate(flops=1000000, bytes_accessed=100000, transcendentals=0),
        name="join",
    )(after, own, odd, even)


def shifted(rows):
    place = lax.broadcasted_iota(jnp.int32, rows.shape, 0) % 8
    before = jnp.where(place == 0, 0.0, jnp.roll(rows, 1, axis=0))
    after = jnp.where(place == 7, 0.0, jnp.roll(rows, -1, axis=0))
    return before, rows, after


def column_windows(cells, p2m_ref, far_rows, near_rows):
    multipole = lax.dot_general(
        cells.astype(BF16), p2m_ref[...], (((1,), (1,)), ((), ())), preferred_element_type=F32
    )
    sources = shifted(multipole.astype(BF16).astype(F32))
    blank = jnp.zeros((8, PAIR), F32)
    count = cells.shape[0] // 64
    for b in range(3):
        for y in range(count):
            slab = sources[b][64 * y : 64 * y + 64]
            for offset_x in range(7):
                if offset_x == 0:
                    window = jnp.concatenate([blank, slab[0:8], blank, slab[16:24]], axis=0)
                elif offset_x == 6:
                    window = jnp.concatenate([slab[40:48], blank, slab[56:64], blank], axis=0)
                else:
                    window = slab[8 * (offset_x - 1) : 8 * (offset_x + 3)]
                far_rows[offset_x, b, 32 * y : 32 * y + 32] = window.astype(BF16)
    before, same, after = shifted(cells)
    lane = lax.broadcasted_iota(jnp.int32, cells.shape, 1)
    beside = jnp.where(lane < WIDTH, after, before)
    for k, kind in enumerate((same, beside)):
        for y in range(count):
            for offset_x in range(3):
                near_rows[offset_x, k, 32 * y : 32 * y + 32] = kind[
                    64 * y + 8 * (offset_x + 1) : 64 * y + 8 * (offset_x + 5)
                ].astype(BF16)


def spans(places, first, offset, parity):
    found = [
        (target, places.index(target + offset + first))
        for target in range(4)
        if target + offset + first in places
        and not (parity and ((offset == 0 and target % 2 == 0) or (offset == 6 and target % 2 == 1)))
    ]
    return found


def add_products(far, near, places, far_rows, near_rows, far_ref, near_ref):
    for offset_y in range(7):
        found = spans(places, -1, offset_y, True)
        if not found:
            continue
        rows = slice(32 * found[0][1], 32 * found[-1][1] + 32)
        chunks, weights = [], []
        for offset_x in range(7):
            inner = 2 <= offset_x <= 4 and 2 <= offset_y <= 4
            for b in range(3):
                if inner and b == 1:
                    continue
                chunks.append(far_rows[offset_x, b, rows])
                weights.append(far_ref[offset_x, offset_y, 2 * b : 2 * b + 2].reshape(PAIR, PAIR))
        product = jnp.dot(
            jnp.concatenate(chunks, axis=1), jnp.concatenate(weights, axis=0), preferred_element_type=F32
        )
        for index, (target, _) in enumerate(found):
            far[32 * target : 32 * target + 32] += product[32 * index : 32 * index + 32]
    for offset_y in range(3):
        found = spans(places, 1, offset_y, False)
        if not found:
            continue
        rows = slice(32 * found[0][1], 32 * found[-1][1] + 32)
        chunks = [near_rows[offset_x, k, rows] for offset_x in range(3) for k in range(2)]
        weights = [near_ref[offset_x, offset_y].reshape(2 * PAIR, PAIR) for offset_x in range(3)]
        product = jnp.dot(
            jnp.concatenate(chunks, axis=1), jnp.concatenate(weights, axis=0), preferred_element_type=F32
        )
        for index, (target, _) in enumerate(found):
            near[32 * target : 32 * target + 32] += product[32 * index : 32 * index + 32]


def inner_kernel(own_ref, far_ref, near_ref, p2m_ref, far_out, near_out, far_rows, near_rows):
    column_windows(own_ref[...].astype(F32), p2m_ref, far_rows, near_rows)
    far_out[...] = jnp.zeros_like(far_out)
    near_out[...] = jnp.zeros_like(near_out)
    add_products(far_out, near_out, [2, 3, 4, 5], far_rows, near_rows, far_ref, near_ref)


def add_halo(cells_ref, trade, far, near, far_ref, near_ref, p2m_ref, far_rows, near_rows):
    place = lax.axis_index("gy")
    first, step = trade
    after = jnp.logical_and(lax.rem(place, step) == first, place + 1 < lax.axis_size("gy"))
    before = jnp.logical_and(lax.rem(place + step - 1, step) == first, place > 0)

    @pl.when(jnp.logical_or(before, after))
    def _():
        column_windows(cells_ref[...].astype(F32), p2m_ref, far_rows, near_rows)

    @pl.when(before)
    def _():
        add_products(far, near, [0, 1], far_rows, near_rows, far_ref, near_ref)

    @pl.when(after)
    def _():
        add_products(far, near, [6, 7], far_rows, near_rows, far_ref, near_ref)


def outer_kernel(
    trade, far_part, near_part, cells_ref, far_ref, near_ref, p2m_ref, far_out, near_out, far_rows, near_rows
):
    far_out[...] = far_part[...]
    near_out[...] = near_part[...]
    add_halo(cells_ref, trade, far_out, near_out, far_ref, near_ref, p2m_ref, far_rows, near_rows)


def last_kernel(
    trade, far_part, near_part, cells_ref, far_ref, near_ref, p2m_ref, l2p_ref,
    out_ref, far, near, far_rows, near_rows,
):
    pairs = out_ref.shape[2] // PAIR
    far[...] = far_part[...]
    near[...] = near_part[...]
    add_halo(cells_ref, trade, far, near, far_ref, near_ref, p2m_ref, far_rows, near_rows)
    near[...] += jnp.dot(far[...].astype(BF16), l2p_ref[...], preferred_element_type=F32)
    for x in range(4):
        for pair in range(pairs):
            out_ref[x, :, pair * PAIR : (pair + 1) * PAIR] = near[
                pl.ds(x * pairs + pair, 4, stride=4 * pairs), :
            ]


def inner(own, far, near, p2m):
    return pl.pallas_call(
        inner_kernel,
        out_shape=[pltpu.VMEM((128, PAIR), F32)] * 2,
        in_specs=[pl.BlockSpec(memory_space=pltpu.VMEM)] * 4,
        out_specs=[pl.BlockSpec(memory_space=pltpu.VMEM)] * 2,
        scratch_shapes=[pltpu.VMEM((7, 3, 128, PAIR), BF16), pltpu.VMEM((3, 2, 128, PAIR), BF16)],
        compiler_params=pltpu.CompilerParams(vmem_limit_bytes=VMEM_LIMIT),
        cost_estimate=pl.CostEstimate(flops=400000000, bytes_accessed=6000000, transcendentals=0),
        name="inner",
    )(own, far, near, p2m)


def outer(trade, far_part, near_part, cells, far, near, p2m):
    return pl.pallas_call(
        functools.partial(outer_kernel, trade),
        out_shape=[pltpu.VMEM((128, PAIR), F32)] * 2,
        in_specs=[pl.BlockSpec(memory_space=pltpu.VMEM)] * 6,
        out_specs=[pl.BlockSpec(memory_space=pltpu.VMEM)] * 2,
        scratch_shapes=[pltpu.VMEM((7, 3, 64, PAIR), BF16), pltpu.VMEM((3, 2, 64, PAIR), BF16)],
        compiler_params=pltpu.CompilerParams(vmem_limit_bytes=VMEM_LIMIT),
        cost_estimate=pl.CostEstimate(flops=200000000, bytes_accessed=3000000, transcendentals=0),
        name="outer",
    )(far_part, near_part, cells, far, near, p2m)


def last(trade, shape, far_part, near_part, cells, far, near, p2m, l2p):
    return pl.pallas_call(
        functools.partial(last_kernel, trade),
        out_shape=jax.ShapeDtypeStruct(shape, F32),
        in_specs=[pl.BlockSpec(memory_space=pltpu.VMEM)] * 7,
        out_specs=pl.BlockSpec(memory_space=pltpu.VMEM),
        scratch_shapes=[
            pltpu.VMEM((128, PAIR), F32),
            pltpu.VMEM((128, PAIR), F32),
            pltpu.VMEM((7, 3, 64, PAIR), BF16),
            pltpu.VMEM((3, 2, 64, PAIR), BF16),
        ],
        compiler_params=pltpu.CompilerParams(vmem_limit_bytes=VMEM_LIMIT),
        cost_estimate=pl.CostEstimate(flops=200000000, bytes_accessed=3000000, transcendentals=0),
        name="last",
    )(far_part, near_part, cells, far, near, p2m, l2p)


def local(density, p2m_operator, m2l_table, near_table, l2p_operator):
    odd, even = swapped(density, "gx", 1, 2), swapped(density, "gx", 0, 2)
    far, near, p2m, l2p = packed(first(), p2m_operator, m2l_table, near_table, l2p_operator)
    own, to_odd, *to_even = joined(p2m, density, odd, even)
    trades = ((0, 4), (1, 2), (2, 4))
    halos = [swapped(part, "gy", *trade) for part, trade in zip((to_even[0], to_odd, to_even[1]), trades)]
    parts = inner(own, far, near, p2m)
    for trade, halo in zip(trades[:-1], halos):
        parts = outer(trade, *parts, halo, far, near, p2m)
    return last(trades[-1], density.shape, *parts, halos[-1], far, near, p2m, l2p)


def solution(mesh):
    placed = (P("gx", "gy", None), P(), P(), P(), P())
    return jax.shard_map(
        local, mesh=mesh, in_specs=placed, out_specs=P("gx", "gy", None), check_vma=False
    )
```

```python
import functools

import jax
import jax.numpy as jnp
from jax import lax
from jax.experimental import pallas as pl
from jax.experimental.pallas import tpu as pltpu
from jax.sharding import PartitionSpec as P

BF16 = jnp.bfloat16
F32 = jnp.float32
WIDTH = 64
PAIR = 2 * WIDTH
VMEM_LIMIT = 40 * 1024 * 1024
SMALL_LIMIT = 8 * 1024 * 1024


AXES = ("gx", "gy")


def swapped(cells, axis, first, step):
    sizes = [lax.axis_size(name) for name in AXES]
    dim = AXES.index(axis)
    pairs = []
    for place in range(sizes[0] * sizes[1]):
        at = list(divmod(place, sizes[1]))
        if at[dim] % step == first and at[dim] + 1 < sizes[dim]:
            at[dim] += 1
        elif at[dim] > 0 and (at[dim] - 1) % step == first:
            at[dim] -= 1
        elif (at[1 - dim] ^ 1) < sizes[1 - dim]:
            at[1 - dim] ^= 1
        else:
            continue
        pairs.append((place, at[0] * sizes[1] + at[1]))
    return lax.ppermute(cells, AXES, pairs)


def square(block):
    rows, columns = block.shape
    if columns < WIDTH:
        block = jnp.concatenate([block, jnp.zeros((rows, WIDTH - columns), BF16)], axis=1)
    if rows < WIDTH:
        block = jnp.concatenate([block, jnp.zeros((WIDTH - rows, WIDTH), BF16)], axis=0)
    return block


def first_kernel(out_ref):
    out_ref[...] = jnp.zeros_like(out_ref)


def first():
    return pl.pallas_call(
        first_kernel,
        out_shape=pltpu.VMEM((8, PAIR), F32),
        out_specs=pl.BlockSpec(memory_space=pltpu.VMEM),
        compiler_params=pltpu.CompilerParams(vmem_limit_bytes=1024 * 1024),
        cost_estimate=pl.CostEstimate(flops=10000000000, bytes_accessed=1000, transcendentals=0),
        name="first",
    )()


def far_blocks(m2l_ref, offset_x, offset_y):
    inner = 2 <= offset_x <= 4 and 2 <= offset_y <= 4
    blank = jnp.zeros((WIDTH, WIDTH), BF16)
    entries = [
        blank if inner and 2 <= offset_z <= 4 else square(m2l_ref[offset_x, offset_y, offset_z])
        for offset_z in range(7)
    ]
    blocks = [jnp.concatenate([entries[s + 1], entries[s]], axis=1) for s in range(6)]
    return [
        None if inner and b == 1 else jnp.concatenate(blocks[2 * b : 2 * b + 2], axis=0) for b in range(3)
    ]


def pack_kernel(first_ref, p2m_ref, near_ref, l2p_ref, near_out, p2m_out, l2p_out):
    blank = jnp.zeros((WIDTH, WIDTH), BF16)
    for offset_x in range(3):
        for offset_y in range(3):
            before, same, after = [near_ref[offset_x, offset_y, z] for z in range(3)]
            upper = jnp.concatenate([same, before], axis=1)
            lower = jnp.concatenate([after, same], axis=1)
            near_out[offset_x, offset_y, 0] = jnp.concatenate([upper, lower], axis=0)
            upper = jnp.concatenate([blank, after], axis=1)
            lower = jnp.concatenate([before, blank], axis=1)
            near_out[offset_x, offset_y, 1] = jnp.concatenate([upper, lower], axis=0)
    p2m = square(p2m_ref[...])
    p2m_out[...] = jnp.concatenate(
        [jnp.concatenate([p2m, blank], axis=1), jnp.concatenate([blank, p2m], axis=1)], axis=0
    )
    l2p = square(l2p_ref[...])
    l2p_out[...] = jnp.concatenate(
        [jnp.concatenate([l2p, blank], axis=1), jnp.concatenate([blank, l2p], axis=1)], axis=0
    )


def packed(start, p2m_operator, near_table, l2p_operator):
    shapes = [(3, 3, 2, PAIR, PAIR), (PAIR, PAIR), (PAIR, PAIR)]
    return pl.pallas_call(
        pack_kernel,
        out_shape=[pltpu.VMEM(shape, BF16) for shape in shapes],
        in_specs=[pl.BlockSpec(memory_space=pltpu.VMEM)] * 4,
        out_specs=[pl.BlockSpec(memory_space=pltpu.VMEM)] * 3,
        compiler_params=pltpu.CompilerParams(vmem_limit_bytes=SMALL_LIMIT),
        cost_estimate=pl.CostEstimate(flops=4000000, bytes_accessed=10000000, transcendentals=0),
        name="pack",
    )(start, p2m_operator.T, near_table, l2p_operator)


def from_neighbours(axis, even_low, odd_low, even_high, odd_high):
    place = lax.axis_index(axis)
    lower = lax.rem(place, 2) == 0
    low = jnp.where(place == 0, 0.0, jnp.where(lower, odd_low, even_low))
    last = place == lax.axis_size(axis) - 1
    high = jnp.where(last, 0.0, jnp.where(lower, even_high, odd_high))
    return low, high


def join_kernel(after_ref, own_ref, odd_ref, even_ref, own_out, odd_out, even_out, again_out, rows_ref):
    pairs = own_ref.shape[2] // PAIR
    for pair in range(pairs):
        lanes = slice(pair * PAIR, (pair + 1) * PAIR)

        def part(ref, x):
            return ref[x, :, lanes].astype(F32)

        for x in range(8):
            if 2 <= x < 6:
                cells = part(own_ref, x - 2)
            else:
                low, high = from_neighbours(
                    "gx",
                    *((part(even_ref, 2 + x), part(odd_ref, 2 + x)) if x < 2 else (0.0, 0.0)),
                    *((part(even_ref, x - 6), part(odd_ref, x - 6)) if x > 5 else (0.0, 0.0)),
                )
                cells = low if x < 2 else high
            rows_ref[pl.ds(x * pairs + pair, 4, stride=8 * pairs), :] = cells
    rows = rows_ref[...]
    own_out[...] = rows.astype(BF16)
    lower = lax.rem(lax.axis_index("gy"), 2) == 0
    head, tail = rows[:128], rows[128:]
    even_out[...] = jnp.where(lower, tail, head).astype(BF16)
    odd_out[...] = jnp.where(lower, head, tail).astype(BF16)
    again_out[...] = jnp.where(lower, tail, head).astype(BF16)


def joined(after, own, odd, even):
    return pl.pallas_call(
        join_kernel,
        out_shape=[pltpu.VMEM((rows, PAIR), BF16) for rows in (256, 128, 128, 128)],
        in_specs=[pl.BlockSpec(memory_space=pltpu.VMEM)] * 4,
        out_specs=[pl.BlockSpec(memory_space=pltpu.VMEM)] * 4,
        scratch_shapes=[pltpu.VMEM((256, PAIR), F32)],
        compiler_params=pltpu.CompilerParams(vmem_limit_bytes=SMALL_LIMIT),
        cost_estimate=pl.CostEstimate(flops=1000000, bytes_accessed=100000, transcendentals=0),
        name="join",
    )(after, own, odd, even)


def shifted(rows):
    place = lax.broadcasted_iota(jnp.int32, rows.shape, 0) % 8
    before = jnp.where(place == 0, 0.0, jnp.roll(rows, 1, axis=0))
    after = jnp.where(place == 7, 0.0, jnp.roll(rows, -1, axis=0))
    return before, rows, after


def column_windows(cells, p2m_ref, far_rows, near_rows):
    multipole = lax.dot_general(
        cells.astype(BF16), p2m_ref[...], (((1,), (1,)), ((), ())), preferred_element_type=F32
    )
    sources = shifted(multipole.astype(BF16).astype(F32))
    blank = jnp.zeros((8, PAIR), F32)
    count = cells.shape[0] // 64
    for b in range(3):
        for y in range(count):
            slab = sources[b][64 * y : 64 * y + 64]
            for offset_x in range(7):
                if offset_x == 0:
                    window = jnp.concatenate([blank, slab[0:8], blank, slab[16:24]], axis=0)
                elif offset_x == 6:
                    window = jnp.concatenate([slab[40:48], blank, slab[56:64], blank], axis=0)
                else:
                    window = slab[8 * (offset_x - 1) : 8 * (offset_x + 3)]
                far_rows[offset_x, b, 32 * y : 32 * y + 32] = window.astype(BF16)
    before, same, after = shifted(cells)
    lane = lax.broadcasted_iota(jnp.int32, cells.shape, 1)
    beside = jnp.where(lane < WIDTH, after, before)
    for k, kind in enumerate((same, beside)):
        for y in range(count):
            for offset_x in range(3):
                near_rows[offset_x, k, 32 * y : 32 * y + 32] = kind[
                    64 * y + 8 * (offset_x + 1) : 64 * y + 8 * (offset_x + 5)
                ].astype(BF16)


def far_product(far_rows, rows, blocks):
    chunks, weights = [], []
    for offset_x in range(7):
        for b, block in enumerate(blocks(offset_x)):
            if block is not None:
                chunks.append(far_rows[offset_x, b, rows])
                weights.append(block)
    return jnp.dot(
        jnp.concatenate(chunks, axis=1), jnp.concatenate(weights, axis=0), preferred_element_type=F32
    )


def near_product(near_rows, rows, near_ref, offset_y):
    chunks = [near_rows[offset_x, k, rows] for offset_x in range(3) for k in range(2)]
    weights = [near_ref[offset_x, offset_y].reshape(2 * PAIR, PAIR) for offset_x in range(3)]
    return jnp.dot(
        jnp.concatenate(chunks, axis=1), jnp.concatenate(weights, axis=0), preferred_element_type=F32
    )


def inner_kernel(own_ref, m2l_ref, near_ref, p2m_ref, far_out, near_out, table_out, far_rows, near_rows):
    column_windows(own_ref[...].astype(F32), p2m_ref, far_rows, near_rows)
    far_out[...] = jnp.zeros_like(far_out)
    for offset_y in range(7):
        targets = [3] if offset_y == 0 else [0] if offset_y == 6 else [
            target for target in range(4) if 0 <= target + offset_y - 3 <= 3
        ]
        start = targets[0] + offset_y - 3

        def packing(offset_x):
            blocks = far_blocks(m2l_ref, offset_x, offset_y)
            if offset_y != 3:
                for b, block in enumerate(blocks):
                    table_out[offset_x, offset_y, b] = jnp.zeros((PAIR, PAIR), BF16) if block is None else block
            return blocks

        product = far_product(far_rows, slice(32 * start, 32 * (start + len(targets))), packing)
        far_out[32 * targets[0] : 32 * (targets[-1] + 1)] += product
    near_out[...] = near_product(near_rows, slice(0, 128), near_ref, 1)
    near_out[32:128] += near_product(near_rows, slice(0, 96), near_ref, 0)
    near_out[0:96] += near_product(near_rows, slice(32, 128), near_ref, 2)


def add_halo(cells_ref, trade, far, near, table_ref, near_ref, p2m_ref, far_rows, near_rows):
    place = lax.axis_index("gy")
    first, step = trade
    after = jnp.logical_and(lax.rem(place, step) == first, place + 1 < lax.axis_size("gy"))
    before = jnp.logical_and(lax.rem(place + step - 1, step) == first, place > 0)

    @pl.when(jnp.logical_or(before, after))
    def _():
        side = jnp.where(before, 0, 1)
        column_windows(cells_ref[...].astype(F32), p2m_ref, far_rows, near_rows)

        def blocks(index):
            return lambda offset_x: [table_ref[offset_x, 4 * side + index, b] for b in range(3)]

        pair = far_product(far_rows, slice(0, 64), blocks(1))
        odd = far_product(far_rows, slice(0, 32), blocks(0))
        even = far_product(far_rows, slice(32, 64), blocks(2))
        far[pl.ds(pl.multiple_of(64 * side, 64), 64)] += pair + jnp.concatenate([even, odd], axis=0)
        rows = pl.ds(pl.multiple_of(32 - 32 * side, 32), 32)
        near[pl.ds(pl.multiple_of(96 * side, 32), 32)] += near_product(near_rows, rows, near_ref, 2 * side)


def outer_kernel(
    trade, far_part, near_part, cells_ref, far_ref, near_ref, p2m_ref, far_out, near_out, far_rows, near_rows
):
    far_out[...] = far_part[...]
    near_out[...] = near_part[...]
    add_halo(cells_ref, trade, far_out, near_out, far_ref, near_ref, p2m_ref, far_rows, near_rows)


def last_kernel(
    trade, far_part, near_part, cells_ref, far_ref, near_ref, p2m_ref, l2p_ref,
    out_ref, far, near, far_rows, near_rows,
):
    pairs = out_ref.shape[2] // PAIR
    far[...] = far_part[...]
    near[...] = near_part[...]
    add_halo(cells_ref, trade, far, near, far_ref, near_ref, p2m_ref, far_rows, near_rows)
    near[...] += jnp.dot(far[...].astype(BF16), l2p_ref[...], preferred_element_type=F32)
    for x in range(4):
        for pair in range(pairs):
            out_ref[x, :, pair * PAIR : (pair + 1) * PAIR] = near[
                pl.ds(x * pairs + pair, 4, stride=4 * pairs), :
            ]


def inner(own, m2l_table, near, p2m):
    return pl.pallas_call(
        inner_kernel,
        out_shape=[
            pltpu.VMEM((128, PAIR), F32),
            pltpu.VMEM((128, PAIR), F32),
            pltpu.VMEM((7, 7, 3, PAIR, PAIR), BF16),
        ],
        in_specs=[pl.BlockSpec(memory_space=pltpu.VMEM)] * 4,
        out_specs=[pl.BlockSpec(memory_space=pltpu.VMEM)] * 3,
        scratch_shapes=[pltpu.VMEM((7, 3, 128, PAIR), BF16), pltpu.VMEM((3, 2, 128, PAIR), BF16)],
        compiler_params=pltpu.CompilerParams(vmem_limit_bytes=VMEM_LIMIT),
        cost_estimate=pl.CostEstimate(flops=400000000, bytes_accessed=6000000, transcendentals=0),
        name="inner",
    )(own, m2l_table, near, p2m)


def outer(trade, far_part, near_part, cells, far, near, p2m):
    return pl.pallas_call(
        functools.partial(outer_kernel, trade),
        out_shape=[pltpu.VMEM((128, PAIR), F32)] * 2,
        in_specs=[pl.BlockSpec(memory_space=pltpu.VMEM)] * 6,
        out_specs=[pl.BlockSpec(memory_space=pltpu.VMEM)] * 2,
        scratch_shapes=[pltpu.VMEM((7, 3, 64, PAIR), BF16), pltpu.VMEM((3, 2, 64, PAIR), BF16)],
        compiler_params=pltpu.CompilerParams(vmem_limit_bytes=VMEM_LIMIT),
        cost_estimate=pl.CostEstimate(flops=200000000, bytes_accessed=3000000, transcendentals=0),
        name="outer",
    )(far_part, near_part, cells, far, near, p2m)


def last(trade, shape, far_part, near_part, cells, far, near, p2m, l2p):
    return pl.pallas_call(
        functools.partial(last_kernel, trade),
        out_shape=jax.ShapeDtypeStruct(shape, F32),
        in_specs=[pl.BlockSpec(memory_space=pltpu.VMEM)] * 7,
        out_specs=pl.BlockSpec(memory_space=pltpu.VMEM),
        scratch_shapes=[
            pltpu.VMEM((128, PAIR), F32),
            pltpu.VMEM((128, PAIR), F32),
            pltpu.VMEM((7, 3, 64, PAIR), BF16),
            pltpu.VMEM((3, 2, 64, PAIR), BF16),
        ],
        compiler_params=pltpu.CompilerParams(vmem_limit_bytes=VMEM_LIMIT),
        cost_estimate=pl.CostEstimate(flops=200000000, bytes_accessed=3000000, transcendentals=0),
        name="last",
    )(far_part, near_part, cells, far, near, p2m, l2p)


def local(density, p2m_operator, m2l_table, near_table, l2p_operator):
    odd, even = swapped(density, "gx", 1, 2), swapped(density, "gx", 0, 2)
    near, p2m, l2p = packed(first(), p2m_operator, near_table, l2p_operator)
    own, to_odd, *to_even = joined(p2m, density, odd, even)
    trades = ((0, 4), (1, 2), (2, 4))
    halos = [swapped(part, "gy", *trade) for part, trade in zip((to_even[0], to_odd, to_even[1]), trades)]
    *parts, far = inner(own, m2l_table, near, p2m)
    for trade, halo in zip(trades[:-1], halos):
        parts = outer(trade, *parts, halo, far, near, p2m)
    return last(trades[-1], density.shape, *parts, halos[-1], far, near, p2m, l2p)


def solution(mesh):
    placed = (P("gx", "gy", None), P(), P(), P(), P())
    return jax.shard_map(
        local, mesh=mesh, in_specs=placed, out_specs=P("gx", "gy", None), check_vma=False
    )
```

```python
import functools

import jax
import jax.numpy as jnp
from jax import lax
from jax.experimental import pallas as pl
from jax.experimental.pallas import tpu as pltpu
from jax.sharding import PartitionSpec as P

BF16 = jnp.bfloat16
F32 = jnp.float32
WIDTH = 64
PAIR = 2 * WIDTH
VMEM_LIMIT = 40 * 1024 * 1024
SMALL_LIMIT = 8 * 1024 * 1024


AXES = ("gx", "gy")


def swapped(cells, axis, first, step):
    sizes = [lax.axis_size(name) for name in AXES]
    dim = AXES.index(axis)
    pairs = []
    for place in range(sizes[0] * sizes[1]):
        at = list(divmod(place, sizes[1]))
        if at[dim] % step == first and at[dim] + 1 < sizes[dim]:
            at[dim] += 1
        elif at[dim] > 0 and (at[dim] - 1) % step == first:
            at[dim] -= 1
        elif (at[1 - dim] ^ 1) < sizes[1 - dim]:
            at[1 - dim] ^= 1
        else:
            continue
        pairs.append((place, at[0] * sizes[1] + at[1]))
    return lax.ppermute(cells, AXES, pairs)


def square(block):
    rows, columns = block.shape
    if columns < WIDTH:
        block = jnp.concatenate([block, jnp.zeros((rows, WIDTH - columns), BF16)], axis=1)
    if rows < WIDTH:
        block = jnp.concatenate([block, jnp.zeros((WIDTH - rows, WIDTH), BF16)], axis=0)
    return block


def first_kernel(out_ref):
    out_ref[...] = jnp.zeros_like(out_ref)


def first():
    return pl.pallas_call(
        first_kernel,
        out_shape=pltpu.VMEM((8, PAIR), F32),
        out_specs=pl.BlockSpec(memory_space=pltpu.VMEM),
        compiler_params=pltpu.CompilerParams(vmem_limit_bytes=1024 * 1024),
        cost_estimate=pl.CostEstimate(flops=10000000000, bytes_accessed=1000, transcendentals=0),
        name="first",
    )()


def far_blocks(m2l_ref, offset_x, offset_y):
    inner = 2 <= offset_x <= 4 and 2 <= offset_y <= 4
    blank = jnp.zeros((WIDTH, WIDTH), BF16)
    entries = [
        blank if inner and 2 <= offset_z <= 4 else square(m2l_ref[offset_x, offset_y, offset_z])
        for offset_z in range(7)
    ]
    blocks = [jnp.concatenate([entries[s + 1], entries[s]], axis=1) for s in range(6)]
    return [
        None if inner and b == 1 else jnp.concatenate(blocks[2 * b : 2 * b + 2], axis=0) for b in range(3)
    ]


def pack_kernel(first_ref, p2m_ref, near_ref, l2p_ref, near_out, p2m_out, l2p_out):
    blank = jnp.zeros((WIDTH, WIDTH), BF16)
    for offset_x in range(3):
        for offset_y in range(3):
            before, same, after = [near_ref[offset_x, offset_y, z] for z in range(3)]
            upper = jnp.concatenate([same, before], axis=1)
            lower = jnp.concatenate([after, same], axis=1)
            near_out[offset_x, offset_y, 0] = jnp.concatenate([upper, lower], axis=0)
            upper = jnp.concatenate([blank, after], axis=1)
            lower = jnp.concatenate([before, blank], axis=1)
            near_out[offset_x, offset_y, 1] = jnp.concatenate([upper, lower], axis=0)
    p2m = square(p2m_ref[...])
    p2m_out[...] = jnp.concatenate(
        [jnp.concatenate([p2m, blank], axis=1), jnp.concatenate([blank, p2m], axis=1)], axis=0
    )
    l2p = square(l2p_ref[...])
    l2p_out[...] = jnp.concatenate(
        [jnp.concatenate([l2p, blank], axis=1), jnp.concatenate([blank, l2p], axis=1)], axis=0
    )


def packed(start, p2m_operator, near_table, l2p_operator):
    shapes = [(3, 3, 2, PAIR, PAIR), (PAIR, PAIR), (PAIR, PAIR)]
    return pl.pallas_call(
        pack_kernel,
        out_shape=[pltpu.VMEM(shape, BF16) for shape in shapes],
        in_specs=[pl.BlockSpec(memory_space=pltpu.VMEM)] * 4,
        out_specs=[pl.BlockSpec(memory_space=pltpu.VMEM)] * 3,
        compiler_params=pltpu.CompilerParams(vmem_limit_bytes=SMALL_LIMIT),
        cost_estimate=pl.CostEstimate(flops=4000000, bytes_accessed=10000000, transcendentals=0),
        name="pack",
    )(start, p2m_operator.T, near_table, l2p_operator)


def from_neighbours(axis, even_low, odd_low, even_high, odd_high):
    place = lax.axis_index(axis)
    lower = lax.rem(place, 2) == 0
    low = jnp.where(place == 0, 0.0, jnp.where(lower, odd_low, even_low))
    last = place == lax.axis_size(axis) - 1
    high = jnp.where(last, 0.0, jnp.where(lower, even_high, odd_high))
    return low, high


def join_kernel(
    trade, own_ref, odd_ref, even_ref, m2l_ref, near_ref, p2m_ref,
    own_out, odd_out, even_out, sums_out, rows_ref, far_rows, near_rows,
):
    pairs = own_ref.shape[2] // PAIR
    for pair in range(pairs):
        lanes = slice(pair * PAIR, (pair + 1) * PAIR)

        def part(ref, x):
            return ref[x, :, lanes].astype(F32)

        for x in range(8):
            if 2 <= x < 6:
                cells = part(own_ref, x - 2)
            else:
                low, high = from_neighbours(
                    "gx",
                    *((part(even_ref, 2 + x), part(odd_ref, 2 + x)) if x < 2 else (0.0, 0.0)),
                    *((part(even_ref, x - 6), part(odd_ref, x - 6)) if x > 5 else (0.0, 0.0)),
                )
                cells = low if x < 2 else high
            rows_ref[pl.ds(x * pairs + pair, 4, stride=8 * pairs), :] = cells
    rows = rows_ref[...]
    own_out[...] = rows.astype(BF16)
    lower = lax.rem(lax.axis_index("gy"), 2) == 0
    head, tail = rows[:128], rows[128:]
    even_out[...] = jnp.where(lower, tail, head).astype(BF16)
    odd_out[...] = jnp.where(lower, head, tail).astype(BF16)
    sums_out[...] = jnp.where(lower, tail, head).astype(BF16)
    before, _ = partners(trade)

    @pl.when(before)
    def _():
        column_windows(rows_ref[:128], p2m_ref, far_rows, near_rows)
        sums = halo_sums(lambda offset_x, index: far_blocks(m2l_ref, offset_x, 4 + index), far_rows)
        sums_out[:64] = sums.astype(BF16)
        sums_out[64:96] = near_product(near_rows, slice(0, 32), near_ref, 2).astype(BF16)
        sums_out[96:] = jnp.zeros((32, PAIR), BF16)


def joined(trade, own, odd, even, m2l_table, near, p2m):
    return pl.pallas_call(
        functools.partial(join_kernel, trade),
        out_shape=[pltpu.VMEM((rows, PAIR), BF16) for rows in (256, 128, 128, 128)],
        in_specs=[pl.BlockSpec(memory_space=pltpu.VMEM)] * 6,
        out_specs=[pl.BlockSpec(memory_space=pltpu.VMEM)] * 4,
        scratch_shapes=[
            pltpu.VMEM((256, PAIR), F32),
            pltpu.VMEM((7, 3, 64, PAIR), BF16),
            pltpu.VMEM((3, 2, 64, PAIR), BF16),
        ],
        compiler_params=pltpu.CompilerParams(vmem_limit_bytes=SMALL_LIMIT),
        cost_estimate=pl.CostEstimate(flops=1000000, bytes_accessed=100000, transcendentals=0),
        name="join",
    )(own, odd, even, m2l_table, near, p2m)


def shifted(rows):
    place = lax.broadcasted_iota(jnp.int32, rows.shape, 0) % 8
    before = jnp.where(place == 0, 0.0, jnp.roll(rows, 1, axis=0))
    after = jnp.where(place == 7, 0.0, jnp.roll(rows, -1, axis=0))
    return before, rows, after


def column_windows(cells, p2m_ref, far_rows, near_rows):
    multipole = lax.dot_general(
        cells.astype(BF16), p2m_ref[...], (((1,), (1,)), ((), ())), preferred_element_type=F32
    )
    sources = shifted(multipole.astype(BF16).astype(F32))
    blank = jnp.zeros((8, PAIR), F32)
    count = cells.shape[0] // 64
    for b in range(3):
        for y in range(count):
            slab = sources[b][64 * y : 64 * y + 64]
            for offset_x in range(7):
                if offset_x == 0:
                    window = jnp.concatenate([blank, slab[0:8], blank, slab[16:24]], axis=0)
                elif offset_x == 6:
                    window = jnp.concatenate([slab[40:48], blank, slab[56:64], blank], axis=0)
                else:
                    window = slab[8 * (offset_x - 1) : 8 * (offset_x + 3)]
                far_rows[offset_x, b, 32 * y : 32 * y + 32] = window.astype(BF16)
    before, same, after = shifted(cells)
    lane = lax.broadcasted_iota(jnp.int32, cells.shape, 1)
    beside = jnp.where(lane < WIDTH, after, before)
    for k, kind in enumerate((same, beside)):
        for y in range(count):
            for offset_x in range(3):
                near_rows[offset_x, k, 32 * y : 32 * y + 32] = kind[
                    64 * y + 8 * (offset_x + 1) : 64 * y + 8 * (offset_x + 5)
                ].astype(BF16)


def far_product(far_rows, rows, blocks):
    chunks, weights = [], []
    for offset_x in range(7):
        for b, block in enumerate(blocks(offset_x)):
            if block is not None:
                chunks.append(far_rows[offset_x, b, rows])
                weights.append(block)
    return jnp.dot(
        jnp.concatenate(chunks, axis=1), jnp.concatenate(weights, axis=0), preferred_element_type=F32
    )


def near_product(near_rows, rows, near_ref, offset_y):
    chunks = [near_rows[offset_x, k, rows] for offset_x in range(3) for k in range(2)]
    weights = [near_ref[offset_x, offset_y].reshape(2 * PAIR, PAIR) for offset_x in range(3)]
    return jnp.dot(
        jnp.concatenate(chunks, axis=1), jnp.concatenate(weights, axis=0), preferred_element_type=F32
    )


def inner_kernel(own_ref, m2l_ref, near_ref, p2m_ref, far_out, near_out, table_out, far_rows, near_rows):
    column_windows(own_ref[...].astype(F32), p2m_ref, far_rows, near_rows)
    far_out[...] = jnp.zeros_like(far_out)
    for offset_y in range(7):
        targets = [3] if offset_y == 0 else [0] if offset_y == 6 else [
            target for target in range(4) if 0 <= target + offset_y - 3 <= 3
        ]
        start = targets[0] + offset_y - 3

        def packing(offset_x):
            blocks = far_blocks(m2l_ref, offset_x, offset_y)
            if offset_y != 3:
                for b, block in enumerate(blocks):
                    table_out[offset_x, offset_y, b] = jnp.zeros((PAIR, PAIR), BF16) if block is None else block
            return blocks

        product = far_product(far_rows, slice(32 * start, 32 * (start + len(targets))), packing)
        far_out[32 * targets[0] : 32 * (targets[-1] + 1)] += product
    near_out[...] = near_product(near_rows, slice(0, 128), near_ref, 1)
    near_out[32:128] += near_product(near_rows, slice(0, 96), near_ref, 0)
    near_out[0:96] += near_product(near_rows, slice(32, 128), near_ref, 2)


def halo_sums(blocks, far_rows):
    pair = far_product(far_rows, slice(0, 64), lambda offset_x: blocks(offset_x, 1))
    odd = far_product(far_rows, slice(0, 32), lambda offset_x: blocks(offset_x, 0))
    even = far_product(far_rows, slice(32, 64), lambda offset_x: blocks(offset_x, 2))
    return pair + jnp.concatenate([even, odd], axis=0)


def add_halo(cells_ref, before, after, far, near, table_ref, near_ref, p2m_ref, far_rows, near_rows):
    @pl.when(jnp.logical_or(before, after))
    def _():
        side = jnp.where(before, 0, 1)
        column_windows(cells_ref[...].astype(F32), p2m_ref, far_rows, near_rows)

        def blocks(offset_x, index):
            return [table_ref[offset_x, 4 * side + index, b] for b in range(3)]

        far[pl.ds(pl.multiple_of(64 * side, 64), 64)] += halo_sums(blocks, far_rows)
        rows = pl.ds(pl.multiple_of(32 - 32 * side, 32), 32)
        near[pl.ds(pl.multiple_of(96 * side, 32), 32)] += near_product(near_rows, rows, near_ref, 2 * side)


def partners(trade):
    place = lax.axis_index("gy")
    first, step = trade
    after = jnp.logical_and(lax.rem(place, step) == first, place + 1 < lax.axis_size("gy"))
    before = jnp.logical_and(lax.rem(place + step - 1, step) == first, place > 0)
    return before, after


def outer_kernel(
    trade, far_part, near_part, cells_ref, far_ref, near_ref, p2m_ref, far_out, near_out, far_rows, near_rows
):
    far_out[...] = far_part[...]
    near_out[...] = near_part[...]
    add_halo(cells_ref, *partners(trade), far_out, near_out, far_ref, near_ref, p2m_ref, far_rows, near_rows)


def last_kernel(
    trade, far_part, near_part, cells_ref, far_ref, near_ref, p2m_ref, l2p_ref,
    out_ref, far, near, far_rows, near_rows,
):
    pairs = out_ref.shape[2] // PAIR
    far[...] = far_part[...]
    near[...] = near_part[...]
    before, after = partners(trade)
    add_halo(cells_ref, before, False, far, near, far_ref, near_ref, p2m_ref, far_rows, near_rows)

    @pl.when(after)
    def _():
        far[64:128] += cells_ref[:64].astype(F32)
        near[96:128] += cells_ref[64:96].astype(F32)

    near[...] += jnp.dot(far[...].astype(BF16), l2p_ref[...], preferred_element_type=F32)
    for x in range(4):
        for pair in range(pairs):
            out_ref[x, :, pair * PAIR : (pair + 1) * PAIR] = near[
                pl.ds(x * pairs + pair, 4, stride=4 * pairs), :
            ]


def inner(own, m2l_table, near, p2m):
    return pl.pallas_call(
        inner_kernel,
        out_shape=[
            pltpu.VMEM((128, PAIR), F32),
            pltpu.VMEM((128, PAIR), F32),
            pltpu.VMEM((7, 7, 3, PAIR, PAIR), BF16),
        ],
        in_specs=[pl.BlockSpec(memory_space=pltpu.VMEM)] * 4,
        out_specs=[pl.BlockSpec(memory_space=pltpu.VMEM)] * 3,
        scratch_shapes=[pltpu.VMEM((7, 3, 128, PAIR), BF16), pltpu.VMEM((3, 2, 128, PAIR), BF16)],
        compiler_params=pltpu.CompilerParams(vmem_limit_bytes=VMEM_LIMIT),
        cost_estimate=pl.CostEstimate(flops=400000000, bytes_accessed=6000000, transcendentals=0),
        name="inner",
    )(own, m2l_table, near, p2m)


def outer(trade, far_part, near_part, cells, far, near, p2m):
    return pl.pallas_call(
        functools.partial(outer_kernel, trade),
        out_shape=[pltpu.VMEM((128, PAIR), F32)] * 2,
        in_specs=[pl.BlockSpec(memory_space=pltpu.VMEM)] * 6,
        out_specs=[pl.BlockSpec(memory_space=pltpu.VMEM)] * 2,
        scratch_shapes=[pltpu.VMEM((7, 3, 64, PAIR), BF16), pltpu.VMEM((3, 2, 64, PAIR), BF16)],
        compiler_params=pltpu.CompilerParams(vmem_limit_bytes=VMEM_LIMIT),
        cost_estimate=pl.CostEstimate(flops=200000000, bytes_accessed=3000000, transcendentals=0),
        name="outer",
    )(far_part, near_part, cells, far, near, p2m)


def last(trade, shape, far_part, near_part, cells, far, near, p2m, l2p):
    return pl.pallas_call(
        functools.partial(last_kernel, trade),
        out_shape=jax.ShapeDtypeStruct(shape, F32),
        in_specs=[pl.BlockSpec(memory_space=pltpu.VMEM)] * 7,
        out_specs=pl.BlockSpec(memory_space=pltpu.VMEM),
        scratch_shapes=[
            pltpu.VMEM((128, PAIR), F32),
            pltpu.VMEM((128, PAIR), F32),
            pltpu.VMEM((7, 3, 64, PAIR), BF16),
            pltpu.VMEM((3, 2, 64, PAIR), BF16),
        ],
        compiler_params=pltpu.CompilerParams(vmem_limit_bytes=VMEM_LIMIT),
        cost_estimate=pl.CostEstimate(flops=200000000, bytes_accessed=3000000, transcendentals=0),
        name="last",
    )(far_part, near_part, cells, far, near, p2m, l2p)


def local(density, p2m_operator, m2l_table, near_table, l2p_operator):
    odd, even = swapped(density, "gx", 1, 2), swapped(density, "gx", 0, 2)
    near, p2m, l2p = packed(first(), p2m_operator, near_table, l2p_operator)
    trades = ((0, 4), (1, 2), (2, 4))
    own, to_odd, to_even, sums = joined(trades[-1], density, odd, even, m2l_table, near, p2m)
    halos = [swapped(part, "gy", *trade) for part, trade in zip((to_even, to_odd, sums), trades)]
    *parts, far = inner(own, m2l_table, near, p2m)
    for trade, halo in zip(trades[:-1], halos):
        parts = outer(trade, *parts, halo, far, near, p2m)
    return last(trades[-1], density.shape, *parts, halos[-1], far, near, p2m, l2p)


def solution(mesh):
    placed = (P("gx", "gy", None), P(), P(), P(), P())
    return jax.shard_map(
        local, mesh=mesh, in_specs=placed, out_specs=P("gx", "gy", None), check_vma=False
    )
```

```python
import functools

import jax
import jax.numpy as jnp
from jax import lax
from jax.experimental import pallas as pl
from jax.experimental.pallas import tpu as pltpu
from jax.sharding import PartitionSpec as P

BF16 = jnp.bfloat16
F32 = jnp.float32
WIDTH = 64
PAIR = 2 * WIDTH
VMEM_LIMIT = 40 * 1024 * 1024
SMALL_LIMIT = 8 * 1024 * 1024


AXES = ("gx", "gy")


def swapped(cells, axis, first, step):
    sizes = [lax.axis_size(name) for name in AXES]
    dim = AXES.index(axis)
    pairs = []
    for place in range(sizes[0] * sizes[1]):
        at = list(divmod(place, sizes[1]))
        if at[dim] % step == first and at[dim] + 1 < sizes[dim]:
            at[dim] += 1
        elif at[dim] > 0 and (at[dim] - 1) % step == first:
            at[dim] -= 1
        elif (at[1 - dim] ^ 1) < sizes[1 - dim]:
            at[1 - dim] ^= 1
        else:
            continue
        pairs.append((place, at[0] * sizes[1] + at[1]))
    return lax.ppermute(cells, AXES, pairs)


def square(block):
    rows, columns = block.shape
    if columns < WIDTH:
        block = jnp.concatenate([block, jnp.zeros((rows, WIDTH - columns), BF16)], axis=1)
    if rows < WIDTH:
        block = jnp.concatenate([block, jnp.zeros((WIDTH - rows, WIDTH), BF16)], axis=0)
    return block


def first_kernel(out_ref):
    out_ref[...] = jnp.zeros_like(out_ref)


def first():
    return pl.pallas_call(
        first_kernel,
        out_shape=pltpu.VMEM((8, PAIR), F32),
        out_specs=pl.BlockSpec(memory_space=pltpu.VMEM),
        compiler_params=pltpu.CompilerParams(vmem_limit_bytes=1024 * 1024),
        cost_estimate=pl.CostEstimate(flops=10000000000, bytes_accessed=1000, transcendentals=0),
        name="first",
    )()


def far_blocks(m2l_ref, offset_x, offset_y):
    inner = 2 <= offset_x <= 4 and 2 <= offset_y <= 4
    blank = jnp.zeros((WIDTH, WIDTH), BF16)
    entries = [
        blank if inner and 2 <= offset_z <= 4 else square(m2l_ref[offset_x, offset_y, offset_z])
        for offset_z in range(7)
    ]
    blocks = [jnp.concatenate([entries[s + 1], entries[s]], axis=1) for s in range(6)]
    return [
        None if inner and b == 1 else jnp.concatenate(blocks[2 * b : 2 * b + 2], axis=0) for b in range(3)
    ]


def pack_kernel(first_ref, p2m_ref, near_ref, l2p_ref, near_out, p2m_out, l2p_out):
    blank = jnp.zeros((WIDTH, WIDTH), BF16)
    for offset_x in range(3):
        for offset_y in range(3):
            before, same, after = [near_ref[offset_x, offset_y, z] for z in range(3)]
            upper = jnp.concatenate([same, before], axis=1)
            lower = jnp.concatenate([after, same], axis=1)
            near_out[offset_x, offset_y, 0] = jnp.concatenate([upper, lower], axis=0)
            upper = jnp.concatenate([blank, after], axis=1)
            lower = jnp.concatenate([before, blank], axis=1)
            near_out[offset_x, offset_y, 1] = jnp.concatenate([upper, lower], axis=0)
    p2m = square(p2m_ref[...])
    p2m_out[...] = jnp.concatenate(
        [jnp.concatenate([p2m, blank], axis=1), jnp.concatenate([blank, p2m], axis=1)], axis=0
    )
    l2p = square(l2p_ref[...])
    l2p_out[...] = jnp.concatenate(
        [jnp.concatenate([l2p, blank], axis=1), jnp.concatenate([blank, l2p], axis=1)], axis=0
    )


def packed(start, p2m_operator, near_table, l2p_operator):
    shapes = [(3, 3, 2, PAIR, PAIR), (PAIR, PAIR), (PAIR, PAIR)]
    return pl.pallas_call(
        pack_kernel,
        out_shape=[pltpu.VMEM(shape, BF16) for shape in shapes],
        in_specs=[pl.BlockSpec(memory_space=pltpu.VMEM)] * 4,
        out_specs=[pl.BlockSpec(memory_space=pltpu.VMEM)] * 3,
        compiler_params=pltpu.CompilerParams(vmem_limit_bytes=SMALL_LIMIT),
        cost_estimate=pl.CostEstimate(flops=4000000, bytes_accessed=10000000, transcendentals=0),
        name="pack",
    )(start, p2m_operator.T, near_table, l2p_operator)


def from_neighbours(axis, even_low, odd_low, even_high, odd_high):
    place = lax.axis_index(axis)
    lower = lax.rem(place, 2) == 0
    low = jnp.where(place == 0, 0.0, jnp.where(lower, odd_low, even_low))
    last = place == lax.axis_size(axis) - 1
    high = jnp.where(last, 0.0, jnp.where(lower, even_high, odd_high))
    return low, high


def join_kernel(
    trade, own_ref, odd_ref, even_ref, m2l_ref, near_ref, p2m_ref,
    own_out, odd_out, even_out, sums_out, rows_ref, far_rows, near_rows,
):
    pairs = own_ref.shape[2] // PAIR
    for pair in range(pairs):
        lanes = slice(pair * PAIR, (pair + 1) * PAIR)

        def part(ref, x):
            return ref[x, :, lanes].astype(F32)

        for x in range(8):
            if 2 <= x < 6:
                cells = part(own_ref, x - 2)
            else:
                low, high = from_neighbours(
                    "gx",
                    *((part(even_ref, 2 + x), part(odd_ref, 2 + x)) if x < 2 else (0.0, 0.0)),
                    *((part(even_ref, x - 6), part(odd_ref, x - 6)) if x > 5 else (0.0, 0.0)),
                )
                cells = low if x < 2 else high
            rows_ref[pl.ds(x * pairs + pair, 4, stride=8 * pairs), :] = cells
    rows = rows_ref[...]
    own_out[...] = rows.astype(BF16)
    lower = lax.rem(lax.axis_index("gy"), 2) == 0
    head, tail = rows[:128], rows[128:]
    even_out[...] = jnp.where(lower, tail, head).astype(BF16)
    odd_out[...] = jnp.where(lower, head, tail).astype(BF16)
    sums_out[...] = jnp.where(lower, tail, head).astype(BF16)
    before, _ = partners(trade)

    @pl.when(before)
    def _():
        column_windows(rows_ref[:128], p2m_ref, far_rows, near_rows)
        sums = halo_sums(lambda offset_x, index: far_blocks(m2l_ref, offset_x, 4 + index), far_rows)
        sums_out[:64] = sums.astype(BF16)
        near = near_product(near_rows, slice(0, 32), near_ref, 2)
        rounded = near.astype(BF16)
        sums_out[64:96] = rounded
        sums_out[96:] = (near - rounded.astype(F32)).astype(BF16)


def joined(trade, own, odd, even, m2l_table, near, p2m):
    return pl.pallas_call(
        functools.partial(join_kernel, trade),
        out_shape=[pltpu.VMEM((rows, PAIR), BF16) for rows in (256, 128, 128, 128)],
        in_specs=[pl.BlockSpec(memory_space=pltpu.VMEM)] * 6,
        out_specs=[pl.BlockSpec(memory_space=pltpu.VMEM)] * 4,
        scratch_shapes=[
            pltpu.VMEM((256, PAIR), F32),
            pltpu.VMEM((7, 3, 64, PAIR), BF16),
            pltpu.VMEM((3, 2, 64, PAIR), BF16),
        ],
        compiler_params=pltpu.CompilerParams(vmem_limit_bytes=SMALL_LIMIT),
        cost_estimate=pl.CostEstimate(flops=1000000, bytes_accessed=100000, transcendentals=0),
        name="join",
    )(own, odd, even, m2l_table, near, p2m)


def shifted(rows):
    place = lax.broadcasted_iota(jnp.int32, rows.shape, 0) % 8
    before = jnp.where(place == 0, 0.0, jnp.roll(rows, 1, axis=0))
    after = jnp.where(place == 7, 0.0, jnp.roll(rows, -1, axis=0))
    return before, rows, after


def column_windows(cells, p2m_ref, far_rows, near_rows):
    multipole = lax.dot_general(
        cells.astype(BF16), p2m_ref[...], (((1,), (1,)), ((), ())), preferred_element_type=F32
    )
    sources = shifted(multipole.astype(BF16).astype(F32))
    blank = jnp.zeros((8, PAIR), F32)
    count = cells.shape[0] // 64
    for b in range(3):
        for y in range(count):
            slab = sources[b][64 * y : 64 * y + 64]
            for offset_x in range(7):
                if offset_x == 0:
                    window = jnp.concatenate([blank, slab[0:8], blank, slab[16:24]], axis=0)
                elif offset_x == 6:
                    window = jnp.concatenate([slab[40:48], blank, slab[56:64], blank], axis=0)
                else:
                    window = slab[8 * (offset_x - 1) : 8 * (offset_x + 3)]
                far_rows[offset_x, b, 32 * y : 32 * y + 32] = window.astype(BF16)
    before, same, after = shifted(cells)
    lane = lax.broadcasted_iota(jnp.int32, cells.shape, 1)
    beside = jnp.where(lane < WIDTH, after, before)
    for k, kind in enumerate((same, beside)):
        for y in range(count):
            for offset_x in range(3):
                near_rows[offset_x, k, 32 * y : 32 * y + 32] = kind[
                    64 * y + 8 * (offset_x + 1) : 64 * y + 8 * (offset_x + 5)
                ].astype(BF16)


def far_product(far_rows, rows, blocks):
    chunks, weights = [], []
    for offset_x in range(7):
        for b, block in enumerate(blocks(offset_x)):
            if block is not None:
                chunks.append(far_rows[offset_x, b, rows])
                weights.append(block)
    return jnp.dot(
        jnp.concatenate(chunks, axis=1), jnp.concatenate(weights, axis=0), preferred_element_type=F32
    )


def near_product(near_rows, rows, near_ref, offset_y):
    chunks = [near_rows[offset_x, k, rows] for offset_x in range(3) for k in range(2)]
    weights = [near_ref[offset_x, offset_y].reshape(2 * PAIR, PAIR) for offset_x in range(3)]
    return jnp.dot(
        jnp.concatenate(chunks, axis=1), jnp.concatenate(weights, axis=0), preferred_element_type=F32
    )


def inner_kernel(own_ref, m2l_ref, near_ref, p2m_ref, far_out, near_out, table_out, far_rows, near_rows):
    column_windows(own_ref[...].astype(F32), p2m_ref, far_rows, near_rows)
    far_out[...] = jnp.zeros_like(far_out)
    for offset_y in range(7):
        targets = [3] if offset_y == 0 else [0] if offset_y == 6 else [
            target for target in range(4) if 0 <= target + offset_y - 3 <= 3
        ]
        start = targets[0] + offset_y - 3

        def packing(offset_x):
            blocks = far_blocks(m2l_ref, offset_x, offset_y)
            if offset_y != 3:
                for b, block in enumerate(blocks):
                    table_out[offset_x, offset_y, b] = jnp.zeros((PAIR, PAIR), BF16) if block is None else block
            return blocks

        product = far_product(far_rows, slice(32 * start, 32 * (start + len(targets))), packing)
        far_out[32 * targets[0] : 32 * (targets[-1] + 1)] += product
    near_out[...] = near_product(near_rows, slice(0, 128), near_ref, 1)
    near_out[32:128] += near_product(near_rows, slice(0, 96), near_ref, 0)
    near_out[0:96] += near_product(near_rows, slice(32, 128), near_ref, 2)


def halo_sums(blocks, far_rows):
    pair = far_product(far_rows, slice(0, 64), lambda offset_x: blocks(offset_x, 1))
    odd = far_product(far_rows, slice(0, 32), lambda offset_x: blocks(offset_x, 0))
    even = far_product(far_rows, slice(32, 64), lambda offset_x: blocks(offset_x, 2))
    return pair + jnp.concatenate([even, odd], axis=0)


def add_halo(cells_ref, before, after, far, near, table_ref, near_ref, p2m_ref, far_rows, near_rows):
    @pl.when(jnp.logical_or(before, after))
    def _():
        side = jnp.where(before, 0, 1)
        column_windows(cells_ref[...].astype(F32), p2m_ref, far_rows, near_rows)

        def blocks(offset_x, index):
            return [table_ref[offset_x, 4 * side + index, b] for b in range(3)]

        far[pl.ds(pl.multiple_of(64 * side, 64), 64)] += halo_sums(blocks, far_rows)
        rows = pl.ds(pl.multiple_of(32 - 32 * side, 32), 32)
        near[pl.ds(pl.multiple_of(96 * side, 32), 32)] += near_product(near_rows, rows, near_ref, 2 * side)


def partners(trade):
    place = lax.axis_index("gy")
    first, step = trade
    after = jnp.logical_and(lax.rem(place, step) == first, place + 1 < lax.axis_size("gy"))
    before = jnp.logical_and(lax.rem(place + step - 1, step) == first, place > 0)
    return before, after


def outer_kernel(
    trade, far_part, near_part, cells_ref, far_ref, near_ref, p2m_ref, far_out, near_out, far_rows, near_rows
):
    far_out[...] = far_part[...]
    near_out[...] = near_part[...]
    add_halo(cells_ref, *partners(trade), far_out, near_out, far_ref, near_ref, p2m_ref, far_rows, near_rows)


def last_kernel(
    trade, far_part, near_part, cells_ref, far_ref, near_ref, p2m_ref, l2p_ref,
    out_ref, far, near, far_rows, near_rows,
):
    pairs = out_ref.shape[2] // PAIR
    far[...] = far_part[...]
    near[...] = near_part[...]
    before, after = partners(trade)
    add_halo(cells_ref, before, False, far, near, far_ref, near_ref, p2m_ref, far_rows, near_rows)

    @pl.when(after)
    def _():
        far[64:128] += cells_ref[:64].astype(F32)
        near[96:128] += cells_ref[64:96].astype(F32) + cells_ref[96:128].astype(F32)

    near[...] += jnp.dot(far[...].astype(BF16), l2p_ref[...], preferred_element_type=F32)
    for x in range(4):
        for pair in range(pairs):
            out_ref[x, :, pair * PAIR : (pair + 1) * PAIR] = near[
                pl.ds(x * pairs + pair, 4, stride=4 * pairs), :
            ]


def inner(own, m2l_table, near, p2m):
    return pl.pallas_call(
        inner_kernel,
        out_shape=[
            pltpu.VMEM((128, PAIR), F32),
            pltpu.VMEM((128, PAIR), F32),
            pltpu.VMEM((7, 7, 3, PAIR, PAIR), BF16),
        ],
        in_specs=[pl.BlockSpec(memory_space=pltpu.VMEM)] * 4,
        out_specs=[pl.BlockSpec(memory_space=pltpu.VMEM)] * 3,
        scratch_shapes=[pltpu.VMEM((7, 3, 128, PAIR), BF16), pltpu.VMEM((3, 2, 128, PAIR), BF16)],
        compiler_params=pltpu.CompilerParams(vmem_limit_bytes=VMEM_LIMIT),
        cost_estimate=pl.CostEstimate(flops=400000000, bytes_accessed=6000000, transcendentals=0),
        name="inner",
    )(own, m2l_table, near, p2m)


def outer(trade, far_part, near_part, cells, far, near, p2m):
    return pl.pallas_call(
        functools.partial(outer_kernel, trade),
        out_shape=[pltpu.VMEM((128, PAIR), F32)] * 2,
        in_specs=[pl.BlockSpec(memory_space=pltpu.VMEM)] * 6,
        out_specs=[pl.BlockSpec(memory_space=pltpu.VMEM)] * 2,
        scratch_shapes=[pltpu.VMEM((7, 3, 64, PAIR), BF16), pltpu.VMEM((3, 2, 64, PAIR), BF16)],
        compiler_params=pltpu.CompilerParams(vmem_limit_bytes=VMEM_LIMIT),
        cost_estimate=pl.CostEstimate(flops=200000000, bytes_accessed=3000000, transcendentals=0),
        name="outer",
    )(far_part, near_part, cells, far, near, p2m)


def last(trade, shape, far_part, near_part, cells, far, near, p2m, l2p):
    return pl.pallas_call(
        functools.partial(last_kernel, trade),
        out_shape=jax.ShapeDtypeStruct(shape, F32),
        in_specs=[pl.BlockSpec(memory_space=pltpu.VMEM)] * 7,
        out_specs=pl.BlockSpec(memory_space=pltpu.VMEM),
        scratch_shapes=[
            pltpu.VMEM((128, PAIR), F32),
            pltpu.VMEM((128, PAIR), F32),
            pltpu.VMEM((7, 3, 64, PAIR), BF16),
            pltpu.VMEM((3, 2, 64, PAIR), BF16),
        ],
        compiler_params=pltpu.CompilerParams(vmem_limit_bytes=VMEM_LIMIT),
        cost_estimate=pl.CostEstimate(flops=200000000, bytes_accessed=3000000, transcendentals=0),
        name="last",
    )(far_part, near_part, cells, far, near, p2m, l2p)


def local(density, p2m_operator, m2l_table, near_table, l2p_operator):
    odd, even = swapped(density, "gx", 1, 2), swapped(density, "gx", 0, 2)
    near, p2m, l2p = packed(first(), p2m_operator, near_table, l2p_operator)
    trades = ((0, 4), (1, 2), (2, 4))
    own, to_odd, to_even, sums = joined(trades[-1], density, odd, even, m2l_table, near, p2m)
    halos = [swapped(part, "gy", *trade) for part, trade in zip((to_even, to_odd, sums), trades)]
    *parts, far = inner(own, m2l_table, near, p2m)
    for trade, halo in zip(trades[:-1], halos):
        parts = outer(trade, *parts, halo, far, near, p2m)
    return last(trades[-1], density.shape, *parts, halos[-1], far, near, p2m, l2p)


def solution(mesh):
    placed = (P("gx", "gy", None), P(), P(), P(), P())
    return jax.shard_map(
        local, mesh=mesh, in_specs=placed, out_specs=P("gx", "gy", None), check_vma=False
    )
```

```python
import functools

import jax
import jax.numpy as jnp
from jax import lax
from jax.experimental import pallas as pl
from jax.experimental.pallas import tpu as pltpu
from jax.sharding import PartitionSpec as P

BF16 = jnp.bfloat16
F32 = jnp.float32
WIDTH = 64
PAIR = 2 * WIDTH
VMEM_LIMIT = 40 * 1024 * 1024
SMALL_LIMIT = 8 * 1024 * 1024


AXES = ("gx", "gy")


def swapped(cells, axis, first, step):
    sizes = [lax.axis_size(name) for name in AXES]
    dim = AXES.index(axis)
    pairs = []
    for place in range(sizes[0] * sizes[1]):
        at = list(divmod(place, sizes[1]))
        if at[dim] % step == first and at[dim] + 1 < sizes[dim]:
            at[dim] += 1
        elif at[dim] > 0 and (at[dim] - 1) % step == first:
            at[dim] -= 1
        elif (at[1 - dim] ^ 1) < sizes[1 - dim]:
            at[1 - dim] ^= 1
        else:
            continue
        pairs.append((place, at[0] * sizes[1] + at[1]))
    return lax.ppermute(cells, AXES, pairs)


def square(block):
    rows, columns = block.shape
    if columns < WIDTH:
        block = jnp.concatenate([block, jnp.zeros((rows, WIDTH - columns), BF16)], axis=1)
    if rows < WIDTH:
        block = jnp.concatenate([block, jnp.zeros((WIDTH - rows, WIDTH), BF16)], axis=0)
    return block


def first_kernel(out_ref):
    out_ref[...] = jnp.zeros_like(out_ref)


def first():
    return pl.pallas_call(
        first_kernel,
        out_shape=pltpu.VMEM((8, PAIR), F32),
        out_specs=pl.BlockSpec(memory_space=pltpu.VMEM),
        compiler_params=pltpu.CompilerParams(vmem_limit_bytes=1024 * 1024),
        cost_estimate=pl.CostEstimate(flops=10000000000, bytes_accessed=1000, transcendentals=0),
        name="first",
    )()


def far_blocks(m2l_ref, offset_x, offset_y):
    inner = 2 <= offset_x <= 4 and 2 <= offset_y <= 4
    blank = jnp.zeros((WIDTH, WIDTH), BF16)
    entries = [
        blank if inner and 2 <= offset_z <= 4 else square(m2l_ref[offset_x, offset_y, offset_z])
        for offset_z in range(7)
    ]
    blocks = [jnp.concatenate([entries[s + 1], entries[s]], axis=1) for s in range(6)]
    return [
        None if inner and b == 1 else jnp.concatenate(blocks[2 * b : 2 * b + 2], axis=0) for b in range(3)
    ]


def pack_kernel(first_ref, p2m_ref, near_ref, l2p_ref, near_out, p2m_out, l2p_out):
    blank = jnp.zeros((WIDTH, WIDTH), BF16)
    for offset_x in range(3):
        for offset_y in range(3):
            before, same, after = [near_ref[offset_x, offset_y, z] for z in range(3)]
            upper = jnp.concatenate([same, before], axis=1)
            lower = jnp.concatenate([after, same], axis=1)
            near_out[offset_x, offset_y, 0] = jnp.concatenate([upper, lower], axis=0)
            upper = jnp.concatenate([blank, after], axis=1)
            lower = jnp.concatenate([before, blank], axis=1)
            near_out[offset_x, offset_y, 1] = jnp.concatenate([upper, lower], axis=0)
    p2m = square(p2m_ref[...])
    p2m_out[...] = jnp.concatenate(
        [jnp.concatenate([p2m, blank], axis=1), jnp.concatenate([blank, p2m], axis=1)], axis=0
    )
    l2p = square(l2p_ref[...])
    l2p_out[...] = jnp.concatenate(
        [jnp.concatenate([l2p, blank], axis=1), jnp.concatenate([blank, l2p], axis=1)], axis=0
    )


def packed(start, p2m_operator, near_table, l2p_operator):
    shapes = [(3, 3, 2, PAIR, PAIR), (PAIR, PAIR), (PAIR, PAIR)]
    return pl.pallas_call(
        pack_kernel,
        out_shape=[pltpu.VMEM(shape, BF16) for shape in shapes],
        in_specs=[pl.BlockSpec(memory_space=pltpu.VMEM)] * 4,
        out_specs=[pl.BlockSpec(memory_space=pltpu.VMEM)] * 3,
        compiler_params=pltpu.CompilerParams(vmem_limit_bytes=SMALL_LIMIT),
        cost_estimate=pl.CostEstimate(flops=4000000, bytes_accessed=10000000, transcendentals=0),
        name="pack",
    )(start, p2m_operator.T, near_table, l2p_operator)


def from_neighbours(axis, even_low, odd_low, even_high, odd_high):
    place = lax.axis_index(axis)
    lower = lax.rem(place, 2) == 0
    low = jnp.where(place == 0, 0.0, jnp.where(lower, odd_low, even_low))
    last = place == lax.axis_size(axis) - 1
    high = jnp.where(last, 0.0, jnp.where(lower, even_high, odd_high))
    return low, high


def join_kernel(
    trade, own_ref, odd_ref, even_ref, m2l_ref, near_ref, p2m_ref,
    own_out, odd_out, even_out, sums_out, ready_out, rows_ref, far_rows, near_rows, own_rows,
):
    pairs = own_ref.shape[2] // PAIR
    for pair in range(pairs):
        lanes = slice(pair * PAIR, (pair + 1) * PAIR)

        def part(ref, x):
            return ref[x, :, lanes].astype(F32)

        for x in range(8):
            if 2 <= x < 6:
                cells = part(own_ref, x - 2)
            else:
                low, high = from_neighbours(
                    "gx",
                    *((part(even_ref, 2 + x), part(odd_ref, 2 + x)) if x < 2 else (0.0, 0.0)),
                    *((part(even_ref, x - 6), part(odd_ref, x - 6)) if x > 5 else (0.0, 0.0)),
                )
                cells = low if x < 2 else high
            rows_ref[pl.ds(x * pairs + pair, 4, stride=8 * pairs), :] = cells
    rows = rows_ref[...]
    own_out[...] = rows.astype(BF16)
    lower = lax.rem(lax.axis_index("gy"), 2) == 0
    head, tail = rows[:128], rows[128:]
    even_out[...] = jnp.where(lower, tail, head).astype(BF16)
    odd_out[...] = jnp.where(lower, head, tail).astype(BF16)
    sums_out[...] = jnp.where(lower, tail, head).astype(BF16)
    before, _ = partners(trade)

    @pl.when(waits_longest())
    def _():
        own_near(rows_ref[...], ready_out, near_ref, own_rows)

    @pl.when(before)
    def _():
        column_windows(rows_ref[:128], p2m_ref, far_rows, near_rows)
        sums = halo_sums(lambda offset_x, index: far_blocks(m2l_ref, offset_x, 4 + index), far_rows)
        sums_out[:64] = sums.astype(BF16)
        near = near_product(near_rows, slice(0, 32), near_ref, 2)
        rounded = near.astype(BF16)
        sums_out[64:96] = rounded
        sums_out[96:] = (near - rounded.astype(F32)).astype(BF16)


def joined(trade, own, odd, even, m2l_table, near, p2m):
    return pl.pallas_call(
        functools.partial(join_kernel, trade),
        out_shape=[pltpu.VMEM((rows, PAIR), BF16) for rows in (256, 128, 128, 128)]
        + [pltpu.VMEM((128, PAIR), F32)],
        in_specs=[pl.BlockSpec(memory_space=pltpu.VMEM)] * 6,
        out_specs=[pl.BlockSpec(memory_space=pltpu.VMEM)] * 5,
        scratch_shapes=[
            pltpu.VMEM((256, PAIR), F32),
            pltpu.VMEM((7, 3, 64, PAIR), BF16),
            pltpu.VMEM((3, 2, 64, PAIR), BF16),
            pltpu.VMEM((3, 2, 128, PAIR), BF16),
        ],
        compiler_params=pltpu.CompilerParams(vmem_limit_bytes=SMALL_LIMIT),
        cost_estimate=pl.CostEstimate(flops=1000000, bytes_accessed=100000, transcendentals=0),
        name="join",
    )(own, odd, even, m2l_table, near, p2m)


def shifted(rows):
    place = lax.broadcasted_iota(jnp.int32, rows.shape, 0) % 8
    before = jnp.where(place == 0, 0.0, jnp.roll(rows, 1, axis=0))
    after = jnp.where(place == 7, 0.0, jnp.roll(rows, -1, axis=0))
    return before, rows, after


def far_windows(cells, p2m_ref, far_rows):
    multipole = lax.dot_general(
        cells.astype(BF16), p2m_ref[...], (((1,), (1,)), ((), ())), preferred_element_type=F32
    )
    sources = shifted(multipole.astype(BF16).astype(F32))
    blank = jnp.zeros((8, PAIR), F32)
    count = cells.shape[0] // 64
    for b in range(3):
        for y in range(count):
            slab = sources[b][64 * y : 64 * y + 64]
            for offset_x in range(7):
                if offset_x == 0:
                    window = jnp.concatenate([blank, slab[0:8], blank, slab[16:24]], axis=0)
                elif offset_x == 6:
                    window = jnp.concatenate([slab[40:48], blank, slab[56:64], blank], axis=0)
                else:
                    window = slab[8 * (offset_x - 1) : 8 * (offset_x + 3)]
                far_rows[offset_x, b, 32 * y : 32 * y + 32] = window.astype(BF16)


def near_windows(cells, near_rows):
    count = cells.shape[0] // 64
    before, same, after = shifted(cells)
    lane = lax.broadcasted_iota(jnp.int32, cells.shape, 1)
    beside = jnp.where(lane < WIDTH, after, before)
    for k, kind in enumerate((same, beside)):
        for y in range(count):
            for offset_x in range(3):
                near_rows[offset_x, k, 32 * y : 32 * y + 32] = kind[
                    64 * y + 8 * (offset_x + 1) : 64 * y + 8 * (offset_x + 5)
                ].astype(BF16)


def column_windows(cells, p2m_ref, far_rows, near_rows):
    far_windows(cells, p2m_ref, far_rows)
    near_windows(cells, near_rows)


def waits_longest():
    return jnp.logical_and(lax.axis_index("gx") < 2, lax.axis_index("gy") == 0)


def own_near(cells, near_out, near_ref, near_rows):
    near_windows(cells, near_rows)
    near_out[...] = near_product(near_rows, slice(0, 128), near_ref, 1)
    near_out[32:128] += near_product(near_rows, slice(0, 96), near_ref, 0)
    near_out[0:96] += near_product(near_rows, slice(32, 128), near_ref, 2)


def far_product(far_rows, rows, blocks):
    chunks, weights = [], []
    for offset_x in range(7):
        for b, block in enumerate(blocks(offset_x)):
            if block is not None:
                chunks.append(far_rows[offset_x, b, rows])
                weights.append(block)
    return jnp.dot(
        jnp.concatenate(chunks, axis=1), jnp.concatenate(weights, axis=0), preferred_element_type=F32
    )


def near_product(near_rows, rows, near_ref, offset_y):
    chunks = [near_rows[offset_x, k, rows] for offset_x in range(3) for k in range(2)]
    weights = [near_ref[offset_x, offset_y].reshape(2 * PAIR, PAIR) for offset_x in range(3)]
    return jnp.dot(
        jnp.concatenate(chunks, axis=1), jnp.concatenate(weights, axis=0), preferred_element_type=F32
    )


def inner_kernel(
    own_ref, ready_ref, m2l_ref, near_ref, p2m_ref, far_out, near_out, table_out, far_rows, near_rows
):
    far_windows(own_ref[...].astype(F32), p2m_ref, far_rows)
    far_out[...] = jnp.zeros_like(far_out)
    for offset_y in range(7):
        targets = [3] if offset_y == 0 else [0] if offset_y == 6 else [
            target for target in range(4) if 0 <= target + offset_y - 3 <= 3
        ]
        start = targets[0] + offset_y - 3

        def packing(offset_x):
            blocks = far_blocks(m2l_ref, offset_x, offset_y)
            if offset_y != 3:
                for b, block in enumerate(blocks):
                    table_out[offset_x, offset_y, b] = jnp.zeros((PAIR, PAIR), BF16) if block is None else block
            return blocks

        product = far_product(far_rows, slice(32 * start, 32 * (start + len(targets))), packing)
        far_out[32 * targets[0] : 32 * (targets[-1] + 1)] += product
    early = waits_longest()

    @pl.when(early)
    def _():
        near_out[...] = ready_ref[...]

    @pl.when(jnp.logical_not(early))
    def _():
        own_near(own_ref[...].astype(F32), near_out, near_ref, near_rows)


def halo_sums(blocks, far_rows):
    pair = far_product(far_rows, slice(0, 64), lambda offset_x: blocks(offset_x, 1))
    odd = far_product(far_rows, slice(0, 32), lambda offset_x: blocks(offset_x, 0))
    even = far_product(far_rows, slice(32, 64), lambda offset_x: blocks(offset_x, 2))
    return pair + jnp.concatenate([even, odd], axis=0)


def add_halo(cells_ref, before, after, far, near, table_ref, near_ref, p2m_ref, far_rows, near_rows):
    @pl.when(jnp.logical_or(before, after))
    def _():
        side = jnp.where(before, 0, 1)
        column_windows(cells_ref[...].astype(F32), p2m_ref, far_rows, near_rows)

        def blocks(offset_x, index):
            return [table_ref[offset_x, 4 * side + index, b] for b in range(3)]

        far[pl.ds(pl.multiple_of(64 * side, 64), 64)] += halo_sums(blocks, far_rows)
        rows = pl.ds(pl.multiple_of(32 - 32 * side, 32), 32)
        near[pl.ds(pl.multiple_of(96 * side, 32), 32)] += near_product(near_rows, rows, near_ref, 2 * side)


def partners(trade):
    place = lax.axis_index("gy")
    first, step = trade
    after = jnp.logical_and(lax.rem(place, step) == first, place + 1 < lax.axis_size("gy"))
    before = jnp.logical_and(lax.rem(place + step - 1, step) == first, place > 0)
    return before, after


def outer_kernel(
    trade, far_part, near_part, cells_ref, far_ref, near_ref, p2m_ref, far_out, near_out, far_rows, near_rows
):
    far_out[...] = far_part[...]
    near_out[...] = near_part[...]
    add_halo(cells_ref, *partners(trade), far_out, near_out, far_ref, near_ref, p2m_ref, far_rows, near_rows)


def last_kernel(
    trade, far_part, near_part, cells_ref, far_ref, near_ref, p2m_ref, l2p_ref,
    out_ref, far, near, far_rows, near_rows,
):
    pairs = out_ref.shape[2] // PAIR
    far[...] = far_part[...]
    near[...] = near_part[...]
    before, after = partners(trade)
    add_halo(cells_ref, before, False, far, near, far_ref, near_ref, p2m_ref, far_rows, near_rows)

    @pl.when(after)
    def _():
        far[64:128] += cells_ref[:64].astype(F32)
        near[96:128] += cells_ref[64:96].astype(F32) + cells_ref[96:128].astype(F32)

    near[...] += jnp.dot(far[...].astype(BF16), l2p_ref[...], preferred_element_type=F32)
    for x in range(4):
        for pair in range(pairs):
            out_ref[x, :, pair * PAIR : (pair + 1) * PAIR] = near[
                pl.ds(x * pairs + pair, 4, stride=4 * pairs), :
            ]


def inner(own, ready, m2l_table, near, p2m):
    return pl.pallas_call(
        inner_kernel,
        out_shape=[
            pltpu.VMEM((128, PAIR), F32),
            pltpu.VMEM((128, PAIR), F32),
            pltpu.VMEM((7, 7, 3, PAIR, PAIR), BF16),
        ],
        in_specs=[pl.BlockSpec(memory_space=pltpu.VMEM)] * 5,
        out_specs=[pl.BlockSpec(memory_space=pltpu.VMEM)] * 3,
        scratch_shapes=[pltpu.VMEM((7, 3, 128, PAIR), BF16), pltpu.VMEM((3, 2, 128, PAIR), BF16)],
        compiler_params=pltpu.CompilerParams(vmem_limit_bytes=VMEM_LIMIT),
        cost_estimate=pl.CostEstimate(flops=400000000, bytes_accessed=6000000, transcendentals=0),
        name="inner",
    )(own, ready, m2l_table, near, p2m)


def outer(trade, far_part, near_part, cells, far, near, p2m):
    return pl.pallas_call(
        functools.partial(outer_kernel, trade),
        out_shape=[pltpu.VMEM((128, PAIR), F32)] * 2,
        in_specs=[pl.BlockSpec(memory_space=pltpu.VMEM)] * 6,
        out_specs=[pl.BlockSpec(memory_space=pltpu.VMEM)] * 2,
        scratch_shapes=[pltpu.VMEM((7, 3, 64, PAIR), BF16), pltpu.VMEM((3, 2, 64, PAIR), BF16)],
        compiler_params=pltpu.CompilerParams(vmem_limit_bytes=VMEM_LIMIT),
        cost_estimate=pl.CostEstimate(flops=200000000, bytes_accessed=3000000, transcendentals=0),
        name="outer",
    )(far_part, near_part, cells, far, near, p2m)


def last(trade, shape, far_part, near_part, cells, far, near, p2m, l2p):
    return pl.pallas_call(
        functools.partial(last_kernel, trade),
        out_shape=jax.ShapeDtypeStruct(shape, F32),
        in_specs=[pl.BlockSpec(memory_space=pltpu.VMEM)] * 7,
        out_specs=pl.BlockSpec(memory_space=pltpu.VMEM),
        scratch_shapes=[
            pltpu.VMEM((128, PAIR), F32),
            pltpu.VMEM((128, PAIR), F32),
            pltpu.VMEM((7, 3, 64, PAIR), BF16),
            pltpu.VMEM((3, 2, 64, PAIR), BF16),
        ],
        compiler_params=pltpu.CompilerParams(vmem_limit_bytes=VMEM_LIMIT),
        cost_estimate=pl.CostEstimate(flops=200000000, bytes_accessed=3000000, transcendentals=0),
        name="last",
    )(far_part, near_part, cells, far, near, p2m, l2p)


def local(density, p2m_operator, m2l_table, near_table, l2p_operator):
    odd, even = swapped(density, "gx", 1, 2), swapped(density, "gx", 0, 2)
    near, p2m, l2p = packed(first(), p2m_operator, near_table, l2p_operator)
    trades = ((0, 4), (1, 2), (2, 4))
    own, to_odd, to_even, sums, ready = joined(trades[-1], density, odd, even, m2l_table, near, p2m)
    halos = [swapped(part, "gy", *trade) for part, trade in zip((to_even, to_odd, sums), trades)]
    *parts, far = inner(own, ready, m2l_table, near, p2m)
    for trade, halo in zip(trades[:-1], halos):
        parts = outer(trade, *parts, halo, far, near, p2m)
    return last(trades[-1], density.shape, *parts, halos[-1], far, near, p2m, l2p)


def solution(mesh):
    placed = (P("gx", "gy", None), P(), P(), P(), P())
    return jax.shard_map(
        local, mesh=mesh, in_specs=placed, out_specs=P("gx", "gy", None), check_vma=False
    )
```

```python
import functools

import jax
import jax.numpy as jnp
from jax import lax
from jax.experimental import pallas as pl
from jax.experimental.pallas import tpu as pltpu
from jax.sharding import PartitionSpec as P

BF16 = jnp.bfloat16
F32 = jnp.float32
WIDTH = 64
PAIR = 2 * WIDTH
VMEM_LIMIT = 40 * 1024 * 1024
SMALL_LIMIT = 8 * 1024 * 1024


AXES = ("gx", "gy")


def swapped(cells, axis, first, step):
    sizes = [lax.axis_size(name) for name in AXES]
    dim = AXES.index(axis)
    pairs = []
    for place in range(sizes[0] * sizes[1]):
        at = list(divmod(place, sizes[1]))
        if at[dim] % step == first and at[dim] + 1 < sizes[dim]:
            at[dim] += 1
        elif at[dim] > 0 and (at[dim] - 1) % step == first:
            at[dim] -= 1
        elif (at[1 - dim] ^ 1) < sizes[1 - dim]:
            at[1 - dim] ^= 1
        else:
            continue
        pairs.append((place, at[0] * sizes[1] + at[1]))
    return lax.ppermute(cells, AXES, pairs)


def square(block):
    rows, columns = block.shape
    if columns < WIDTH:
        block = jnp.concatenate([block, jnp.zeros((rows, WIDTH - columns), BF16)], axis=1)
    if rows < WIDTH:
        block = jnp.concatenate([block, jnp.zeros((WIDTH - rows, WIDTH), BF16)], axis=0)
    return block


def first_kernel(out_ref):
    out_ref[...] = jnp.zeros_like(out_ref)


def first():
    return pl.pallas_call(
        first_kernel,
        out_shape=pltpu.VMEM((8, PAIR), F32),
        out_specs=pl.BlockSpec(memory_space=pltpu.VMEM),
        compiler_params=pltpu.CompilerParams(vmem_limit_bytes=1024 * 1024),
        cost_estimate=pl.CostEstimate(flops=10000000000, bytes_accessed=1000, transcendentals=0),
        name="first",
    )()


def far_blocks(m2l_ref, offset_x, offset_y):
    inner = 2 <= offset_x <= 4 and 2 <= offset_y <= 4
    blank = jnp.zeros((WIDTH, WIDTH), BF16)
    entries = [
        blank if inner and 2 <= offset_z <= 4 else square(m2l_ref[offset_x, offset_y, offset_z])
        for offset_z in range(7)
    ]
    blocks = [jnp.concatenate([entries[s + 1], entries[s]], axis=1) for s in range(6)]
    return [
        None if inner and b == 1 else jnp.concatenate(blocks[2 * b : 2 * b + 2], axis=0) for b in range(3)
    ]


def pack_kernel(first_ref, p2m_ref, near_ref, l2p_ref, near_out, p2m_out, l2p_out):
    blank = jnp.zeros((WIDTH, WIDTH), BF16)
    for offset_x in range(3):
        for offset_y in range(3):
            before, same, after = [near_ref[offset_x, offset_y, z] for z in range(3)]
            upper = jnp.concatenate([same, before], axis=1)
            lower = jnp.concatenate([after, same], axis=1)
            near_out[offset_x, offset_y, 0] = jnp.concatenate([upper, lower], axis=0)
            upper = jnp.concatenate([blank, after], axis=1)
            lower = jnp.concatenate([before, blank], axis=1)
            near_out[offset_x, offset_y, 1] = jnp.concatenate([upper, lower], axis=0)
    p2m = square(p2m_ref[...])
    p2m_out[...] = jnp.concatenate(
        [jnp.concatenate([p2m, blank], axis=1), jnp.concatenate([blank, p2m], axis=1)], axis=0
    )
    l2p = square(l2p_ref[...])
    l2p_out[...] = jnp.concatenate(
        [jnp.concatenate([l2p, blank], axis=1), jnp.concatenate([blank, l2p], axis=1)], axis=0
    )


def packed(start, p2m_operator, near_table, l2p_operator):
    shapes = [(3, 3, 2, PAIR, PAIR), (PAIR, PAIR), (PAIR, PAIR)]
    return pl.pallas_call(
        pack_kernel,
        out_shape=[pltpu.VMEM(shape, BF16) for shape in shapes],
        in_specs=[pl.BlockSpec(memory_space=pltpu.VMEM)] * 4,
        out_specs=[pl.BlockSpec(memory_space=pltpu.VMEM)] * 3,
        compiler_params=pltpu.CompilerParams(vmem_limit_bytes=SMALL_LIMIT),
        cost_estimate=pl.CostEstimate(flops=4000000, bytes_accessed=10000000, transcendentals=0),
        name="pack",
    )(start, p2m_operator.T, near_table, l2p_operator)


def from_neighbours(axis, even_low, odd_low, even_high, odd_high):
    place = lax.axis_index(axis)
    lower = lax.rem(place, 2) == 0
    low = jnp.where(place == 0, 0.0, jnp.where(lower, odd_low, even_low))
    last = place == lax.axis_size(axis) - 1
    high = jnp.where(last, 0.0, jnp.where(lower, even_high, odd_high))
    return low, high


def join_kernel(
    trade, own_ref, odd_ref, even_ref, m2l_ref, near_ref, p2m_ref,
    own_out, odd_out, even_out, sums_out, ready_out, rows_ref, far_rows, near_rows, own_rows,
):
    pairs = own_ref.shape[2] // PAIR
    for pair in range(pairs):
        lanes = slice(pair * PAIR, (pair + 1) * PAIR)

        def part(ref, x):
            return ref[x, :, lanes].astype(F32)

        for x in range(8):
            if 2 <= x < 6:
                cells = part(own_ref, x - 2)
            else:
                low, high = from_neighbours(
                    "gx",
                    *((part(even_ref, 2 + x), part(odd_ref, 2 + x)) if x < 2 else (0.0, 0.0)),
                    *((part(even_ref, x - 6), part(odd_ref, x - 6)) if x > 5 else (0.0, 0.0)),
                )
                cells = low if x < 2 else high
            rows_ref[pl.ds(x * pairs + pair, 4, stride=8 * pairs), :] = cells
    rows = rows_ref[...]
    own_out[...] = rows.astype(BF16)
    lower = lax.rem(lax.axis_index("gy"), 2) == 0
    head, tail = rows[:128], rows[128:]
    even_out[...] = jnp.where(lower, tail, head).astype(BF16)
    odd_out[...] = jnp.where(lower, head, tail).astype(BF16)
    sums_out[...] = jnp.where(lower, tail, head).astype(BF16)
    before, _ = partners(trade)

    @pl.when(waits_longest())
    def _():
        own_near(rows_ref[...], ready_out, near_ref, own_rows)

    @pl.when(before)
    def _():
        near_windows(rows_ref[:64], near_rows)
        far_windows(rows_ref[:128], p2m_ref, far_rows)
        sums = halo_sums(lambda offset_x, index: far_blocks(m2l_ref, offset_x, 4 + index), far_rows)
        sums_out[:64] = sums.astype(BF16)
        near = near_product(near_rows, slice(0, 32), near_ref, 2)
        rounded = near.astype(BF16)
        sums_out[64:96] = rounded
        sums_out[96:] = (near - rounded.astype(F32)).astype(BF16)


def joined(trade, own, odd, even, m2l_table, near, p2m):
    return pl.pallas_call(
        functools.partial(join_kernel, trade),
        out_shape=[pltpu.VMEM((rows, PAIR), BF16) for rows in (256, 128, 128, 128)]
        + [pltpu.VMEM((128, PAIR), F32)],
        in_specs=[pl.BlockSpec(memory_space=pltpu.VMEM)] * 6,
        out_specs=[pl.BlockSpec(memory_space=pltpu.VMEM)] * 5,
        scratch_shapes=[
            pltpu.VMEM((256, PAIR), F32),
            pltpu.VMEM((7, 3, 64, PAIR), BF16),
            pltpu.VMEM((3, 2, 64, PAIR), BF16),
            pltpu.VMEM((3, 2, 128, PAIR), BF16),
        ],
        compiler_params=pltpu.CompilerParams(vmem_limit_bytes=SMALL_LIMIT),
        cost_estimate=pl.CostEstimate(flops=1000000, bytes_accessed=100000, transcendentals=0),
        name="join",
    )(own, odd, even, m2l_table, near, p2m)


def shifted(rows):
    place = lax.broadcasted_iota(jnp.int32, rows.shape, 0) % 8
    before = jnp.where(place == 0, 0.0, jnp.roll(rows, 1, axis=0))
    after = jnp.where(place == 7, 0.0, jnp.roll(rows, -1, axis=0))
    return before, rows, after


def far_windows(cells, p2m_ref, far_rows):
    multipole = lax.dot_general(
        cells.astype(BF16), p2m_ref[...], (((1,), (1,)), ((), ())), preferred_element_type=F32
    )
    sources = shifted(multipole.astype(BF16).astype(F32))
    blank = jnp.zeros((8, PAIR), F32)
    count = cells.shape[0] // 64
    for b in range(3):
        for y in range(count):
            slab = sources[b][64 * y : 64 * y + 64]
            for offset_x in range(7):
                if offset_x == 0:
                    window = jnp.concatenate([blank, slab[0:8], blank, slab[16:24]], axis=0)
                elif offset_x == 6:
                    window = jnp.concatenate([slab[40:48], blank, slab[56:64], blank], axis=0)
                else:
                    window = slab[8 * (offset_x - 1) : 8 * (offset_x + 3)]
                far_rows[offset_x, b, 32 * y : 32 * y + 32] = window.astype(BF16)


def near_windows(cells, near_rows):
    count = cells.shape[0] // 64
    before, same, after = shifted(cells)
    lane = lax.broadcasted_iota(jnp.int32, cells.shape, 1)
    beside = jnp.where(lane < WIDTH, after, before)
    for k, kind in enumerate((same, beside)):
        for y in range(count):
            for offset_x in range(3):
                near_rows[offset_x, k, 32 * y : 32 * y + 32] = kind[
                    64 * y + 8 * (offset_x + 1) : 64 * y + 8 * (offset_x + 5)
                ].astype(BF16)


def waits_longest():
    return jnp.logical_and(lax.axis_index("gx") < 2, lax.axis_index("gy") == 0)


def own_near(cells, near_out, near_ref, near_rows):
    near_windows(cells, near_rows)
    near_out[...] = near_product(near_rows, slice(0, 128), near_ref, 1)
    near_out[32:128] += near_product(near_rows, slice(0, 96), near_ref, 0)
    near_out[0:96] += near_product(near_rows, slice(32, 128), near_ref, 2)


def far_product(far_rows, rows, blocks):
    chunks, weights = [], []
    for offset_x in range(7):
        for b, block in enumerate(blocks(offset_x)):
            if block is not None:
                chunks.append(far_rows[offset_x, b, rows])
                weights.append(block)
    return jnp.dot(
        jnp.concatenate(chunks, axis=1), jnp.concatenate(weights, axis=0), preferred_element_type=F32
    )


def near_product(near_rows, rows, near_ref, offset_y):
    chunks = [near_rows[offset_x, k, rows] for offset_x in range(3) for k in range(2)]
    weights = [near_ref[offset_x, offset_y].reshape(2 * PAIR, PAIR) for offset_x in range(3)]
    return jnp.dot(
        jnp.concatenate(chunks, axis=1), jnp.concatenate(weights, axis=0), preferred_element_type=F32
    )


def inner_kernel(
    own_ref, ready_ref, m2l_ref, near_ref, p2m_ref, far_out, near_out, table_out, far_rows, near_rows
):
    far_windows(own_ref[...].astype(F32), p2m_ref, far_rows)
    far_out[...] = jnp.zeros_like(far_out)
    for offset_y in range(7):
        targets = [3] if offset_y == 0 else [0] if offset_y == 6 else [
            target for target in range(4) if 0 <= target + offset_y - 3 <= 3
        ]
        start = targets[0] + offset_y - 3

        def packing(offset_x):
            blocks = far_blocks(m2l_ref, offset_x, offset_y)
            if offset_y != 3:
                for b, block in enumerate(blocks):
                    table_out[offset_x, offset_y, b] = jnp.zeros((PAIR, PAIR), BF16) if block is None else block
            return blocks

        product = far_product(far_rows, slice(32 * start, 32 * (start + len(targets))), packing)
        far_out[32 * targets[0] : 32 * (targets[-1] + 1)] += product
    early = waits_longest()

    @pl.when(early)
    def _():
        near_out[...] = ready_ref[...]

    @pl.when(jnp.logical_not(early))
    def _():
        own_near(own_ref[...].astype(F32), near_out, near_ref, near_rows)


def halo_sums(blocks, far_rows):
    odd = far_product(far_rows, slice(0, 32), lambda offset_x: blocks(offset_x, 0))
    even = far_product(far_rows, slice(32, 64), lambda offset_x: blocks(offset_x, 2))
    pair = far_product(far_rows, slice(0, 64), lambda offset_x: blocks(offset_x, 1))
    return pair + jnp.concatenate([even, odd], axis=0)


def add_halo(cells_ref, side, far, near, table_ref, near_ref, p2m_ref, far_rows, near_rows):
    cells = cells_ref[...].astype(F32)
    far_windows(cells, p2m_ref, far_rows)
    near_windows(cells[64 - 64 * side : 128 - 64 * side], near_rows)

    def blocks(offset_x, index):
        offset_y = 4 * side + index
        inner = 2 <= offset_x <= 4 and 2 <= offset_y <= 4
        return [None if inner and b == 1 else table_ref[offset_x, offset_y, b] for b in range(3)]

    far[64 * side : 64 * side + 64] += halo_sums(blocks, far_rows)
    near[96 * side : 96 * side + 32] += near_product(
        near_rows, slice(0, 32), near_ref, 2 * side
    )


def partners(trade):
    place = lax.axis_index("gy")
    first, step = trade
    after = jnp.logical_and(lax.rem(place, step) == first, place + 1 < lax.axis_size("gy"))
    before = jnp.logical_and(lax.rem(place + step - 1, step) == first, place > 0)
    return before, after


def outer_kernel(
    trade, far_part, near_part, cells_ref, far_ref, near_ref, p2m_ref, far_out, near_out, far_rows, near_rows
):
    far_out[...] = far_part[...]
    near_out[...] = near_part[...]
    for side, used in enumerate(partners(trade)):

        @pl.when(used)
        def _():
            add_halo(cells_ref, side, far_out, near_out, far_ref, near_ref, p2m_ref, far_rows, near_rows)


def last_kernel(
    trade, far_part, near_part, cells_ref, far_ref, near_ref, p2m_ref, l2p_ref,
    out_ref, far, near, far_rows, near_rows,
):
    pairs = out_ref.shape[2] // PAIR
    far[...] = far_part[...]
    near[...] = near_part[...]
    before, after = partners(trade)

    @pl.when(before)
    def _():
        add_halo(cells_ref, 0, far, near, far_ref, near_ref, p2m_ref, far_rows, near_rows)

    @pl.when(after)
    def _():
        far[64:128] += cells_ref[:64].astype(F32)
        near[96:128] += cells_ref[64:96].astype(F32) + cells_ref[96:128].astype(F32)

    near[...] += jnp.dot(far[...].astype(BF16), l2p_ref[...], preferred_element_type=F32)
    for x in range(4):
        for pair in range(pairs):
            out_ref[x, :, pair * PAIR : (pair + 1) * PAIR] = near[
                pl.ds(x * pairs + pair, 4, stride=4 * pairs), :
            ]


def inner(own, ready, m2l_table, near, p2m):
    return pl.pallas_call(
        inner_kernel,
        out_shape=[
            pltpu.VMEM((128, PAIR), F32),
            pltpu.VMEM((128, PAIR), F32),
            pltpu.VMEM((7, 7, 3, PAIR, PAIR), BF16),
        ],
        in_specs=[pl.BlockSpec(memory_space=pltpu.VMEM)] * 5,
        out_specs=[pl.BlockSpec(memory_space=pltpu.VMEM)] * 3,
        scratch_shapes=[pltpu.VMEM((7, 3, 128, PAIR), BF16), pltpu.VMEM((3, 2, 128, PAIR), BF16)],
        compiler_params=pltpu.CompilerParams(vmem_limit_bytes=VMEM_LIMIT),
        cost_estimate=pl.CostEstimate(flops=400000000, bytes_accessed=6000000, transcendentals=0),
        name="inner",
    )(own, ready, m2l_table, near, p2m)


def outer(trade, far_part, near_part, cells, far, near, p2m):
    return pl.pallas_call(
        functools.partial(outer_kernel, trade),
        out_shape=[pltpu.VMEM((128, PAIR), F32)] * 2,
        in_specs=[pl.BlockSpec(memory_space=pltpu.VMEM)] * 6,
        out_specs=[pl.BlockSpec(memory_space=pltpu.VMEM)] * 2,
        scratch_shapes=[pltpu.VMEM((7, 3, 64, PAIR), BF16), pltpu.VMEM((3, 2, 64, PAIR), BF16)],
        compiler_params=pltpu.CompilerParams(vmem_limit_bytes=VMEM_LIMIT),
        cost_estimate=pl.CostEstimate(flops=200000000, bytes_accessed=3000000, transcendentals=0),
        name="outer",
    )(far_part, near_part, cells, far, near, p2m)


def last(trade, shape, far_part, near_part, cells, far, near, p2m, l2p):
    return pl.pallas_call(
        functools.partial(last_kernel, trade),
        out_shape=jax.ShapeDtypeStruct(shape, F32),
        in_specs=[pl.BlockSpec(memory_space=pltpu.VMEM)] * 7,
        out_specs=pl.BlockSpec(memory_space=pltpu.VMEM),
        scratch_shapes=[
            pltpu.VMEM((128, PAIR), F32),
            pltpu.VMEM((128, PAIR), F32),
            pltpu.VMEM((7, 3, 64, PAIR), BF16),
            pltpu.VMEM((3, 2, 64, PAIR), BF16),
        ],
        compiler_params=pltpu.CompilerParams(vmem_limit_bytes=VMEM_LIMIT),
        cost_estimate=pl.CostEstimate(flops=200000000, bytes_accessed=3000000, transcendentals=0),
        name="last",
    )(far_part, near_part, cells, far, near, p2m, l2p)


def local(density, p2m_operator, m2l_table, near_table, l2p_operator):
    odd, even = swapped(density, "gx", 1, 2), swapped(density, "gx", 0, 2)
    near, p2m, l2p = packed(first(), p2m_operator, near_table, l2p_operator)
    trades = ((0, 4), (1, 2), (2, 4))
    own, to_odd, to_even, sums, ready = joined(trades[-1], density, odd, even, m2l_table, near, p2m)
    halos = [swapped(part, "gy", *trade) for part, trade in zip((to_even, to_odd, sums), trades)]
    *parts, far = inner(own, ready, m2l_table, near, p2m)
    for trade, halo in zip(trades[:-1], halos):
        parts = outer(trade, *parts, halo, far, near, p2m)
    return last(trades[-1], density.shape, *parts, halos[-1], far, near, p2m, l2p)


def solution(mesh):
    placed = (P("gx", "gy", None), P(), P(), P(), P())
    return jax.shard_map(
        local, mesh=mesh, in_specs=placed, out_specs=P("gx", "gy", None), check_vma=False
    )
```

```python
import functools

import jax
import jax.numpy as jnp
from jax import lax
from jax.experimental import pallas as pl
from jax.experimental.pallas import tpu as pltpu
from jax.sharding import PartitionSpec as P

BF16 = jnp.bfloat16
F32 = jnp.float32
WIDTH = 64
PAIR = 2 * WIDTH
VMEM_LIMIT = 40 * 1024 * 1024
SMALL_LIMIT = 8 * 1024 * 1024


AXES = ("gx", "gy")


def swapped(cells, axis, first, step):
    sizes = [lax.axis_size(name) for name in AXES]
    dim = AXES.index(axis)
    pairs = []
    for place in range(sizes[0] * sizes[1]):
        at = list(divmod(place, sizes[1]))
        if at[dim] % step == first and at[dim] + 1 < sizes[dim]:
            at[dim] += 1
        elif at[dim] > 0 and (at[dim] - 1) % step == first:
            at[dim] -= 1
        elif (at[1 - dim] ^ 1) < sizes[1 - dim]:
            at[1 - dim] ^= 1
        else:
            continue
        pairs.append((place, at[0] * sizes[1] + at[1]))
    return lax.ppermute(cells, AXES, pairs)


def square(block):
    rows, columns = block.shape
    if columns < WIDTH:
        block = jnp.concatenate([block, jnp.zeros((rows, WIDTH - columns), BF16)], axis=1)
    if rows < WIDTH:
        block = jnp.concatenate([block, jnp.zeros((WIDTH - rows, WIDTH), BF16)], axis=0)
    return block


def first_kernel(out_ref):
    out_ref[...] = jnp.zeros_like(out_ref)


def first():
    return pl.pallas_call(
        first_kernel,
        out_shape=pltpu.VMEM((8, PAIR), F32),
        out_specs=pl.BlockSpec(memory_space=pltpu.VMEM),
        compiler_params=pltpu.CompilerParams(vmem_limit_bytes=1024 * 1024),
        cost_estimate=pl.CostEstimate(flops=10000000000, bytes_accessed=1000, transcendentals=0),
        name="first",
    )()


def far_blocks(m2l_ref, offset_x, offset_y):
    inner = 2 <= offset_x <= 4 and 2 <= offset_y <= 4
    blank = jnp.zeros((WIDTH, WIDTH), BF16)
    entries = [
        blank if inner and 2 <= offset_z <= 4 else square(m2l_ref[offset_x, offset_y, offset_z])
        for offset_z in range(7)
    ]
    blocks = [jnp.concatenate([entries[s + 1], entries[s]], axis=1) for s in range(6)]
    return [
        None if inner and b == 1 else jnp.concatenate(blocks[2 * b : 2 * b + 2], axis=0) for b in range(3)
    ]


def pack_kernel(first_ref, p2m_ref, near_ref, l2p_ref, near_out, p2m_out, l2p_out):
    blank = jnp.zeros((WIDTH, WIDTH), BF16)
    for offset_x in range(3):
        for offset_y in range(3):
            before, same, after = [near_ref[offset_x, offset_y, z] for z in range(3)]
            upper = jnp.concatenate([same, before], axis=1)
            lower = jnp.concatenate([after, same], axis=1)
            near_out[offset_x, offset_y, 0] = jnp.concatenate([upper, lower], axis=0)
            upper = jnp.concatenate([blank, after], axis=1)
            lower = jnp.concatenate([before, blank], axis=1)
            near_out[offset_x, offset_y, 1] = jnp.concatenate([upper, lower], axis=0)
    p2m = square(p2m_ref[...])
    p2m_out[...] = jnp.concatenate(
        [jnp.concatenate([p2m, blank], axis=1), jnp.concatenate([blank, p2m], axis=1)], axis=0
    )
    l2p = square(l2p_ref[...])
    l2p_out[...] = jnp.concatenate(
        [jnp.concatenate([l2p, blank], axis=1), jnp.concatenate([blank, l2p], axis=1)], axis=0
    )


def packed(start, p2m_operator, near_table, l2p_operator):
    shapes = [(3, 3, 2, PAIR, PAIR), (PAIR, PAIR), (PAIR, PAIR)]
    return pl.pallas_call(
        pack_kernel,
        out_shape=[pltpu.VMEM(shape, BF16) for shape in shapes],
        in_specs=[pl.BlockSpec(memory_space=pltpu.VMEM)] * 4,
        out_specs=[pl.BlockSpec(memory_space=pltpu.VMEM)] * 3,
        compiler_params=pltpu.CompilerParams(vmem_limit_bytes=SMALL_LIMIT),
        cost_estimate=pl.CostEstimate(flops=4000000, bytes_accessed=10000000, transcendentals=0),
        name="pack",
    )(start, p2m_operator.T, near_table, l2p_operator)


def from_neighbours(axis, even_low, odd_low, even_high, odd_high):
    place = lax.axis_index(axis)
    lower = lax.rem(place, 2) == 0
    low = jnp.where(place == 0, 0.0, jnp.where(lower, odd_low, even_low))
    last = place == lax.axis_size(axis) - 1
    high = jnp.where(last, 0.0, jnp.where(lower, even_high, odd_high))
    return low, high


def join_kernel(
    trade, own_ref, even_ref, odd_ref, m2l_ref, near_ref, p2m_ref,
    own_out, odd_out, even_out, sums_out, rows_ref, far_rows, near_rows,
):
    pairs = own_ref.shape[2] // PAIR
    for pair in range(pairs):
        lanes = slice(pair * PAIR, (pair + 1) * PAIR)

        def part(ref, x):
            return ref[x, :, lanes].astype(F32)

        for x in range(8):
            if 2 <= x < 6:
                cells = part(own_ref, x - 2)
            else:
                low, high = from_neighbours(
                    "gx",
                    *((part(even_ref, 2 + x), part(odd_ref, 2 + x)) if x < 2 else (0.0, 0.0)),
                    *((part(even_ref, x - 6), part(odd_ref, x - 6)) if x > 5 else (0.0, 0.0)),
                )
                cells = low if x < 2 else high
            rows_ref[pl.ds(x * pairs + pair, 4, stride=8 * pairs), :] = cells
    rows = rows_ref[...]
    own_out[...] = rows.astype(BF16)
    lower = lax.rem(lax.axis_index("gy"), 2) == 0
    head, tail = rows[:128], rows[128:]
    even_out[...] = jnp.where(lower, tail, head).astype(BF16)
    odd_out[...] = jnp.where(lower, head, tail).astype(BF16)
    sums_out[...] = jnp.where(lower, tail, head).astype(BF16)
    before, _ = partners(trade)

    @pl.when(before)
    def _():
        column_windows(rows_ref[:128], p2m_ref, far_rows, near_rows)
        sums = halo_sums(lambda offset_x, index: far_blocks(m2l_ref, offset_x, 4 + index), far_rows)
        sums_out[:64] = sums.astype(BF16)
        near = near_product(near_rows, slice(0, 32), near_ref, 2)
        rounded = near.astype(BF16)
        sums_out[64:96] = rounded
        sums_out[96:] = (near - rounded.astype(F32)).astype(BF16)


def joined(trade, own, odd, even, m2l_table, near, p2m):
    return pl.pallas_call(
        functools.partial(join_kernel, trade),
        out_shape=[pltpu.VMEM((rows, PAIR), BF16) for rows in (256, 128, 128, 128)],
        in_specs=[pl.BlockSpec(memory_space=pltpu.VMEM)] * 6,
        out_specs=[pl.BlockSpec(memory_space=pltpu.VMEM)] * 4,
        scratch_shapes=[
            pltpu.VMEM((256, PAIR), F32),
            pltpu.VMEM((7, 3, 64, PAIR), BF16),
            pltpu.VMEM((3, 2, 64, PAIR), BF16),
        ],
        compiler_params=pltpu.CompilerParams(vmem_limit_bytes=SMALL_LIMIT),
        cost_estimate=pl.CostEstimate(flops=1000000, bytes_accessed=100000, transcendentals=0),
        name="join",
    )(own, even, odd, m2l_table, near, p2m)


def shifted(rows):
    place = lax.broadcasted_iota(jnp.int32, rows.shape, 0) % 8
    before = jnp.where(place == 0, 0.0, jnp.roll(rows, 1, axis=0))
    after = jnp.where(place == 7, 0.0, jnp.roll(rows, -1, axis=0))
    return before, rows, after


def column_windows(cells, p2m_ref, far_rows, near_rows):
    multipole = lax.dot_general(
        cells.astype(BF16), p2m_ref[...], (((1,), (1,)), ((), ())), preferred_element_type=F32
    )
    sources = shifted(multipole.astype(BF16).astype(F32))
    blank = jnp.zeros((8, PAIR), F32)
    count = cells.shape[0] // 64
    for b in range(3):
        for y in range(count):
            slab = sources[b][64 * y : 64 * y + 64]
            for offset_x in range(7):
                if offset_x == 0:
                    window = jnp.concatenate([blank, slab[0:8], blank, slab[16:24]], axis=0)
                elif offset_x == 6:
                    window = jnp.concatenate([slab[40:48], blank, slab[56:64], blank], axis=0)
                else:
                    window = slab[8 * (offset_x - 1) : 8 * (offset_x + 3)]
                far_rows[offset_x, b, 32 * y : 32 * y + 32] = window.astype(BF16)
    before, same, after = shifted(cells)
    lane = lax.broadcasted_iota(jnp.int32, cells.shape, 1)
    beside = jnp.where(lane < WIDTH, after, before)
    for k, kind in enumerate((same, beside)):
        for y in range(count):
            for offset_x in range(3):
                near_rows[offset_x, k, 32 * y : 32 * y + 32] = kind[
                    64 * y + 8 * (offset_x + 1) : 64 * y + 8 * (offset_x + 5)
                ].astype(BF16)


def far_product(far_rows, rows, blocks):
    chunks, weights = [], []
    for offset_x in range(7):
        for b, block in enumerate(blocks(offset_x)):
            if block is not None:
                chunks.append(far_rows[offset_x, b, rows])
                weights.append(block)
    return jnp.dot(
        jnp.concatenate(chunks, axis=1), jnp.concatenate(weights, axis=0), preferred_element_type=F32
    )


def near_product(near_rows, rows, near_ref, offset_y):
    chunks = [near_rows[offset_x, k, rows] for offset_x in range(3) for k in range(2)]
    weights = [near_ref[offset_x, offset_y].reshape(2 * PAIR, PAIR) for offset_x in range(3)]
    return jnp.dot(
        jnp.concatenate(chunks, axis=1), jnp.concatenate(weights, axis=0), preferred_element_type=F32
    )


def inner_kernel(own_ref, m2l_ref, near_ref, p2m_ref, far_out, near_out, table_out, far_rows, near_rows):
    column_windows(own_ref[...].astype(F32), p2m_ref, far_rows, near_rows)
    far_out[...] = jnp.zeros_like(far_out)
    for offset_y in range(7):
        targets = [3] if offset_y == 0 else [0] if offset_y == 6 else [
            target for target in range(4) if 0 <= target + offset_y - 3 <= 3
        ]
        start = targets[0] + offset_y - 3

        def packing(offset_x):
            blocks = far_blocks(m2l_ref, offset_x, offset_y)
            if offset_y != 3:
                for b, block in enumerate(blocks):
                    table_out[offset_x, offset_y, b] = jnp.zeros((PAIR, PAIR), BF16) if block is None else block
            return blocks

        product = far_product(far_rows, slice(32 * start, 32 * (start + len(targets))), packing)
        far_out[32 * targets[0] : 32 * (targets[-1] + 1)] += product
    near_out[...] = near_product(near_rows, slice(0, 128), near_ref, 1)
    near_out[32:128] += near_product(near_rows, slice(0, 96), near_ref, 0)
    near_out[0:96] += near_product(near_rows, slice(32, 128), near_ref, 2)


def halo_sums(blocks, far_rows):
    pair = far_product(far_rows, slice(0, 64), lambda offset_x: blocks(offset_x, 1))
    odd = far_product(far_rows, slice(0, 32), lambda offset_x: blocks(offset_x, 0))
    even = far_product(far_rows, slice(32, 64), lambda offset_x: blocks(offset_x, 2))
    return pair + jnp.concatenate([even, odd], axis=0)


def add_halo(cells_ref, before, after, far, near, table_ref, near_ref, p2m_ref, far_rows, near_rows):
    @pl.when(jnp.logical_or(before, after))
    def _():
        side = jnp.where(before, 0, 1)
        column_windows(cells_ref[...].astype(F32), p2m_ref, far_rows, near_rows)

        def blocks(offset_x, index):
            return [table_ref[offset_x, 4 * side + index, b] for b in range(3)]

        far[pl.ds(pl.multiple_of(64 * side, 64), 64)] += halo_sums(blocks, far_rows)
        rows = pl.ds(pl.multiple_of(32 - 32 * side, 32), 32)
        near[pl.ds(pl.multiple_of(96 * side, 32), 32)] += near_product(near_rows, rows, near_ref, 2 * side)


def partners(trade):
    place = lax.axis_index("gy")
    first, step = trade
    after = jnp.logical_and(lax.rem(place, step) == first, place + 1 < lax.axis_size("gy"))
    before = jnp.logical_and(lax.rem(place + step - 1, step) == first, place > 0)
    return before, after


def outer_kernel(
    trade, far_part, near_part, cells_ref, far_ref, near_ref, p2m_ref, far_out, near_out, far_rows, near_rows
):
    far_out[...] = far_part[...]
    near_out[...] = near_part[...]
    add_halo(cells_ref, *partners(trade), far_out, near_out, far_ref, near_ref, p2m_ref, far_rows, near_rows)


def last_kernel(
    trade, far_part, near_part, cells_ref, far_ref, near_ref, p2m_ref, l2p_ref,
    out_ref, far, near, far_rows, near_rows,
):
    pairs = out_ref.shape[2] // PAIR
    far[...] = far_part[...]
    near[...] = near_part[...]
    before, after = partners(trade)
    add_halo(cells_ref, before, False, far, near, far_ref, near_ref, p2m_ref, far_rows, near_rows)

    @pl.when(after)
    def _():
        far[64:128] += cells_ref[:64].astype(F32)
        near[96:128] += cells_ref[64:96].astype(F32) + cells_ref[96:128].astype(F32)

    near[...] += jnp.dot(far[...].astype(BF16), l2p_ref[...], preferred_element_type=F32)
    for x in range(4):
        for pair in range(pairs):
            out_ref[x, :, pair * PAIR : (pair + 1) * PAIR] = near[
                pl.ds(x * pairs + pair, 4, stride=4 * pairs), :
            ]


def inner(own, m2l_table, near, p2m):
    return pl.pallas_call(
        inner_kernel,
        out_shape=[
            pltpu.VMEM((128, PAIR), F32),
            pltpu.VMEM((128, PAIR), F32),
            pltpu.VMEM((7, 7, 3, PAIR, PAIR), BF16),
        ],
        in_specs=[pl.BlockSpec(memory_space=pltpu.VMEM)] * 4,
        out_specs=[pl.BlockSpec(memory_space=pltpu.VMEM)] * 3,
        scratch_shapes=[pltpu.VMEM((7, 3, 128, PAIR), BF16), pltpu.VMEM((3, 2, 128, PAIR), BF16)],
        compiler_params=pltpu.CompilerParams(vmem_limit_bytes=VMEM_LIMIT),
        cost_estimate=pl.CostEstimate(flops=400000000, bytes_accessed=6000000, transcendentals=0),
        name="inner",
    )(own, m2l_table, near, p2m)


def outer(trade, far_part, near_part, cells, far, near, p2m):
    return pl.pallas_call(
        functools.partial(outer_kernel, trade),
        out_shape=[pltpu.VMEM((128, PAIR), F32)] * 2,
        in_specs=[pl.BlockSpec(memory_space=pltpu.VMEM)] * 6,
        out_specs=[pl.BlockSpec(memory_space=pltpu.VMEM)] * 2,
        scratch_shapes=[pltpu.VMEM((7, 3, 64, PAIR), BF16), pltpu.VMEM((3, 2, 64, PAIR), BF16)],
        compiler_params=pltpu.CompilerParams(vmem_limit_bytes=VMEM_LIMIT),
        cost_estimate=pl.CostEstimate(flops=200000000, bytes_accessed=3000000, transcendentals=0),
        name="outer",
    )(far_part, near_part, cells, far, near, p2m)


def last(trade, shape, far_part, near_part, cells, far, near, p2m, l2p):
    return pl.pallas_call(
        functools.partial(last_kernel, trade),
        out_shape=jax.ShapeDtypeStruct(shape, F32),
        in_specs=[pl.BlockSpec(memory_space=pltpu.VMEM)] * 7,
        out_specs=pl.BlockSpec(memory_space=pltpu.VMEM),
        scratch_shapes=[
            pltpu.VMEM((128, PAIR), F32),
            pltpu.VMEM((128, PAIR), F32),
            pltpu.VMEM((7, 3, 64, PAIR), BF16),
            pltpu.VMEM((3, 2, 64, PAIR), BF16),
        ],
        compiler_params=pltpu.CompilerParams(vmem_limit_bytes=VMEM_LIMIT),
        cost_estimate=pl.CostEstimate(flops=200000000, bytes_accessed=3000000, transcendentals=0),
        name="last",
    )(far_part, near_part, cells, far, near, p2m, l2p)


def local(density, p2m_operator, m2l_table, near_table, l2p_operator):
    odd, even = swapped(density, "gx", 1, 2), swapped(density, "gx", 0, 2)
    near, p2m, l2p = packed(first(), p2m_operator, near_table, l2p_operator)
    trades = ((0, 4), (1, 2), (2, 4))
    own, to_odd, to_even, sums = joined(trades[-1], density, odd, even, m2l_table, near, p2m)
    halos = [swapped(part, "gy", *trade) for part, trade in zip((to_even, to_odd, sums), trades)]
    *parts, far = inner(own, m2l_table, near, p2m)
    for trade, halo in zip(trades[:-1], halos):
        parts = outer(trade, *parts, halo, far, near, p2m)
    return last(trades[-1], density.shape, *parts, halos[-1], far, near, p2m, l2p)


def solution(mesh):
    placed = (P("gx", "gy", None), P(), P(), P(), P())
    return jax.shard_map(
        local, mesh=mesh, in_specs=placed, out_specs=P("gx", "gy", None), check_vma=False
    )
```

```python
import functools

import jax
import jax.numpy as jnp
from jax import lax
from jax.experimental import pallas as pl
from jax.experimental.pallas import tpu as pltpu
from jax.sharding import PartitionSpec as P

BF16 = jnp.bfloat16
F32 = jnp.float32
WIDTH = 64
PAIR = 2 * WIDTH
VMEM_LIMIT = 40 * 1024 * 1024
SMALL_LIMIT = 8 * 1024 * 1024


AXES = ("gx", "gy")


def swapped(cells, axis, first, step):
    sizes = [lax.axis_size(name) for name in AXES]
    dim = AXES.index(axis)
    pairs = []
    for place in range(sizes[0] * sizes[1]):
        at = list(divmod(place, sizes[1]))
        if at[dim] % step == first and at[dim] + 1 < sizes[dim]:
            at[dim] += 1
        elif at[dim] > 0 and (at[dim] - 1) % step == first:
            at[dim] -= 1
        elif (at[1 - dim] ^ 1) < sizes[1 - dim]:
            at[1 - dim] ^= 1
        else:
            continue
        pairs.append((place, at[0] * sizes[1] + at[1]))
    return lax.ppermute(cells, AXES, pairs)


def square(block):
    rows, columns = block.shape
    if columns < WIDTH:
        block = jnp.concatenate([block, jnp.zeros((rows, WIDTH - columns), BF16)], axis=1)
    if rows < WIDTH:
        block = jnp.concatenate([block, jnp.zeros((WIDTH - rows, WIDTH), BF16)], axis=0)
    return block


def first_kernel(out_ref):
    out_ref[...] = jnp.zeros_like(out_ref)


def first():
    return pl.pallas_call(
        first_kernel,
        out_shape=pltpu.VMEM((8, PAIR), F32),
        out_specs=pl.BlockSpec(memory_space=pltpu.VMEM),
        compiler_params=pltpu.CompilerParams(vmem_limit_bytes=1024 * 1024),
        cost_estimate=pl.CostEstimate(flops=10000000000, bytes_accessed=1000, transcendentals=0),
        name="first",
    )()


def far_blocks(m2l_ref, offset_x, offset_y):
    inner = 2 <= offset_x <= 4 and 2 <= offset_y <= 4
    blank = jnp.zeros((WIDTH, WIDTH), BF16)
    entries = [
        blank if inner and 2 <= offset_z <= 4 else square(m2l_ref[offset_x, offset_y, offset_z])
        for offset_z in range(7)
    ]
    blocks = [jnp.concatenate([entries[s + 1], entries[s]], axis=1) for s in range(6)]
    return [
        None if inner and b == 1 else jnp.concatenate(blocks[2 * b : 2 * b + 2], axis=0) for b in range(3)
    ]


def pack_kernel(first_ref, p2m_ref, near_ref, l2p_ref, near_out, p2m_out, l2p_out):
    blank = jnp.zeros((WIDTH, WIDTH), BF16)
    for offset_x in range(3):
        for offset_y in range(3):
            before, same, after = [near_ref[offset_x, offset_y, z] for z in range(3)]
            upper = jnp.concatenate([same, before], axis=1)
            lower = jnp.concatenate([after, same], axis=1)
            near_out[offset_x, offset_y, 0] = jnp.concatenate([upper, lower], axis=0)
            upper = jnp.concatenate([blank, after], axis=1)
            lower = jnp.concatenate([before, blank], axis=1)
            near_out[offset_x, offset_y, 1] = jnp.concatenate([upper, lower], axis=0)
    p2m = square(p2m_ref[...])
    p2m_out[...] = jnp.concatenate(
        [jnp.concatenate([p2m, blank], axis=1), jnp.concatenate([blank, p2m], axis=1)], axis=0
    )
    l2p = square(l2p_ref[...])
    l2p_out[...] = jnp.concatenate(
        [jnp.concatenate([l2p, blank], axis=1), jnp.concatenate([blank, l2p], axis=1)], axis=0
    )


def packed(start, p2m_operator, near_table, l2p_operator):
    shapes = [(3, 3, 2, PAIR, PAIR), (PAIR, PAIR), (PAIR, PAIR)]
    return pl.pallas_call(
        pack_kernel,
        out_shape=[pltpu.VMEM(shape, BF16) for shape in shapes],
        in_specs=[pl.BlockSpec(memory_space=pltpu.VMEM)] * 4,
        out_specs=[pl.BlockSpec(memory_space=pltpu.VMEM)] * 3,
        compiler_params=pltpu.CompilerParams(vmem_limit_bytes=SMALL_LIMIT),
        cost_estimate=pl.CostEstimate(flops=4000000, bytes_accessed=10000000, transcendentals=0),
        name="pack",
    )(start, p2m_operator.T, near_table, l2p_operator)


def from_neighbours(axis, even_low, odd_low, even_high, odd_high):
    place = lax.axis_index(axis)
    lower = lax.rem(place, 2) == 0
    low = jnp.where(place == 0, 0.0, jnp.where(lower, odd_low, even_low))
    last = place == lax.axis_size(axis) - 1
    high = jnp.where(last, 0.0, jnp.where(lower, even_high, odd_high))
    return low, high


def join_kernel(
    trade, own_ref, odd_ref, even_ref, m2l_ref, near_ref, p2m_ref,
    own_out, odd_out, even_out, sums_out, rows_ref, far_rows, near_rows,
):
    pairs = own_ref.shape[2] // PAIR
    for pair in range(pairs):
        lanes = slice(pair * PAIR, (pair + 1) * PAIR)

        def part(ref, x):
            return ref[x, :, lanes].astype(F32)

        for x in range(8):
            if 2 <= x < 6:
                cells = part(own_ref, x - 2)
            else:
                low, high = from_neighbours(
                    "gx",
                    *((part(even_ref, 2 + x), part(odd_ref, 2 + x)) if x < 2 else (0.0, 0.0)),
                    *((part(even_ref, x - 6), part(odd_ref, x - 6)) if x > 5 else (0.0, 0.0)),
                )
                cells = low if x < 2 else high
            rows_ref[pl.ds(x * pairs + pair, 4, stride=8 * pairs), :] = cells
    rows = rows_ref[...]
    own_out[...] = rows.astype(BF16)
    lower = lax.rem(lax.axis_index("gy"), 2) == 0
    head, tail = rows[:128], rows[128:]
    even_out[...] = jnp.where(lower, tail, head).astype(BF16)
    odd_out[...] = jnp.where(lower, head, tail).astype(BF16)
    sums_out[...] = jnp.where(lower, tail, head).astype(BF16)
    before, _ = partners(trade)

    @pl.when(before)
    def _():
        near_windows(rows_ref[:64], near_rows)
        far_windows(rows_ref[:128], p2m_ref, far_rows)
        sums = halo_sums(lambda offset_x, index: far_blocks(m2l_ref, offset_x, 4 + index), far_rows)
        sums_out[:64] = sums.astype(BF16)
        near = near_product(near_rows, slice(0, 32), near_ref, 2)
        rounded = near.astype(BF16)
        sums_out[64:96] = rounded
        sums_out[96:] = (near - rounded.astype(F32)).astype(BF16)


def joined(trade, own, odd, even, m2l_table, near, p2m):
    return pl.pallas_call(
        functools.partial(join_kernel, trade),
        out_shape=[pltpu.VMEM((rows, PAIR), BF16) for rows in (256, 128, 128, 128)],
        in_specs=[pl.BlockSpec(memory_space=pltpu.VMEM)] * 6,
        out_specs=[pl.BlockSpec(memory_space=pltpu.VMEM)] * 4,
        scratch_shapes=[
            pltpu.VMEM((256, PAIR), F32),
            pltpu.VMEM((7, 3, 64, PAIR), BF16),
            pltpu.VMEM((3, 2, 64, PAIR), BF16),
        ],
        compiler_params=pltpu.CompilerParams(vmem_limit_bytes=SMALL_LIMIT),
        cost_estimate=pl.CostEstimate(flops=1000000, bytes_accessed=100000, transcendentals=0),
        name="join",
    )(own, odd, even, m2l_table, near, p2m)


def shifted(rows):
    place = lax.broadcasted_iota(jnp.int32, rows.shape, 0) % 8
    before = jnp.where(place == 0, 0.0, jnp.roll(rows, 1, axis=0))
    after = jnp.where(place == 7, 0.0, jnp.roll(rows, -1, axis=0))
    return before, rows, after


def far_windows(cells, p2m_ref, far_rows):
    multipole = lax.dot_general(
        cells.astype(BF16), p2m_ref[...], (((1,), (1,)), ((), ())), preferred_element_type=F32
    )
    sources = shifted(multipole.astype(BF16).astype(F32))
    blank = jnp.zeros((8, PAIR), F32)
    count = cells.shape[0] // 64
    for b in range(3):
        for y in range(count):
            slab = sources[b][64 * y : 64 * y + 64]
            for offset_x in range(7):
                if offset_x == 0:
                    window = jnp.concatenate([blank, slab[0:8], blank, slab[16:24]], axis=0)
                elif offset_x == 6:
                    window = jnp.concatenate([slab[40:48], blank, slab[56:64], blank], axis=0)
                else:
                    window = slab[8 * (offset_x - 1) : 8 * (offset_x + 3)]
                far_rows[offset_x, b, 32 * y : 32 * y + 32] = window.astype(BF16)


def near_windows(cells, near_rows):
    count = cells.shape[0] // 64
    before, same, after = shifted(cells)
    lane = lax.broadcasted_iota(jnp.int32, cells.shape, 1)
    beside = jnp.where(lane < WIDTH, after, before)
    for k, kind in enumerate((same, beside)):
        for y in range(count):
            for offset_x in range(3):
                near_rows[offset_x, k, 32 * y : 32 * y + 32] = kind[
                    64 * y + 8 * (offset_x + 1) : 64 * y + 8 * (offset_x + 5)
                ].astype(BF16)


def own_near(cells, near_out, near_ref, near_rows):
    near_windows(cells, near_rows)
    near_out[...] = near_product(near_rows, slice(0, 128), near_ref, 1)
    near_out[32:128] += near_product(near_rows, slice(0, 96), near_ref, 0)
    near_out[0:96] += near_product(near_rows, slice(32, 128), near_ref, 2)


def far_product(far_rows, rows, blocks):
    chunks, weights = [], []
    for offset_x in range(7):
        for b, block in enumerate(blocks(offset_x)):
            if block is not None:
                chunks.append(far_rows[offset_x, b, rows])
                weights.append(block)
    return jnp.dot(
        jnp.concatenate(chunks, axis=1), jnp.concatenate(weights, axis=0), preferred_element_type=F32
    )


def near_product(near_rows, rows, near_ref, offset_y):
    chunks = [near_rows[offset_x, k, rows] for offset_x in range(3) for k in range(2)]
    weights = [near_ref[offset_x, offset_y].reshape(2 * PAIR, PAIR) for offset_x in range(3)]
    return jnp.dot(
        jnp.concatenate(chunks, axis=1), jnp.concatenate(weights, axis=0), preferred_element_type=F32
    )


def inner_kernel(
    own_ref, m2l_ref, near_ref, p2m_ref, far_out, near_out, table_out, far_rows, near_rows
):
    far_windows(own_ref[...].astype(F32), p2m_ref, far_rows)
    far_out[...] = jnp.zeros_like(far_out)
    for offset_y in range(7):
        targets = [3] if offset_y == 0 else [0] if offset_y == 6 else [
            target for target in range(4) if 0 <= target + offset_y - 3 <= 3
        ]
        start = targets[0] + offset_y - 3

        def packing(offset_x):
            blocks = far_blocks(m2l_ref, offset_x, offset_y)
            if offset_y != 3:
                for b, block in enumerate(blocks):
                    table_out[offset_x, offset_y, b] = jnp.zeros((PAIR, PAIR), BF16) if block is None else block
            return blocks

        product = far_product(far_rows, slice(32 * start, 32 * (start + len(targets))), packing)
        far_out[32 * targets[0] : 32 * (targets[-1] + 1)] += product
    own_near(own_ref[...].astype(F32), near_out, near_ref, near_rows)


def halo_sums(blocks, far_rows):
    odd = far_product(far_rows, slice(0, 32), lambda offset_x: blocks(offset_x, 0))
    even = far_product(far_rows, slice(32, 64), lambda offset_x: blocks(offset_x, 2))
    pair = far_product(far_rows, slice(0, 64), lambda offset_x: blocks(offset_x, 1))
    return pair + jnp.concatenate([even, odd], axis=0)


def add_halo(cells_ref, side, far, near, table_ref, near_ref, p2m_ref, far_rows, near_rows):
    cells = cells_ref[...].astype(F32)
    far_windows(cells, p2m_ref, far_rows)
    near_windows(cells[64 - 64 * side : 128 - 64 * side], near_rows)

    def blocks(offset_x, index):
        offset_y = 4 * side + index
        inner = 2 <= offset_x <= 4 and 2 <= offset_y <= 4
        return [None if inner and b == 1 else table_ref[offset_x, offset_y, b] for b in range(3)]

    far[64 * side : 64 * side + 64] += halo_sums(blocks, far_rows)
    near[96 * side : 96 * side + 32] += near_product(
        near_rows, slice(0, 32), near_ref, 2 * side
    )


def partners(trade):
    place = lax.axis_index("gy")
    first, step = trade
    after = jnp.logical_and(lax.rem(place, step) == first, place + 1 < lax.axis_size("gy"))
    before = jnp.logical_and(lax.rem(place + step - 1, step) == first, place > 0)
    return before, after


def outer_kernel(
    trade, far_part, near_part, cells_ref, far_ref, near_ref, p2m_ref, far_out, near_out, far_rows, near_rows
):
    far_out[...] = far_part[...]
    near_out[...] = near_part[...]
    for side, used in enumerate(partners(trade)):

        @pl.when(used)
        def _():
            add_halo(cells_ref, side, far_out, near_out, far_ref, near_ref, p2m_ref, far_rows, near_rows)


def last_kernel(
    trade, far_part, near_part, cells_ref, far_ref, near_ref, p2m_ref, l2p_ref,
    out_ref, far, near, far_rows, near_rows,
):
    pairs = out_ref.shape[2] // PAIR
    far[...] = far_part[...]
    near[...] = near_part[...]
    before, after = partners(trade)

    @pl.when(before)
    def _():
        add_halo(cells_ref, 0, far, near, far_ref, near_ref, p2m_ref, far_rows, near_rows)

    @pl.when(after)
    def _():
        far[64:128] += cells_ref[:64].astype(F32)
        near[96:128] += cells_ref[64:96].astype(F32) + cells_ref[96:128].astype(F32)

    near[...] += jnp.dot(far[...].astype(BF16), l2p_ref[...], preferred_element_type=F32)
    for x in range(4):
        for pair in range(pairs):
            out_ref[x, :, pair * PAIR : (pair + 1) * PAIR] = near[
                pl.ds(x * pairs + pair, 4, stride=4 * pairs), :
            ]


def inner(own, m2l_table, near, p2m):
    return pl.pallas_call(
        inner_kernel,
        out_shape=[
            pltpu.VMEM((128, PAIR), F32),
            pltpu.VMEM((128, PAIR), F32),
            pltpu.VMEM((7, 7, 3, PAIR, PAIR), BF16),
        ],
        in_specs=[pl.BlockSpec(memory_space=pltpu.VMEM)] * 4,
        out_specs=[pl.BlockSpec(memory_space=pltpu.VMEM)] * 3,
        scratch_shapes=[pltpu.VMEM((7, 3, 128, PAIR), BF16), pltpu.VMEM((3, 2, 128, PAIR), BF16)],
        compiler_params=pltpu.CompilerParams(vmem_limit_bytes=VMEM_LIMIT),
        cost_estimate=pl.CostEstimate(flops=400000000, bytes_accessed=6000000, transcendentals=0),
        name="inner",
    )(own, m2l_table, near, p2m)


def outer(trade, far_part, near_part, cells, far, near, p2m):
    return pl.pallas_call(
        functools.partial(outer_kernel, trade),
        out_shape=[pltpu.VMEM((128, PAIR), F32)] * 2,
        in_specs=[pl.BlockSpec(memory_space=pltpu.VMEM)] * 6,
        out_specs=[pl.BlockSpec(memory_space=pltpu.VMEM)] * 2,
        scratch_shapes=[pltpu.VMEM((7, 3, 64, PAIR), BF16), pltpu.VMEM((3, 2, 64, PAIR), BF16)],
        compiler_params=pltpu.CompilerParams(vmem_limit_bytes=VMEM_LIMIT),
        cost_estimate=pl.CostEstimate(flops=200000000, bytes_accessed=3000000, transcendentals=0),
        name="outer",
    )(far_part, near_part, cells, far, near, p2m)


def last(trade, shape, far_part, near_part, cells, far, near, p2m, l2p):
    return pl.pallas_call(
        functools.partial(last_kernel, trade),
        out_shape=jax.ShapeDtypeStruct(shape, F32),
        in_specs=[pl.BlockSpec(memory_space=pltpu.VMEM)] * 7,
        out_specs=pl.BlockSpec(memory_space=pltpu.VMEM),
        scratch_shapes=[
            pltpu.VMEM((128, PAIR), F32),
            pltpu.VMEM((128, PAIR), F32),
            pltpu.VMEM((7, 3, 64, PAIR), BF16),
            pltpu.VMEM((3, 2, 64, PAIR), BF16),
        ],
        compiler_params=pltpu.CompilerParams(vmem_limit_bytes=VMEM_LIMIT),
        cost_estimate=pl.CostEstimate(flops=200000000, bytes_accessed=3000000, transcendentals=0),
        name="last",
    )(far_part, near_part, cells, far, near, p2m, l2p)


def local(density, p2m_operator, m2l_table, near_table, l2p_operator):
    odd, even = swapped(density, "gx", 1, 2), swapped(density, "gx", 0, 2)
    near, p2m, l2p = packed(first(), p2m_operator, near_table, l2p_operator)
    trades = ((0, 4), (1, 2), (2, 4))
    own, to_odd, to_even, sums = joined(trades[-1], density, odd, even, m2l_table, near, p2m)
    halos = [swapped(part, "gy", *trade) for part, trade in zip((to_even, to_odd, sums), trades)]
    *parts, far = inner(own, m2l_table, near, p2m)
    for trade, halo in zip(trades[:-1], halos):
        parts = outer(trade, *parts, halo, far, near, p2m)
    return last(trades[-1], density.shape, *parts, halos[-1], far, near, p2m, l2p)


def solution(mesh):
    placed = (P("gx", "gy", None), P(), P(), P(), P())
    return jax.shard_map(
        local, mesh=mesh, in_specs=placed, out_specs=P("gx", "gy", None), check_vma=False
    )
```

```python
import functools

import jax
import jax.numpy as jnp
from jax import lax
from jax.experimental import pallas as pl
from jax.experimental.pallas import tpu as pltpu
from jax.sharding import PartitionSpec as P

BF16 = jnp.bfloat16
F32 = jnp.float32
WIDTH = 64
PAIR = 2 * WIDTH
VMEM_LIMIT = 40 * 1024 * 1024
SMALL_LIMIT = 8 * 1024 * 1024


AXES = ("gx", "gy")


def swapped(cells, axis, first, step):
    sizes = [lax.axis_size(name) for name in AXES]
    dim = AXES.index(axis)
    pairs = []
    for place in range(sizes[0] * sizes[1]):
        at = list(divmod(place, sizes[1]))
        if at[dim] % step == first and at[dim] + 1 < sizes[dim]:
            at[dim] += 1
        elif at[dim] > 0 and (at[dim] - 1) % step == first:
            at[dim] -= 1
        elif (at[1 - dim] ^ 1) < sizes[1 - dim]:
            at[1 - dim] ^= 1
        else:
            continue
        pairs.append((place, at[0] * sizes[1] + at[1]))
    return lax.ppermute(cells, AXES, pairs)


def square(block):
    rows, columns = block.shape
    if columns < WIDTH:
        block = jnp.concatenate([block, jnp.zeros((rows, WIDTH - columns), BF16)], axis=1)
    if rows < WIDTH:
        block = jnp.concatenate([block, jnp.zeros((WIDTH - rows, WIDTH), BF16)], axis=0)
    return block


def first_kernel(out_ref):
    out_ref[...] = jnp.zeros_like(out_ref)


def first():
    return pl.pallas_call(
        first_kernel,
        out_shape=pltpu.VMEM((8, PAIR), F32),
        out_specs=pl.BlockSpec(memory_space=pltpu.VMEM),
        compiler_params=pltpu.CompilerParams(vmem_limit_bytes=1024 * 1024),
        cost_estimate=pl.CostEstimate(flops=10000000000, bytes_accessed=1000, transcendentals=0),
        name="first",
    )()


def far_blocks(m2l_ref, offset_x, offset_y):
    inner = 2 <= offset_x <= 4 and 2 <= offset_y <= 4
    blank = jnp.zeros((WIDTH, WIDTH), BF16)
    entries = [
        blank if inner and 2 <= offset_z <= 4 else square(m2l_ref[offset_x, offset_y, offset_z])
        for offset_z in range(7)
    ]
    blocks = [jnp.concatenate([entries[s + 1], entries[s]], axis=1) for s in range(6)]
    return [
        None if inner and b == 1 else jnp.concatenate(blocks[2 * b : 2 * b + 2], axis=0) for b in range(3)
    ]


def pack_kernel(first_ref, p2m_ref, near_ref, l2p_ref, near_out, p2m_out, l2p_out):
    blank = jnp.zeros((WIDTH, WIDTH), BF16)
    for offset_x in range(3):
        for offset_y in range(3):
            before, same, after = [near_ref[offset_x, offset_y, z] for z in range(3)]
            upper = jnp.concatenate([same, before], axis=1)
            lower = jnp.concatenate([after, same], axis=1)
            near_out[offset_x, offset_y, 0] = jnp.concatenate([upper, lower], axis=0)
            upper = jnp.concatenate([blank, after], axis=1)
            lower = jnp.concatenate([before, blank], axis=1)
            near_out[offset_x, offset_y, 1] = jnp.concatenate([upper, lower], axis=0)
    p2m = square(p2m_ref[...])
    p2m_out[...] = jnp.concatenate(
        [jnp.concatenate([p2m, blank], axis=1), jnp.concatenate([blank, p2m], axis=1)], axis=0
    )
    l2p = square(l2p_ref[...])
    l2p_out[...] = jnp.concatenate(
        [jnp.concatenate([l2p, blank], axis=1), jnp.concatenate([blank, l2p], axis=1)], axis=0
    )


def packed(start, p2m_operator, near_table, l2p_operator):
    shapes = [(3, 3, 2, PAIR, PAIR), (PAIR, PAIR), (PAIR, PAIR)]
    return pl.pallas_call(
        pack_kernel,
        out_shape=[pltpu.VMEM(shape, BF16) for shape in shapes],
        in_specs=[pl.BlockSpec(memory_space=pltpu.VMEM)] * 4,
        out_specs=[pl.BlockSpec(memory_space=pltpu.VMEM)] * 3,
        compiler_params=pltpu.CompilerParams(vmem_limit_bytes=SMALL_LIMIT),
        cost_estimate=pl.CostEstimate(flops=4000000, bytes_accessed=10000000, transcendentals=0),
        name="pack",
    )(start, p2m_operator.T, near_table, l2p_operator)


def from_neighbours(axis, even_low, odd_low, even_high, odd_high):
    place = lax.axis_index(axis)
    lower = lax.rem(place, 2) == 0
    low = jnp.where(place == 0, 0.0, jnp.where(lower, odd_low, even_low))
    last = place == lax.axis_size(axis) - 1
    high = jnp.where(last, 0.0, jnp.where(lower, even_high, odd_high))
    return low, high


def join_kernel(
    trade, own_ref, odd_ref, even_ref, m2l_ref, near_ref, p2m_ref,
    own_out, odd_out, even_out, sums_out, rows_ref, far_rows, near_rows,
):
    pairs = own_ref.shape[2] // PAIR
    for pair in range(pairs):
        lanes = slice(pair * PAIR, (pair + 1) * PAIR)

        def part(ref, x):
            return ref[x, :, lanes].astype(F32)

        for x in range(8):
            if 2 <= x < 6:
                cells = part(own_ref, x - 2)
            else:
                low, high = from_neighbours(
                    "gx",
                    *((part(even_ref, 2 + x), part(odd_ref, 2 + x)) if x < 2 else (0.0, 0.0)),
                    *((part(even_ref, x - 6), part(odd_ref, x - 6)) if x > 5 else (0.0, 0.0)),
                )
                cells = low if x < 2 else high
            rows_ref[pl.ds(x * pairs + pair, 4, stride=8 * pairs), :] = cells
    rows = rows_ref[...]
    own_out[...] = rows.astype(BF16)
    lower = lax.rem(lax.axis_index("gy"), 2) == 0
    head, tail = rows[:128], rows[128:]
    even_out[...] = jnp.where(lower, tail, head).astype(BF16)
    odd_out[...] = jnp.where(lower, head, tail).astype(BF16)
    sums_out[...] = jnp.where(lower, tail, head).astype(BF16)
    before, _ = partners(trade)

    @pl.when(before)
    def _():
        column_windows(rows_ref[:128], p2m_ref, far_rows, near_rows)
        sums = halo_sums(lambda offset_x, index: far_blocks(m2l_ref, offset_x, 4 + index), far_rows)
        sums_out[:64] = sums.astype(BF16)
        near = near_product(near_rows, slice(0, 32), near_ref, 2)
        rounded = near.astype(BF16)
        sums_out[64:96] = rounded
        sums_out[96:] = (near - rounded.astype(F32)).astype(BF16)


def joined(trade, own, odd, even, m2l_table, near, p2m):
    return pl.pallas_call(
        functools.partial(join_kernel, trade),
        out_shape=[pltpu.VMEM((rows, PAIR), BF16) for rows in (256, 128, 128, 128)],
        in_specs=[pl.BlockSpec(memory_space=pltpu.VMEM)] * 6,
        out_specs=[pl.BlockSpec(memory_space=pltpu.VMEM)] * 4,
        scratch_shapes=[
            pltpu.VMEM((256, PAIR), F32),
            pltpu.VMEM((7, 3, 64, PAIR), BF16),
            pltpu.VMEM((3, 2, 64, PAIR), BF16),
        ],
        compiler_params=pltpu.CompilerParams(vmem_limit_bytes=SMALL_LIMIT),
        cost_estimate=pl.CostEstimate(flops=1000000, bytes_accessed=100000, transcendentals=0),
        name="join",
    )(own, odd, even, m2l_table, near, p2m)


def shifted(rows):
    place = lax.broadcasted_iota(jnp.int32, rows.shape, 0) % 8
    before = jnp.where(place == 0, 0.0, jnp.roll(rows, 1, axis=0))
    after = jnp.where(place == 7, 0.0, jnp.roll(rows, -1, axis=0))
    return before, rows, after


def column_windows(cells, p2m_ref, far_rows, near_rows):
    multipole = lax.dot_general(
        cells.astype(BF16), p2m_ref[...], (((1,), (1,)), ((), ())), preferred_element_type=F32
    )
    sources = shifted(multipole.astype(BF16).astype(F32))
    blank = jnp.zeros((8, PAIR), F32)
    count = cells.shape[0] // 64
    for b in range(3):
        for y in range(count):
            slab = sources[b][64 * y : 64 * y + 64]
            for offset_x in range(7):
                if offset_x == 0:
                    window = jnp.concatenate([blank, slab[0:8], blank, slab[16:24]], axis=0)
                elif offset_x == 6:
                    window = jnp.concatenate([slab[40:48], blank, slab[56:64], blank], axis=0)
                else:
                    window = slab[8 * (offset_x - 1) : 8 * (offset_x + 3)]
                far_rows[offset_x, b, 32 * y : 32 * y + 32] = window.astype(BF16)
    before, same, after = shifted(cells)
    lane = lax.broadcasted_iota(jnp.int32, cells.shape, 1)
    beside = jnp.where(lane < WIDTH, after, before)
    for k, kind in enumerate((same, beside)):
        for y in range(count):
            for offset_x in range(3):
                near_rows[offset_x, k, 32 * y : 32 * y + 32] = kind[
                    64 * y + 8 * (offset_x + 1) : 64 * y + 8 * (offset_x + 5)
                ].astype(BF16)


def far_product(far_rows, rows, blocks):
    chunks, weights = [], []
    for offset_x in range(7):
        for b, block in enumerate(blocks(offset_x)):
            if block is not None:
                chunks.append(far_rows[offset_x, b, rows])
                weights.append(block)
    return jnp.dot(
        jnp.concatenate(chunks, axis=1), jnp.concatenate(weights, axis=0), preferred_element_type=F32
    )


def near_product(near_rows, rows, near_ref, offset_y):
    chunks = [near_rows[offset_x, k, rows] for offset_x in range(3) for k in range(2)]
    weights = [near_ref[offset_x, offset_y].reshape(2 * PAIR, PAIR) for offset_x in range(3)]
    return jnp.dot(
        jnp.concatenate(chunks, axis=1), jnp.concatenate(weights, axis=0), preferred_element_type=F32
    )


def inner_kernel(own_ref, m2l_ref, near_ref, p2m_ref, far_out, near_out, table_out, far_rows, near_rows):
    column_windows(own_ref[...].astype(F32), p2m_ref, far_rows, near_rows)
    near_out[...] = near_product(near_rows, slice(0, 128), near_ref, 1)
    near_out[32:128] += near_product(near_rows, slice(0, 96), near_ref, 0)
    near_out[0:96] += near_product(near_rows, slice(32, 128), near_ref, 2)
    far_out[...] = jnp.zeros_like(far_out)
    for offset_y in range(7):
        targets = [3] if offset_y == 0 else [0] if offset_y == 6 else [
            target for target in range(4) if 0 <= target + offset_y - 3 <= 3
        ]
        start = targets[0] + offset_y - 3

        def packing(offset_x):
            blocks = far_blocks(m2l_ref, offset_x, offset_y)
            if offset_y != 3:
                for b, block in enumerate(blocks):
                    table_out[offset_x, offset_y, b] = jnp.zeros((PAIR, PAIR), BF16) if block is None else block
            return blocks

        product = far_product(far_rows, slice(32 * start, 32 * (start + len(targets))), packing)
        far_out[32 * targets[0] : 32 * (targets[-1] + 1)] += product


def halo_sums(blocks, far_rows):
    pair = far_product(far_rows, slice(0, 64), lambda offset_x: blocks(offset_x, 1))
    odd = far_product(far_rows, slice(0, 32), lambda offset_x: blocks(offset_x, 0))
    even = far_product(far_rows, slice(32, 64), lambda offset_x: blocks(offset_x, 2))
    return pair + jnp.concatenate([even, odd], axis=0)


def add_halo(cells_ref, before, after, far, near, table_ref, near_ref, p2m_ref, far_rows, near_rows):
    @pl.when(jnp.logical_or(before, after))
    def _():
        side = jnp.where(before, 0, 1)
        column_windows(cells_ref[...].astype(F32), p2m_ref, far_rows, near_rows)

        def blocks(offset_x, index):
            return [table_ref[offset_x, 4 * side + index, b] for b in range(3)]

        far[pl.ds(pl.multiple_of(64 * side, 64), 64)] += halo_sums(blocks, far_rows)
        rows = pl.ds(pl.multiple_of(32 - 32 * side, 32), 32)
        near[pl.ds(pl.multiple_of(96 * side, 32), 32)] += near_product(near_rows, rows, near_ref, 2 * side)


def partners(trade):
    place = lax.axis_index("gy")
    first, step = trade
    after = jnp.logical_and(lax.rem(place, step) == first, place + 1 < lax.axis_size("gy"))
    before = jnp.logical_and(lax.rem(place + step - 1, step) == first, place > 0)
    return before, after


def outer_kernel(
    trade, far_part, near_part, cells_ref, far_ref, near_ref, p2m_ref, far_out, near_out, far_rows, near_rows
):
    far_out[...] = far_part[...]
    near_out[...] = near_part[...]
    add_halo(cells_ref, *partners(trade), far_out, near_out, far_ref, near_ref, p2m_ref, far_rows, near_rows)


def last_kernel(
    trade, far_part, near_part, cells_ref, far_ref, near_ref, p2m_ref, l2p_ref,
    out_ref, far, near, far_rows, near_rows,
):
    pairs = out_ref.shape[2] // PAIR
    far[...] = far_part[...]
    near[...] = near_part[...]
    before, after = partners(trade)
    add_halo(cells_ref, before, False, far, near, far_ref, near_ref, p2m_ref, far_rows, near_rows)

    @pl.when(after)
    def _():
        far[64:128] += cells_ref[:64].astype(F32)
        near[96:128] += cells_ref[64:96].astype(F32) + cells_ref[96:128].astype(F32)

    near[...] += jnp.dot(far[...].astype(BF16), l2p_ref[...], preferred_element_type=F32)
    for x in range(4):
        for pair in range(pairs):
            out_ref[x, :, pair * PAIR : (pair + 1) * PAIR] = near[
                pl.ds(x * pairs + pair, 4, stride=4 * pairs), :
            ]


def inner(own, m2l_table, near, p2m):
    return pl.pallas_call(
        inner_kernel,
        out_shape=[
            pltpu.VMEM((128, PAIR), F32),
            pltpu.VMEM((128, PAIR), F32),
            pltpu.VMEM((7, 7, 3, PAIR, PAIR), BF16),
        ],
        in_specs=[pl.BlockSpec(memory_space=pltpu.VMEM)] * 4,
        out_specs=[pl.BlockSpec(memory_space=pltpu.VMEM)] * 3,
        scratch_shapes=[pltpu.VMEM((7, 3, 128, PAIR), BF16), pltpu.VMEM((3, 2, 128, PAIR), BF16)],
        compiler_params=pltpu.CompilerParams(vmem_limit_bytes=VMEM_LIMIT),
        cost_estimate=pl.CostEstimate(flops=400000000, bytes_accessed=6000000, transcendentals=0),
        name="inner",
    )(own, m2l_table, near, p2m)


def outer(trade, far_part, near_part, cells, far, near, p2m):
    return pl.pallas_call(
        functools.partial(outer_kernel, trade),
        out_shape=[pltpu.VMEM((128, PAIR), F32)] * 2,
        in_specs=[pl.BlockSpec(memory_space=pltpu.VMEM)] * 6,
        out_specs=[pl.BlockSpec(memory_space=pltpu.VMEM)] * 2,
        scratch_shapes=[pltpu.VMEM((7, 3, 64, PAIR), BF16), pltpu.VMEM((3, 2, 64, PAIR), BF16)],
        compiler_params=pltpu.CompilerParams(vmem_limit_bytes=VMEM_LIMIT),
        cost_estimate=pl.CostEstimate(flops=200000000, bytes_accessed=3000000, transcendentals=0),
        name="outer",
    )(far_part, near_part, cells, far, near, p2m)


def last(trade, shape, far_part, near_part, cells, far, near, p2m, l2p):
    return pl.pallas_call(
        functools.partial(last_kernel, trade),
        out_shape=jax.ShapeDtypeStruct(shape, F32),
        in_specs=[pl.BlockSpec(memory_space=pltpu.VMEM)] * 7,
        out_specs=pl.BlockSpec(memory_space=pltpu.VMEM),
        scratch_shapes=[
            pltpu.VMEM((128, PAIR), F32),
            pltpu.VMEM((128, PAIR), F32),
            pltpu.VMEM((7, 3, 64, PAIR), BF16),
            pltpu.VMEM((3, 2, 64, PAIR), BF16),
        ],
        compiler_params=pltpu.CompilerParams(vmem_limit_bytes=VMEM_LIMIT),
        cost_estimate=pl.CostEstimate(flops=200000000, bytes_accessed=3000000, transcendentals=0),
        name="last",
    )(far_part, near_part, cells, far, near, p2m, l2p)


def local(density, p2m_operator, m2l_table, near_table, l2p_operator):
    odd, even = swapped(density, "gx", 1, 2), swapped(density, "gx", 0, 2)
    near, p2m, l2p = packed(first(), p2m_operator, near_table, l2p_operator)
    trades = ((0, 4), (1, 2), (2, 4))
    own, to_odd, to_even, sums = joined(trades[-1], density, odd, even, m2l_table, near, p2m)
    halos = [swapped(part, "gy", *trade) for part, trade in zip((to_even, to_odd, sums), trades)]
    *parts, far = inner(own, m2l_table, near, p2m)
    for trade, halo in zip(trades[:-1], halos):
        parts = outer(trade, *parts, halo, far, near, p2m)
    return last(trades[-1], density.shape, *parts, halos[-1], far, near, p2m, l2p)


def solution(mesh):
    placed = (P("gx", "gy", None), P(), P(), P(), P())
    return jax.shard_map(
        local, mesh=mesh, in_specs=placed, out_specs=P("gx", "gy", None), check_vma=False
    )
```
